512 devices in a mesh: slab: 64 (over z, y), atom: 8 (over x, core).
Axes of the slice: x: 4, y: 4, z: 16, core: 2. Of those that a mesh axis runs over, the one named last changes fastest.
Arguments:
- atom_feats: bfloat16 [32768, 3200], P(('slab', 'atom')), may hold values from -6 to 6
- species: int32 [32768], P(('slab', 'atom')), may hold values from 0 to 7
- send_rows: int32 [64, 8, 4, 64], P('slab', 'atom'), may hold values from 0 to 64
- neighbours: int32 [16, 8192], P('atom', 'slab'), may hold values from 0 to 320, as said below
- harmonics: float32 [25, 16, 8192], P(None, 'atom', 'slab'), may hold values from -1 to 1
- distances: float32 [16, 8192], P('atom', 'slab'), may hold values from 0.5 to 3.8
- target: float32 [8192], P('slab'), may hold values from -6 to 6
- w_deg: bfloat16 [5, 128, 128], replicated, may hold values from -0.5 to 0.5
- w_gate: bfloat16 [128, 512], replicated, may hold values from -0.5 to 0.5
- embed: float32 [8, 128], replicated, may hold values from -3 to 3
- w_radial: float32 [8, 640], replicated, may hold values from -2 to 2
- w_hidden: float32 [128, 128], replicated, may hold values from -0.5 to 0.5
- b_hidden: float32 [128], replicated, may hold values from -3 to 3
- w_out: float32 [128], replicated, may hold values from -0.5 to 0.5
Outputs:
- loss: float32 [], replicated
- density: float32 [8192], P('slab')
- grad_deg: float32 [5, 128, 128], replicated
- grad_gate: float32 [128, 512], replicated
- grad_embed: float32 [8, 128], replicated
- grad_radial: float32 [8, 640], replicated
- grad_hidden: float32 [128, 128], replicated
- grad_hbias: float32 [128], replicated
- grad_out: float32 [128], replicated
The draws below stay inside these ranges and needn't reach their ends.
Inputs may be any that keep to these rules, and one draw needn't show every extreme that they name: `send_rows`: entries name rows of one device's atoms; the value 64 marks an empty slot. `neighbours`: entries name rows of the buffer of the probe's slab and the row's shard; 320 is its zero row and marks an empty slot.
All inputs are finite; a program needn't handle non-finite values.
Results may differ from the reference program's by a relative error of at most 0.0055.
Values may be sent and summed in bfloat16 or wider, within the bound.
No kernel may reach another device: no remote copies, remote signals or barrier semaphores. Data moves between devices by JAX's collectives and lax.ppermute only.
A program may use at most 128 MiB of HBM per device.

```python
import math
import jax
import jax.numpy as jnp
from jax import lax

C = 128
NDEG = 5
LM = 25
NB = 8
SPEC = 8
ATOM_DEV = 64
CAP = 64
SLOTS = 2
P_DEV = 128
ATOMS = 32768
TOT_PROBES = 8192
BUF = 320
N_SLAB = 64
N_ATOM = 8


def draw_neighbours(key, part):
    key = jax.random.fold_in(key, 1)
    first_key, second_key = jax.random.split(key)
    shape = (N_ATOM * SLOTS, TOT_PROBES)
    picked = jax.random.randint(first_key, shape, 0, BUF, dtype=jnp.int32)
    empty = jax.random.randint(second_key, shape, 0, 4, dtype=jnp.int32) == 0
    return jnp.where(empty, BUF, picked).astype(jnp.int32)


def plant(drawn, own_key, low, high):
    shape = drawn.shape
    place = [jax.random.randint(jax.random.fold_in(own_key, axis), (), 0, shape[axis]) for axis in range(len(shape))]
    drawn = drawn.at[tuple(place)].set(low)
    longest = shape.index(max(shape))
    place[longest] = (place[longest] + 1) % shape[longest]
    return drawn.at[tuple(place)].set(high)


def block_levels(own_key, shape, shards, smallest, largest):
    level, own = 1.0, jax.random.fold_in(own_key, 6)
    for dim, shards_of in shards:
        draws = jnp.exp(jax.random.uniform(jax.random.fold_in(own, dim), (shards_of,), jnp.float32, smallest / len(shards), largest / len(shards)))
        level = level * jnp.repeat(draws, shape[dim] // shards_of).reshape([-1 if axis == dim else 1 for axis in range(len(shape))])
    return level


def scatter_about(key, dims, scale, reach, cuts=(), held_as=jnp.bfloat16):
    array = scale * jax.random.normal(key, dims, jnp.float32)
    if cuts:
        array = array * block_levels(key, dims, cuts, -0.22, 0.18)
    return jnp.clip(array, -reach, reach).astype(held_as)


def setup_inputs(seed: int = 0) -> dict:
    key_of = jax.random.split(jax.random.key(seed), 15)
    atom_feats = scatter_about(key_of[0], (ATOMS, LM * C), 1.0, 6.0, ((0, 512),))
    species = plant(jax.random.randint(key_of[1], (ATOMS,), 0, SPEC), jax.random.fold_in(key_of[1], 1), 0, SPEC - 1).astype(jnp.int32)
    send_rows = plant(jax.random.randint(key_of[2], (N_SLAB, N_ATOM, 4, CAP), 0, ATOM_DEV + 1), jax.random.fold_in(key_of[2], 1), 0, ATOM_DEV).astype(jnp.int32)
    neighbours = draw_neighbours(jax.random.fold_in(key_of[14], 71), 0)
    harmonics = scatter_about(key_of[4], (LM, N_ATOM * SLOTS, TOT_PROBES), 0.15, 1.0, ((1, 8), (2, 64)), jnp.float32)
    distances = jnp.clip(0.5 + 3.3 * jax.random.uniform(key_of[5], (N_ATOM * SLOTS, TOT_PROBES), jnp.float32) ** block_levels(key_of[5], (N_ATOM * SLOTS, TOT_PROBES), ((0, 8), (1, 64)), -0.2, 0.2), 0.5, 3.8)
    target = scatter_about(key_of[6], (TOT_PROBES,), 1.0, 6.0, ((0, 64),), jnp.float32)
    w_deg = scatter_about(key_of[7], (NDEG, C, C), C ** -0.5, 0.5)
    w_gate = scatter_about(key_of[8], (C, (NDEG - 1) * C), C ** -0.5, 0.5)
    embed = scatter_about(key_of[9], (SPEC, C), 0.5, 3.0, (), jnp.float32)
    w_radial = scatter_about(key_of[10], (NB, NDEG * C), NB ** -0.5, 2.0, (), jnp.float32)
    w_hidden = scatter_about(key_of[11], (C, C), C ** -0.5, 0.5, (), jnp.float32)
    b_hidden = scatter_about(key_of[12], (C,), 0.5, 3.0, (), jnp.float32)
    w_out = scatter_about(key_of[13], (C,), C ** -0.5, 0.5, (), jnp.float32)
    return dict(atom_feats=atom_feats, species=species, send_rows=send_rows, neighbours=neighbours, harmonics=harmonics, distances=distances, target=target, w_deg=w_deg, w_gate=w_gate, embed=embed, w_radial=w_radial, w_hidden=w_hidden, b_hidden=b_hidden, w_out=w_out)


OFFSETS = (-2, -1, 1, 2)
CUTOFF = 4.0
PRECISE = lax.Precision.HIGHEST

def silu_slope(values):
    logistic = jax.nn.sigmoid(values)
    return logistic * (1.0 + values * (1.0 - logistic))

def contract_rows(left, right, precision=None):
    return lax.dot_general(left, right, (((0,), (0,)), ((), ())), preferred_element_type=jnp.float32, precision=precision)

def encode(features, species, w_deg, w_gate, embed):
    atoms = features.shape[0]
    chans = w_deg.shape[1]
    degrees = w_deg.shape[0]
    kinds = embed.shape[0]
    blocks = features.reshape(atoms, degrees * degrees, chans)
    mixed = []
    for degree in range(degrees):
        lower = degree * degree
        upper = (degree + 1) * (degree + 1)
        flat = blocks[:, lower:upper, :].reshape(-1, chans)
        mixed.append(jnp.dot(flat, w_deg[degree], preferred_element_type=jnp.float32).reshape(atoms, upper - lower, chans))
    gates = jax.nn.sigmoid(jnp.dot(blocks[:, 0, :], w_gate, preferred_element_type=jnp.float32))
    onehot = (species[:, None] == jnp.arange(kinds, dtype=jnp.int32)[None, :]).astype(jnp.float32)
    looked_up = jnp.dot(onehot, embed, precision=PRECISE)
    pieces = [blocks[:, 0:1, :].astype(jnp.float32) + jax.nn.silu(mixed[0]) + looked_up[:, None, :]]
    for degree in range(1, degrees):
        lower = degree * degree
        upper = (degree + 1) * (degree + 1)
        gate = gates[:, (degree - 1) * chans:degree * chans]
        pieces.append(blocks[:, lower:upper, :].astype(jnp.float32) + mixed[degree] * gate[:, None, :])
    updated = jnp.concatenate(pieces, axis=1).reshape(atoms, -1).astype(jnp.bfloat16)
    return (updated, (mixed, gates, onehot))

def encode_grads(features, saved, cotangent, w_deg):
    mixed, gates, onehot = saved
    atoms = features.shape[0]
    chans = w_deg.shape[1]
    degrees = w_deg.shape[0]
    blocks = features.reshape(atoms, degrees * degrees, chans)
    upstream = cotangent.reshape(atoms, degrees * degrees, chans)
    scalar_up = upstream[:, 0, :]
    grad_embed = contract_rows(onehot, scalar_up, PRECISE)
    first = (scalar_up * silu_slope(mixed[0][:, 0, :])).astype(jnp.bfloat16)
    grad_list = [contract_rows(blocks[:, 0, :], first)]
    pre_list = []
    for degree in range(1, degrees):
        lower = degree * degree
        upper = (degree + 1) * (degree + 1)
        gate = gates[:, (degree - 1) * chans:degree * chans]
        local_up = upstream[:, lower:upper, :]
        mixed_grad = (local_up * gate[:, None, :]).astype(jnp.bfloat16).reshape(-1, chans)
        grad_list.append(contract_rows(blocks[:, lower:upper, :].reshape(-1, chans), mixed_grad))
        pre_list.append(lax.optimization_barrier(jnp.sum(local_up * mixed[degree], axis=1)) * gate * (1.0 - gate))
    gate_input = jnp.concatenate(pre_list, axis=1).astype(jnp.bfloat16)
    grad_gate = contract_rows(blocks[:, 0, :], gate_input)
    return (jnp.stack(grad_list), grad_gate, grad_embed)

def radial_basis(distance, count):
    orders = jnp.arange(1, count + 1).astype(jnp.float32)
    phase = math.pi * distance / CUTOFF
    envelope = 0.5 * (jnp.cos(phase) + 1.0) / distance
    return jnp.sin(phase[:, None] * orders[None, :]) * envelope[:, None]

def pair_sums(gathered, harm, chans):
    degrees = math.isqrt(harm.shape[0])
    sums = []
    for degree in range(degrees):
        total = None
        for comp in range(degree * degree, (degree + 1) * (degree + 1)):
            term = harm[comp][:, None] * gathered[:, comp * chans:(comp + 1) * chans].astype(jnp.float32)
            total = term if total is None else total + term
        sums.append(total)
    return sums

def probe_forward(gathered, harm, basis, w_radial):
    degrees = math.isqrt(harm.shape[0])
    chans = w_radial.shape[1] // degrees
    radial = jnp.dot(basis, w_radial, precision=PRECISE)
    sums = pair_sums(gathered, harm, chans)
    result = None
    for degree in range(degrees):
        term = radial[:, degree * chans:(degree + 1) * chans] * sums[degree]
        result = term if result is None else result + term
    return result

def probe_backward(gathered, harm, basis, w_radial, upstream):
    degrees = math.isqrt(harm.shape[0])
    chans = w_radial.shape[1] // degrees
    radial = jnp.dot(basis, w_radial, precision=PRECISE)
    sums = pair_sums(gathered, harm, chans)
    radial_up = jnp.concatenate([sums[degree] * upstream for degree in range(degrees)], axis=1)
    row_parts = []
    for degree in range(degrees):
        inner = radial[:, degree * chans:(degree + 1) * chans] * upstream
        for comp in range(degree * degree, (degree + 1) * (degree + 1)):
            row_parts.append(harm[comp][:, None] * inner)
    return (jnp.concatenate(row_parts, axis=1), contract_rows(basis, radial_up, PRECISE))

def readout(summed, target, w_hidden, b_hidden, w_out, scale):
    hidden_pre = jnp.dot(summed, w_hidden, precision=PRECISE) + b_hidden[None, :]
    activated = jax.nn.silu(hidden_pre)
    density = jnp.dot(activated, w_out, precision=PRECISE)
    error = density - target
    loss = 0.5 * scale * jnp.sum(error * error)
    error_grad = error * scale
    grad_out = jnp.dot(error_grad, activated, precision=PRECISE)
    pre_grad = error_grad[:, None] * w_out[None, :] * silu_slope(hidden_pre)
    grad_hidden = contract_rows(summed, pre_grad, PRECISE)
    grad_hbias = lax.optimization_barrier(jnp.sum(pre_grad, axis=0))
    summed_grad = jnp.dot(pre_grad, w_hidden.T, precision=PRECISE)
    return (density, summed_grad, (grad_hidden, grad_hbias, grad_out), loss)

def buffer_table(send_rows):
    slab_ids = jnp.arange(N_SLAB, dtype=jnp.int32)
    shard_ids = jnp.arange(N_ATOM, dtype=jnp.int32)
    local_ids = jnp.arange(ATOM_DEV, dtype=jnp.int32)
    owners = (slab_ids[:, None, None] * N_ATOM + shard_ids[None, :, None]) * ATOM_DEV + local_ids[None, None, :]
    pieces = [owners.astype(jnp.int32)]
    for which in range(len(OFFSETS)):
        source = (slab_ids - OFFSETS[which]) % N_SLAB
        local = send_rows[source, :, which, :]
        base = (source[:, None] * N_ATOM + shard_ids[None, :]) * ATOM_DEV
        pieces.append(jnp.where(local < ATOM_DEV, base[:, :, None] + local, ATOMS).astype(jnp.int32))
    pieces.append(jnp.full((N_SLAB, N_ATOM, 1), ATOMS, dtype=jnp.int32))
    return jnp.concatenate(pieces, axis=2).astype(jnp.int32)

def reference(atom_feats, species, send_rows, neighbours, harmonics, distances, target, w_deg, w_gate, embed, w_radial, w_hidden, b_hidden, w_out):
    device_total = N_SLAB * N_ATOM
    width = LM * C
    feat_blocks = atom_feats.reshape(device_total, ATOM_DEV, width)
    kind_blocks = species.reshape(device_total, ATOM_DEV)
    encoded = lax.map(lambda item: encode(item[0], item[1], w_deg, w_gate, embed)[0], (feat_blocks, kind_blocks))
    table_rows = jnp.concatenate([encoded.reshape(ATOMS, width), jnp.zeros((1, width), jnp.bfloat16)], axis=0)
    lookup = buffer_table(send_rows)
    slab_nbr = neighbours.reshape(N_ATOM * SLOTS, N_SLAB, P_DEV).transpose(1, 0, 2)
    slab_harm = harmonics.reshape(LM, N_ATOM * SLOTS, N_SLAB, P_DEV).transpose(2, 0, 1, 3)
    slab_dist = distances.reshape(N_ATOM * SLOTS, N_SLAB, P_DEV).transpose(1, 0, 2)

    def pairs_of(index):
        local_rows = slab_nbr[index].reshape(N_ATOM, SLOTS * P_DEV)
        global_rows = jnp.take_along_axis(lookup[index], local_rows, axis=1).reshape(-1)
        return (global_rows, slab_harm[index].reshape(LM, -1), radial_basis(slab_dist[index].reshape(-1), NB))

    def forward_slab(index):
        global_rows, harm, basis = pairs_of(index)
        contrib = probe_forward(table_rows[global_rows], harm, basis, w_radial)
        return contrib.reshape(N_ATOM * SLOTS, P_DEV, C).sum(axis=0)
    summed = lax.map(forward_slab, jnp.arange(N_SLAB, dtype=jnp.int32)).reshape(TOT_PROBES, C)
    scale = 1.0 / math.sqrt(TOT_PROBES)
    density, summed_grad, head_grads, loss = readout(summed, target, w_hidden, b_hidden, w_out, scale)
    slab_grad = summed_grad.reshape(N_SLAB, P_DEV, C)

    def backward_slab(index, carry):
        row_grads, radial_grad = carry
        global_rows, harm, basis = pairs_of(index)
        upstream = jnp.broadcast_to(slab_grad[index][None], (N_ATOM * SLOTS, P_DEV, C)).reshape(-1, C)
        pair_grads, weight_grad = probe_backward(table_rows[global_rows], harm, basis, w_radial, upstream)
        return (row_grads.at[global_rows].add(pair_grads), radial_grad + weight_grad)
    start = (jnp.zeros((ATOMS + 1, width), jnp.float32), jnp.zeros(w_radial.shape, jnp.float32))
    row_grads, grad_radial = lax.fori_loop(0, N_SLAB, backward_slab, start)
    grad_blocks = row_grads[:ATOMS].reshape(device_total, ATOM_DEV, width)

    def encoder_grads(item):
        features, kinds_row, cotangent = item
        saved = encode(features, kinds_row, w_deg, w_gate, embed)[1]
        return encode_grads(features, saved, cotangent, w_deg)
    deg_parts, gate_parts, embed_parts = lax.map(encoder_grads, (feat_blocks, kind_blocks, grad_blocks))
    return (loss, density, deg_parts.sum(axis=0), gate_parts.sum(axis=0), embed_parts.sum(axis=0), grad_radial, head_grads[0], head_grads[1], head_grads[2])
```

```python
import functools
import math

import jax
import jax.numpy as jnp
from jax import lax
from jax.experimental import pallas as pl
from jax.experimental.pallas import tpu as pltpu
from jax.sharding import Mesh, PartitionSpec as P

OFFSETS = (-2, -1, 1, 2)
CUTOFF = 4.0
PRECISE = lax.Precision.HIGHEST
F32 = jnp.float32
BF16 = jnp.bfloat16
SLAB = ("z", "y")
ATOM = ("x", "c")
PLANE = ("y", "x", "c")
DEGREES = 5
COMPS = DEGREES * DEGREES
CHANS = 128
ATOMS = 64
SLOTS = 2
PROBES = 128
SOURCES = 1 + len(OFFSETS)
SPAN = SLOTS * PROBES
PAIRS = SOURCES * SPAN
FIELDS = 32
BASES = 8
KINDS = 8
PAYLOAD = 1536


def first_rows(degree):
    return degree * degree * ATOMS, (degree + 1) * (degree + 1) * ATOMS


def lanes(block):
    return slice(block * CHANS, (block + 1) * CHANS)


def along_first(left, right, precision=None):
    return lax.dot_general(
        left, right, (((0,), (0,)), ((), ())), preferred_element_type=F32, precision=precision
    )


def along_last(left, right, precision=None):
    return lax.dot_general(
        left, right, (((1,), (1,)), ((), ())), preferred_element_type=F32, precision=precision
    )


def matmul(left, right, precision=None):
    return jnp.dot(left, right, preferred_element_type=F32, precision=precision)


def component_rows(feats_ref, degree):
    parts = [feats_ref[:, lanes(m)] for m in range(degree * degree, (degree + 1) * (degree + 1))]
    return parts[0] if degree == 0 else jnp.concatenate(parts, axis=0)


def over_components(gate, degree):
    return jnp.concatenate([gate] * (2 * degree + 1), axis=0)


def kind_rows(species_ref):
    ids = lax.broadcasted_iota(jnp.int32, (KINDS, ATOMS), 0)
    return (ids == species_ref[...]).astype(F32)


def encode_kernel(feats_ref, species_ref, w_deg_ref, w_gate_ref, embed_ref, rows_ref):
    scalar = feats_ref[:, lanes(0)]
    gates = jax.nn.sigmoid(matmul(scalar, w_gate_ref[...]))
    for degree in range(DEGREES):
        low, high = first_rows(degree)
        rows = component_rows(feats_ref, degree)
        mixed = matmul(rows, w_deg_ref[degree])
        if degree == 0:
            added = jax.nn.silu(mixed) + along_first(
                kind_rows(species_ref), embed_ref[...], PRECISE
            )
        else:
            added = mixed * over_components(gates[:, lanes(degree - 1)], degree)
        rows_ref[low:high, :] = (rows.astype(F32) + added).astype(BF16)


def pair_kernel(rows_ref, lists_ref, w_radial_ref, *refs):
    packs = refs[:SOURCES]
    out_refs = refs[SOURCES : 2 * SOURCES]
    spread_ref, sums_ref, radial_ref, basis_ref = refs[2 * SOURCES :]
    sub = lax.broadcasted_iota(jnp.int32, (ATOMS, PROBES), 0).astype(F32)
    dists = []
    for source in range(SOURCES):
        pack = packs[source]
        if source > 0:
            which = source - 1
            ids = lax.broadcasted_iota(jnp.int32, (ATOMS, ATOMS), 0)
            owners = (ids == lists_ref[which : which + 1, :]).astype(BF16)
        for slot in range(SLOTS):
            start = source * SPAN + slot * PROBES
            picked = pack[slot, COMPS + 1 : COMPS + 2, :] - float(source * ATOMS)
            hot = (picked == sub).astype(F32)
            if source > 0:
                hot = matmul(owners, hot.astype(BF16))
            for m in range(COMPS):
                spread_ref[m * ATOMS : (m + 1) * ATOMS, start : start + PROBES] = (
                    hot * pack[slot, m : m + 1, :]
                ).astype(BF16)
            dists.append(pack[slot, COMPS : COMPS + 1, :])
    dist = jnp.concatenate(dists, axis=1)
    orders = lax.broadcasted_iota(jnp.int32, (BASES, PAIRS), 0).astype(F32) + 1.0
    phase = math.pi * dist / CUTOFF
    envelope = 0.5 * (jnp.cos(phase) + 1.0) / dist
    basis = jnp.sin(phase * orders) * envelope
    basis_ref[...] = basis
    total = None
    for degree in range(DEGREES):
        low, high = first_rows(degree)
        radial = along_first(w_radial_ref[:, lanes(degree)], basis, PRECISE)
        radial_ref[lanes(degree), :] = radial
        sums = along_first(rows_ref[low:high, :], spread_ref[low:high, :])
        sums_ref[lanes(degree), :] = sums
        term = radial * sums
        total = term if total is None else total + term
    for source in range(SOURCES):
        start = source * SPAN
        out_refs[source][...] = (
            total[:, start : start + PROBES] + total[:, start + PROBES : start + SPAN]
        )


def silu_slope(values):
    logistic = jax.nn.sigmoid(values)
    return logistic * (1.0 + values * (1.0 - logistic))


def columns_of(row):
    return jnp.broadcast_to(row, (CHANS, CHANS)).T


def readout_kernel(
    scale, weight, gathered_ref, target_ref, w_hidden_ref, b_hidden_ref, w_out_ref,
    density_ref, upstream_ref, head_ref,
):
    summed = gathered_ref[0]
    for shard in range(1, gathered_ref.shape[0]):
        summed = summed + gathered_ref[shard]
    w_hidden = w_hidden_ref[...]
    w_out = columns_of(w_out_ref[...])
    hidden_pre = along_first(w_hidden, summed, PRECISE) + columns_of(b_hidden_ref[...])
    activated = jax.nn.silu(hidden_pre)
    density = jnp.sum(activated * w_out, axis=0, keepdims=True)
    density_ref[...] = density
    error = density - target_ref[...]
    error_grad = error * scale
    pre_grad = w_out * silu_slope(hidden_pre) * error_grad
    upstream_ref[...] = matmul(w_hidden, pre_grad, PRECISE)
    head_ref[0:CHANS, :] = along_last(summed, pre_grad, PRECISE) * weight
    bias = jnp.sum(pre_grad.T, axis=0, keepdims=True) * weight
    out = jnp.sum((activated * error_grad).T, axis=0, keepdims=True) * weight
    loss = error * error * (0.5 * scale * weight)
    head_ref[CHANS : CHANS + 16, :] = jnp.concatenate(
        [bias, out, loss, jnp.zeros((13, CHANS), F32)], axis=0
    )


def backward_kernel(
    feats_ref, species_ref, w_deg_ref, w_gate_ref, spread_ref, sums_ref, radial_ref, basis_ref,
    head_ref, *refs,
):
    upstreams = refs[:SOURCES]
    payload_ref = refs[SOURCES]
    upstream = jnp.concatenate([ref[...] for ref in upstreams for slot in range(SLOTS)], axis=1)
    scalar = feats_ref[:, lanes(0)]
    gates = jax.nn.sigmoid(matmul(scalar, w_gate_ref[...]))
    radial_grads = []
    for degree in range(DEGREES):
        low, high = first_rows(degree)
        inner = (radial_ref[lanes(degree), :] * upstream).astype(BF16)
        grads = along_last(spread_ref[low:high, :], inner)
        radial_grads.append(
            along_last(basis_ref[...], sums_ref[lanes(degree), :] * upstream, PRECISE)
        )
        rows = component_rows(feats_ref, degree)
        mixed = matmul(rows, w_deg_ref[degree])
        if degree == 0:
            mixed_grad = grads * silu_slope(mixed)
            embed_grad = matmul(kind_rows(species_ref), grads, PRECISE)
        else:
            gate = gates[:, lanes(degree - 1)]
            mixed_grad = grads * over_components(gate, degree)
            product = grads * mixed
            total = product[0:ATOMS, :]
            for comp in range(1, 2 * degree + 1):
                total = total + product[comp * ATOMS : (comp + 1) * ATOMS, :]
            pre = (total * gate * (1.0 - gate)).astype(BF16)
            start = (DEGREES + degree - 1) * CHANS
            payload_ref[start : start + CHANS, :] = along_first(scalar, pre).astype(BF16)
        payload_ref[degree * CHANS : (degree + 1) * CHANS, :] = along_first(
            rows, mixed_grad.astype(BF16)
        ).astype(BF16)
    base = (2 * DEGREES - 1) * CHANS
    payload_ref[base : base + CHANS + 16, :] = head_ref[...].astype(BF16)
    base += CHANS + 16
    payload_ref[base : base + 48, :] = jnp.concatenate(
        radial_grads + [embed_grad], axis=0
    ).astype(BF16)
    base += 48
    payload_ref[base:, :] = jnp.zeros((PAYLOAD - base, CHANS), BF16)


def unpack_kernel(
    payload_ref, loss_ref, deg_ref, gate_ref, embed_ref, radial_ref, hidden_ref, bias_ref, out_ref
):
    for degree in range(DEGREES):
        deg_ref[degree] = payload_ref[lanes(degree), :].astype(F32)
    for degree in range(1, DEGREES):
        gate_ref[:, lanes(degree - 1)] = payload_ref[lanes(DEGREES + degree - 1), :].astype(F32)
    base = (2 * DEGREES - 1) * CHANS
    hidden_ref[...] = payload_ref[base : base + CHANS, :].astype(F32)
    base += CHANS
    misc = payload_ref[base : base + 16, :].astype(F32)
    bias_ref[...] = misc[0:1, :]
    out_ref[...] = misc[1:2, :]
    loss_ref[...] = jnp.sum(misc[2:3, :], axis=1, keepdims=True)
    base += 16
    small = payload_ref[base : base + 48, :].astype(F32)
    for degree in range(DEGREES):
        radial_ref[:, lanes(degree)] = small[degree * BASES : (degree + 1) * BASES, :]
    embed_ref[...] = small[DEGREES * BASES :, :]


def shape(dims, dtype=F32):
    return jax.ShapeDtypeStruct(dims, dtype)


def call(kernel, outs, name):
    return pl.pallas_call(
        kernel,
        out_shape=outs,
        name=name,
        compiler_params=pltpu.CompilerParams(vmem_limit_bytes=48 * 1024 * 1024),
    )


def passed_along(block, distance):
    count = lax.axis_size(SLAB)
    route = [(i, (i + distance) % count) for i in range(count)]
    return lax.ppermute(block, SLAB, route)


def to_all(block, axes):
    count = lax.axis_size(axes)
    return lax.all_to_all(jnp.broadcast_to(block[None], (count,) + block.shape), axes, 0, 0)


def sum_parts(parts):
    return jnp.sum(parts.astype(F32), axis=0).astype(BF16)


def reduce_all(payload):
    count = lax.axis_size(PLANE)
    parts = payload.reshape(count, PAYLOAD // count, CHANS)
    part = sum_parts(lax.all_to_all(parts, PLANE, 0, 0))
    part = sum_parts(to_all(part, ("z",)))
    return to_all(part, PLANE).reshape(PAYLOAD, CHANS)


def on_device(
    atom_feats, species, send_rows, neighbours, harmonics, distances, target,
    w_deg, w_gate, embed, w_radial, w_hidden, b_hidden, w_out,
):
    slab_count = lax.axis_size(SLAB)
    shard_count = lax.axis_size(ATOM)
    scale = 1.0 / math.sqrt(PROBES * slab_count)
    species = species.reshape(1, ATOMS)
    lists = send_rows[0, 0]
    with jax.named_scope("pack_pairs"):
        pack = jnp.concatenate(
            [
                harmonics.transpose(1, 0, 2),
                distances[:, None, :],
                neighbours.astype(F32)[:, None, :],
                jnp.zeros((SLOTS, FIELDS - COMPS - 2, PROBES), F32),
            ],
            axis=1,
        )
    with jax.named_scope("exchange_pairs"):
        packs = [pack] + [passed_along(pack, -offset) for offset in OFFSETS]
    rows = call(encode_kernel, shape((COMPS * ATOMS, CHANS), BF16), "encode")(
        atom_feats, species, w_deg, w_gate, embed
    )
    outs = call(
        pair_kernel,
        [shape((CHANS, PROBES))] * SOURCES
        + [
            shape((COMPS * ATOMS, PAIRS), BF16),
            shape((DEGREES * CHANS, PAIRS)),
            shape((DEGREES * CHANS, PAIRS)),
            shape((BASES, PAIRS)),
        ],
        "pair_sums",
    )(rows, lists, w_radial, *packs)
    values = outs[:SOURCES]
    spread, sums, radial, basis = outs[SOURCES:]
    with jax.named_scope("exchange_sums"):
        partial_value = values[0]
        for which, offset in enumerate(OFFSETS):
            partial_value = partial_value + passed_along(values[1 + which], offset)
    with jax.named_scope("gather_shards"):
        gathered = to_all(partial_value, ATOM)
    density, upstream, head = call(
        functools.partial(readout_kernel, scale, 1.0 / shard_count),
        [shape((1, PROBES)), shape((CHANS, PROBES)), shape((CHANS + 16, CHANS))],
        "readout",
    )(
        gathered, target.reshape(1, PROBES), w_hidden, b_hidden.reshape(1, CHANS),
        w_out.reshape(1, CHANS),
    )
    with jax.named_scope("exchange_grads"):
        upstreams = [upstream] + [passed_along(upstream, -offset) for offset in OFFSETS]
    payload = call(backward_kernel, shape((PAYLOAD, CHANS), BF16), "backward")(
        atom_feats, species, w_deg, w_gate, spread, sums, radial, basis, head, *upstreams
    )
    with jax.named_scope("reduce_grads"):
        payload = reduce_all(payload)
    loss, deg, gate, embed_grad, radial_grad, hidden, bias, out = call(
        unpack_kernel,
        [
            shape((1, 1)),
            shape((DEGREES, CHANS, CHANS)),
            shape((CHANS, (DEGREES - 1) * CHANS)),
            shape((KINDS, CHANS)),
            shape((BASES, DEGREES * CHANS)),
            shape((CHANS, CHANS)),
            shape((1, CHANS)),
            shape((1, CHANS)),
        ],
        "unpack",
    )(payload)
    return (
        loss.reshape(()), density.reshape(PROBES), deg, gate, embed_grad, radial_grad, hidden,
        bias.reshape(CHANS), out.reshape(CHANS),
    )


def solution(mesh):
    slabs, shards = mesh.devices.shape
    fine = Mesh(mesh.devices.reshape(slabs // 4, 4, shards // 2, 2), ("z", "y", "x", "c"))
    in_specs = (
        P(SLAB + ATOM, None),
        P(SLAB + ATOM),
        P(SLAB, ATOM, None, None),
        P(ATOM, SLAB),
        P(None, ATOM, SLAB),
        P(ATOM, SLAB),
        P(SLAB),
        P(),
        P(),
        P(),
        P(),
        P(),
        P(),
        P(),
    )
    out_specs = (P(), P(SLAB), P(), P(), P(), P(), P(), P(), P())
    return jax.shard_map(
        on_device, mesh=fine, in_specs=in_specs, out_specs=out_specs, check_vma=False
    )
```

```python
import functools
import math

import jax
import jax.numpy as jnp
from jax import lax
from jax.experimental import pallas as pl
from jax.experimental.pallas import tpu as pltpu
from jax.sharding import Mesh, PartitionSpec as P

OFFSETS = (-2, -1, 1, 2)
CUTOFF = 4.0
PRECISE = lax.Precision.HIGHEST
F32 = jnp.float32
BF16 = jnp.bfloat16
SLAB = ("z", "y")
ATOM = ("x", "c")
PLANE = ("y", "x", "c")
DEGREES = 5
COMPS = DEGREES * DEGREES
CHANS = 128
ATOMS = 64
SLOTS = 2
PROBES = 128
DELTAS = (0,) + OFFSETS
SOURCES = len(DELTAS)
SPAN = SLOTS * PROBES
PAIRS = SOURCES * SPAN
FIELDS = 32
BASES = 8
KINDS = 8
PAYLOAD = 1536


def first_rows(degree):
    return degree * degree * ATOMS, (degree + 1) * (degree + 1) * ATOMS


def lanes(block):
    return slice(block * CHANS, (block + 1) * CHANS)


def along_first(left, right, precision=None):
    return lax.dot_general(
        left, right, (((0,), (0,)), ((), ())), preferred_element_type=F32, precision=precision
    )


def along_last(left, right, precision=None):
    return lax.dot_general(
        left, right, (((1,), (1,)), ((), ())), preferred_element_type=F32, precision=precision
    )


def matmul(left, right, precision=None):
    return jnp.dot(left, right, preferred_element_type=F32, precision=precision)


def component_rows(feats_ref, degree):
    parts = [feats_ref[:, lanes(m)] for m in range(degree * degree, (degree + 1) * (degree + 1))]
    return parts[0] if degree == 0 else jnp.concatenate(parts, axis=0)


def over_components(gate, degree):
    return jnp.concatenate([gate] * (2 * degree + 1), axis=0)


def kind_rows(species_ref):
    ids = lax.broadcasted_iota(jnp.int32, (KINDS, ATOMS), 0)
    return (ids == species_ref[...]).astype(F32)


def encode_kernel(
    feats_hbm, species_ref, w_deg_hbm, w_gate_hbm, embed_ref, lists_ref, w_radial_ref,
    rows_ref, owners_ref, split_ref, feats_ref, w_deg_ref, w_gate_ref, sems,
):
    copies = [
        pltpu.make_async_copy(source, target, sems.at[index])
        for index, (source, target) in enumerate(
            ((w_gate_hbm, w_gate_ref), (feats_hbm, feats_ref), (w_deg_hbm, w_deg_ref))
        )
    ]
    for copy in copies:
        copy.start()
    ids = lax.broadcasted_iota(jnp.int32, (ATOMS, ATOMS), 0)
    for which in range(len(OFFSETS)):
        owners_ref[which] = (ids == lists_ref[which : which + 1, :]).astype(BF16)
    split_ref[...] = stacked(w_radial_ref[...], (0, 0, 1, 1, 0, 2))
    for copy in copies:
        copy.wait()
    scalar = feats_ref[:, lanes(0)]
    gates = jax.nn.sigmoid(matmul(scalar, w_gate_ref[...]))
    for degree in range(DEGREES):
        low, high = first_rows(degree)
        rows = component_rows(feats_ref, degree)
        mixed = matmul(rows, w_deg_ref[degree])
        if degree == 0:
            added = jax.nn.silu(mixed) + along_first(
                kind_rows(species_ref), embed_ref[...], PRECISE
            )
        else:
            added = mixed * over_components(gates[:, lanes(degree - 1)], degree)
        rows_ref[low:high, :] = (rows.astype(F32) + added).astype(BF16)


def parts_of(values):
    high = values.astype(BF16)
    rest = values - high.astype(F32)
    middle = rest.astype(BF16)
    low = (rest - middle.astype(F32)).astype(BF16)
    return high, middle, low


def stacked(values, order):
    parts = [part.astype(F32) for part in parts_of(values)]
    return jnp.concatenate([parts[index] for index in order], axis=0).astype(BF16)


def plane_place(delta):
    row = lax.axis_index("y") + delta
    below, above = row < 0, row > 3
    place = jnp.where(below, row + 2, jnp.where(above, row - 2, row))
    return place, jnp.where(jnp.logical_or(below, above), 1, 0)


def pack_kernel(harm_ref, dist_ref, nbr_ref, target_ref, pack_ref):
    pack_ref[0:COMPS] = harm_ref[...]
    pack_ref[COMPS] = dist_ref[...]
    pack_ref[COMPS + 1] = nbr_ref[...].astype(F32)
    pack_ref[COMPS + 2] = jnp.broadcast_to(target_ref[...], (SLOTS, PROBES))
    pack_ref[COMPS + 3 :] = jnp.zeros((FIELDS - COMPS - 3, SLOTS, PROBES), F32)


def pair_kernel(
    packs_ref, rows_ref, owners_ref, split_ref,
    out_ref, spread_ref, sums_ref, radial_ref, basis_ref,
):
    shards, chunk = out_ref.shape[1], out_ref.shape[3]
    sub = lax.broadcasted_iota(jnp.int32, (ATOMS, PROBES), 0).astype(F32)
    dists, places = [], []
    for source in range(SOURCES):
        place, part = plane_place(DELTAS[source])
        places.append((place, part))
        for slot in range(SLOTS):
            start = source * SPAN + slot * PROBES

            def row(field):
                return packs_ref[place, part, field, slot : slot + 1, :]

            hot = (row(COMPS + 1) - float(source * ATOMS) == sub).astype(F32)
            if source > 0:
                hot = matmul(owners_ref[source - 1], hot.astype(BF16))
            for m in range(COMPS):
                spread_ref[m * ATOMS : (m + 1) * ATOMS, start : start + PROBES] = (
                    hot * row(m)
                ).astype(BF16)
            dists.append(row(COMPS))
    dist = jnp.concatenate(dists, axis=1)
    orders = lax.broadcasted_iota(jnp.int32, (BASES, PAIRS), 0).astype(F32) + 1.0
    phase = math.pi * dist / CUTOFF
    envelope = 0.5 * (jnp.cos(phase) + 1.0) / dist
    basis = jnp.sin(phase * orders) * envelope
    basis_ref[...] = basis
    basis_split = stacked(basis, (0, 1, 0, 1, 2, 0))
    total = None
    for degree in range(DEGREES):
        low, high = first_rows(degree)
        radial = along_first(split_ref[:, lanes(degree)], basis_split)
        radial_ref[lanes(degree), :] = radial
        sums = along_first(rows_ref[low:high, :], spread_ref[low:high, :])
        sums_ref[lanes(degree), :] = sums
        term = radial * sums
        total = term if total is None else total + term
    out_ref[...] = jnp.zeros(out_ref.shape, F32)
    for source in range(SOURCES):
        start = source * SPAN
        value = (total[:, start : start + PROBES] + total[:, start + PROBES : start + SPAN]).T
        place, part = places[source]
        for shard in range(shards):
            out_ref[place, shard, part] = value[shard * chunk : (shard + 1) * chunk, :]


def silu_slope(values):
    logistic = jax.nn.sigmoid(values)
    return logistic * (1.0 + values * (1.0 - logistic))


def sum_kernel(parts_ref, out_ref):
    total = parts_ref[0].astype(F32)
    for index in range(1, parts_ref.shape[0]):
        total = total + parts_ref[index].astype(F32)
    if len(out_ref.shape) == len(parts_ref.shape):
        for copy in range(out_ref.shape[0]):
            out_ref[copy] = total.astype(out_ref.dtype)
    else:
        out_ref[...] = total.astype(out_ref.dtype)


def readout_kernel(
    scale, mine_ref, theirs_ref, pack_ref, their_pack_ref, w_hidden_ref, b_hidden_ref, w_out_ref,
    up_ref, head_ref, column_ref,
):
    chunk = mine_ref.shape[1]
    shard = lax.axis_index("x") * lax.axis_size("c") + lax.axis_index("c")
    start = pl.multiple_of(shard * chunk, chunk)
    summed = jnp.concatenate(
        [mine_ref[0] + theirs_ref[1], theirs_ref[0] + mine_ref[1]], axis=0
    )
    targets = []
    for ref in (pack_ref, their_pack_ref):
        column_ref[...] = jnp.broadcast_to(ref[COMPS + 2, 0:1, :], (PROBES, PROBES)).T
        targets.append(column_ref[pl.ds(start, chunk), :])
    target = jnp.concatenate(targets, axis=0)
    w_hidden = w_hidden_ref[...]
    w_out = w_out_ref[...]
    hidden_pre = matmul(summed, w_hidden, PRECISE) + b_hidden_ref[...]
    activated = jax.nn.silu(hidden_pre)
    density = jnp.sum(activated * w_out, axis=1, keepdims=True)
    error = density - target
    error_grad = error * scale
    pre_grad = w_out * silu_slope(hidden_pre) * error_grad
    spot = lax.broadcasted_iota(jnp.int32, (chunk, PROBES), 0) + start
    mask = (spot == lax.broadcasted_iota(jnp.int32, (chunk, PROBES), 1)).astype(F32)
    up_ref[0 : 2 * chunk, :] = along_last(pre_grad, w_hidden, PRECISE)
    density_row = jnp.sum(mask * density[0:chunk, :], axis=0, keepdims=True)
    up_ref[2 * chunk :, :] = jnp.broadcast_to(density_row, (8, PROBES))
    mine, own_error = pre_grad[0:chunk, :], error[0:chunk, :]
    head_ref[0:CHANS, :] = along_first(summed[0:chunk, :], mine, PRECISE)
    bias = jnp.sum(mine, axis=0, keepdims=True)
    out = jnp.sum(activated[0:chunk, :] * error_grad[0:chunk, :], axis=0, keepdims=True)
    loss = jnp.sum(mask * own_error * own_error * (0.5 * scale), axis=0, keepdims=True)
    head_ref[CHANS : CHANS + 16, :] = jnp.concatenate(
        [bias, out, loss, jnp.zeros((13, CHANS), F32)], axis=0
    )


def backward_kernel(
    feats_ref, species_ref, w_deg_ref, w_gate_ref, spread_ref, sums_ref, radial_ref, basis_ref,
    head_ref, up_ref, payload_ref, density_ref,
):
    shards = up_ref.shape[1]
    chunk = PROBES // shards
    blocks = []
    for delta in DELTAS:
        place, part = plane_place(delta)
        begin = pl.multiple_of(part * chunk, chunk)
        block = jnp.concatenate(
            [up_ref[place, shard, pl.ds(begin, chunk), :] for shard in range(shards)], axis=0
        ).T
        blocks += [block] * SLOTS
    upstream = jnp.concatenate(blocks, axis=1)
    density = None
    for shard in range(shards):
        row = up_ref[lax.axis_index("y"), shard, 2 * chunk : 2 * chunk + 1, :]
        density = row if density is None else density + row
    density_ref[...] = density
    scalar = feats_ref[:, lanes(0)]
    gates = jax.nn.sigmoid(matmul(scalar, w_gate_ref[...]))
    basis_split = stacked(basis_ref[...], (0, 1))
    radial_grads = []
    for degree in range(DEGREES):
        low, high = first_rows(degree)
        inner = (radial_ref[lanes(degree), :] * upstream).astype(BF16)
        grads = along_last(spread_ref[low:high, :], inner)
        product = sums_ref[lanes(degree), :] * upstream
        main = product.astype(BF16)
        rest = (product - main.astype(F32)).astype(BF16)
        both = along_last(main, basis_split) + along_last(rest, basis_split)
        radial_grads.append((both[:, 0:BASES] + both[:, BASES : 2 * BASES]).T)
        rows = component_rows(feats_ref, degree)
        mixed = matmul(rows, w_deg_ref[degree])
        if degree == 0:
            mixed_grad = grads * silu_slope(mixed)
            embed_grad = matmul(kind_rows(species_ref), grads, PRECISE)
        else:
            gate = gates[:, lanes(degree - 1)]
            mixed_grad = grads * over_components(gate, degree)
            product = grads * mixed
            total = product[0:ATOMS, :]
            for comp in range(1, 2 * degree + 1):
                total = total + product[comp * ATOMS : (comp + 1) * ATOMS, :]
            pre = (total * gate * (1.0 - gate)).astype(BF16)
            start = (DEGREES + degree - 1) * CHANS
            payload_ref[start : start + CHANS, :] = along_first(scalar, pre).astype(BF16)
        payload_ref[degree * CHANS : (degree + 1) * CHANS, :] = along_first(
            rows, mixed_grad.astype(BF16)
        ).astype(BF16)
    base = (2 * DEGREES - 1) * CHANS
    payload_ref[base : base + CHANS + 16, :] = head_ref[...].astype(BF16)
    base += CHANS + 16
    payload_ref[base : base + 48, :] = jnp.concatenate(
        radial_grads + [embed_grad], axis=0
    ).astype(BF16)
    base += 48
    payload_ref[base:, :] = jnp.zeros((PAYLOAD - base, CHANS), BF16)


def unpack_kernel(
    payload_ref, loss_ref, deg_ref, gate_ref, embed_ref, radial_ref, hidden_ref, bias_ref, out_ref
):
    for degree in range(DEGREES):
        deg_ref[degree] = payload_ref[lanes(degree), :].astype(F32)
    for degree in range(1, DEGREES):
        gate_ref[:, lanes(degree - 1)] = payload_ref[lanes(DEGREES + degree - 1), :].astype(F32)
    base = (2 * DEGREES - 1) * CHANS
    hidden_ref[...] = payload_ref[base : base + CHANS, :].astype(F32)
    base += CHANS
    misc = payload_ref[base : base + 16, :].astype(F32)
    bias_ref[...] = misc[0:1, :]
    out_ref[...] = misc[1:2, :]
    loss_ref[...] = jnp.sum(misc[2:3, :], axis=1, keepdims=True)
    base += 16
    small = payload_ref[base : base + 48, :].astype(F32)
    for degree in range(DEGREES):
        radial_ref[:, lanes(degree)] = small[degree * BASES : (degree + 1) * BASES, :]
    embed_ref[...] = small[DEGREES * BASES :, :]


def shape(dims, dtype=F32):
    return jax.ShapeDtypeStruct(dims, dtype)


def call(kernel, outs, name, **options):
    return pl.pallas_call(
        kernel,
        out_shape=outs,
        name=name,
        compiler_params=pltpu.CompilerParams(vmem_limit_bytes=48 * 1024 * 1024),
        **options,
    )


def to_partner(block):
    count = lax.axis_size(SLAB)
    route = [(i, (i + (2 if i % 4 >= 2 else -2)) % count) for i in range(count)]
    return lax.ppermute(block, SLAB, route)


def to_all(block, axes):
    count = lax.axis_size(axes)
    return lax.all_to_all(jnp.broadcast_to(block[None], (count,) + block.shape), axes, 0, 0)


def reduce_all(payload):
    count = lax.axis_size(PLANE)
    depth = lax.axis_size("z")
    rows = PAYLOAD // count
    parts = lax.all_to_all(payload.reshape(count, rows, CHANS), PLANE, 0, 0)
    copies = call(sum_kernel, shape((depth, rows, CHANS), BF16), "sum_plane")(parts)
    parts = lax.all_to_all(copies, "z", 0, 0)
    copies = call(sum_kernel, shape((count, rows, CHANS), BF16), "sum_depth")(parts)
    return lax.all_to_all(copies, PLANE, 0, 0).reshape(PAYLOAD, CHANS)


def on_device(
    atom_feats, species, send_rows, neighbours, harmonics, distances, target,
    w_deg, w_gate, embed, w_radial, w_hidden, b_hidden, w_out,
):
    slab_count = lax.axis_size(SLAB)
    shards = lax.axis_size(ATOM)
    chunk = PROBES // shards
    scale = 1.0 / math.sqrt(PROBES * slab_count)
    species = species.reshape(1, ATOMS)
    pack = call(pack_kernel, shape((FIELDS, SLOTS, PROBES)), "pack")(
        harmonics, distances, neighbours, target.reshape(1, PROBES)
    )
    with jax.named_scope("exchange_pairs"):
        their_pack = to_partner(pack)
    whole = pl.BlockSpec(memory_space=pltpu.VMEM)
    apart = pl.BlockSpec(memory_space=pl.ANY)
    rows, owners, split = call(
        encode_kernel,
        [
            shape((COMPS * ATOMS, CHANS), BF16),
            shape((len(OFFSETS), ATOMS, ATOMS), BF16),
            shape((6 * BASES, DEGREES * CHANS), BF16),
        ],
        "encode",
        in_specs=[apart, whole, apart, apart, whole, whole, whole],
        scratch_shapes=[
            pltpu.VMEM(atom_feats.shape, BF16),
            pltpu.VMEM(w_deg.shape, BF16),
            pltpu.VMEM(w_gate.shape, BF16),
            pltpu.SemaphoreType.DMA((3,)),
        ],
    )(atom_feats, species, w_deg, w_gate, embed, send_rows[0, 0], w_radial)
    with jax.named_scope("gather_pairs"):
        packs = to_all(jnp.stack([pack, their_pack]), "y")
    values, spread, sums, radial, basis = call(
        pair_kernel,
        [
            shape((4, shards, 2, chunk, CHANS)),
            shape((COMPS * ATOMS, PAIRS), BF16),
            shape((DEGREES * CHANS, PAIRS)),
            shape((DEGREES * CHANS, PAIRS)),
            shape((BASES, PAIRS)),
        ],
        "pair_sums",
    )(packs, rows, owners, split)
    with jax.named_scope("scatter_sums"):
        parts = lax.all_to_all(values.reshape(4 * shards, 2, chunk, CHANS), PLANE, 0, 0)
    mine = call(sum_kernel, shape((2, chunk, CHANS)), "sum_sources")(parts)
    with jax.named_scope("exchange_sums"):
        theirs = to_partner(mine)
    up, head = call(
        functools.partial(readout_kernel, scale),
        [shape((2 * chunk + 8, CHANS)), shape((CHANS + 16, CHANS))],
        "readout",
        scratch_shapes=[pltpu.VMEM((PROBES, PROBES), F32)],
    )(
        mine, theirs, pack, their_pack, w_hidden, b_hidden.reshape(1, CHANS),
        w_out.reshape(1, CHANS),
    )
    with jax.named_scope("gather_grads"):
        ups = to_all(up, PLANE).reshape(4, shards, 2 * chunk + 8, CHANS)
    payload, density = call(
        backward_kernel, [shape((PAYLOAD, CHANS), BF16), shape((1, PROBES))], "backward"
    )(atom_feats, species, w_deg, w_gate, spread, sums, radial, basis, head, ups)
    with jax.named_scope("reduce_grads"):
        payload = reduce_all(payload)
    loss, deg, gate, embed_grad, radial_grad, hidden, bias, out = call(
        unpack_kernel,
        [
            shape((1, 1)),
            shape((DEGREES, CHANS, CHANS)),
            shape((CHANS, (DEGREES - 1) * CHANS)),
            shape((KINDS, CHANS)),
            shape((BASES, DEGREES * CHANS)),
            shape((CHANS, CHANS)),
            shape((1, CHANS)),
            shape((1, CHANS)),
        ],
        "unpack",
    )(payload)
    return (
        loss.reshape(()), density.reshape(PROBES), deg, gate, embed_grad, radial_grad, hidden,
        bias.reshape(CHANS), out.reshape(CHANS),
    )


def solution(mesh):
    slabs, shards = mesh.devices.shape
    fine = Mesh(mesh.devices.reshape(slabs // 4, 4, shards // 2, 2), ("z", "y", "x", "c"))
    in_specs = (
        P(SLAB + ATOM, None),
        P(SLAB + ATOM),
        P(SLAB, ATOM, None, None),
        P(ATOM, SLAB),
        P(None, ATOM, SLAB),
        P(ATOM, SLAB),
        P(SLAB),
        P(),
        P(),
        P(),
        P(),
        P(),
        P(),
        P(),
    )
    out_specs = (P(), P(SLAB), P(), P(), P(), P(), P(), P(), P())
    return jax.shard_map(
        on_device, mesh=fine, in_specs=in_specs, out_specs=out_specs, check_vma=False
    )
```

```python
import functools
import math

import jax
import jax.numpy as jnp
from jax import lax
from jax.experimental import pallas as pl
from jax.experimental.pallas import tpu as pltpu
from jax.sharding import Mesh, PartitionSpec as P

OFFSETS = (-2, -1, 1, 2)
CUTOFF = 4.0
PRECISE = lax.Precision.HIGHEST
F32 = jnp.float32
BF16 = jnp.bfloat16
SLAB = ("z", "y")
ATOM = ("x", "c")
PLANE = ("y", "x", "c")
DEGREES = 5
COMPS = DEGREES * DEGREES
CHANS = 128
ATOMS = 64
SLOTS = 2
PROBES = 128
DELTAS = (0,) + OFFSETS
SOURCES = len(DELTAS)
SPAN = SLOTS * PROBES
PAIRS = SOURCES * SPAN
FIELDS = 32
BASES = 8
KINDS = 8
PAYLOAD = 1536
LIMIT = 63


def first_rows(degree):
    return degree * degree * ATOMS, (degree + 1) * (degree + 1) * ATOMS


def lanes(block):
    return slice(block * CHANS, (block + 1) * CHANS)


def along_first(left, right, precision=None):
    return lax.dot_general(
        left, right, (((0,), (0,)), ((), ())), preferred_element_type=F32, precision=precision
    )


def along_last(left, right, precision=None):
    return lax.dot_general(
        left, right, (((1,), (1,)), ((), ())), preferred_element_type=F32, precision=precision
    )


def matmul(left, right, precision=None):
    return jnp.dot(left, right, preferred_element_type=F32, precision=precision)


def component_rows(feats_ref, degree):
    parts = [feats_ref[:, lanes(m)] for m in range(degree * degree, (degree + 1) * (degree + 1))]
    return parts[0] if degree == 0 else jnp.concatenate(parts, axis=0)


def over_components(gate, degree):
    return jnp.concatenate([gate] * (2 * degree + 1), axis=0)


def kind_rows(species_ref):
    ids = lax.broadcasted_iota(jnp.int32, (KINDS, ATOMS), 0)
    return (ids == species_ref[...]).astype(F32)


def started(pairs, sems):
    copies = [
        pltpu.make_async_copy(source, target, sems.at[index])
        for index, (source, target) in enumerate(pairs)
    ]
    for copy in copies:
        copy.start()
    return copies


def encode_kernel(
    feats_hbm, species_hbm, w_deg_hbm, w_gate_hbm, embed_hbm, lists_hbm, w_radial_hbm,
    rows_ref, owners_ref, split_ref,
    feats_ref, species_ref, w_deg_ref, w_gate_ref, embed_ref, lists_ref, w_radial_ref, sems,
):
    copies = started(
        (
            (feats_hbm, feats_ref),
            (species_hbm, species_ref),
            (w_deg_hbm, w_deg_ref),
            (w_gate_hbm, w_gate_ref),
            (embed_hbm, embed_ref),
            (lists_hbm, lists_ref),
            (w_radial_hbm, w_radial_ref),
        ),
        sems,
    )
    for copy in copies:
        copy.wait()
    ids = lax.broadcasted_iota(jnp.int32, (ATOMS, ATOMS), 0)
    for which in range(len(OFFSETS)):
        owners_ref[which] = (ids == lists_ref[which : which + 1, :]).astype(BF16)
    split_ref[...] = stacked(w_radial_ref[...], (0, 0, 1, 1, 0, 2))
    scalar = feats_ref[:, lanes(0)]
    gates = jax.nn.sigmoid(matmul(scalar, w_gate_ref[...]))
    for degree in range(DEGREES):
        low, high = first_rows(degree)
        rows = component_rows(feats_ref, degree)
        mixed = matmul(rows, w_deg_ref[degree])
        if degree == 0:
            added = jax.nn.silu(mixed) + along_first(
                kind_rows(species_ref), embed_ref[...], PRECISE
            )
        else:
            added = mixed * over_components(gates[:, lanes(degree - 1)], degree)
        rows_ref[low:high, :] = (rows.astype(F32) + added).astype(BF16)


def parts_of(values):
    high = values.astype(BF16)
    rest = values - high.astype(F32)
    middle = rest.astype(BF16)
    low = (rest - middle.astype(F32)).astype(BF16)
    return high, middle, low


def stacked(values, order):
    parts = [part.astype(F32) for part in parts_of(values)]
    return jnp.concatenate([parts[index] for index in order], axis=0).astype(BF16)


def plane_place(delta):
    row = lax.axis_index("y") + delta
    below, above = row < 0, row > 3
    place = jnp.where(below, row + 2, jnp.where(above, row - 2, row))
    return place, jnp.where(jnp.logical_or(below, above), 1, 0)


def pack_kernel(harm_hbm, dist_hbm, nbr_hbm, target_hbm, pack_ref, nbr_ref, target_ref, sems):
    copies = started(
        (
            (harm_hbm, pack_ref.at[pl.ds(0, COMPS)]),
            (dist_hbm, pack_ref.at[COMPS]),
            (nbr_hbm, nbr_ref),
            (target_hbm, target_ref),
        ),
        sems,
    )
    for copy in copies:
        copy.wait()
    pack_ref[COMPS + 1] = nbr_ref[...].astype(F32)
    pack_ref[COMPS + 2] = jnp.broadcast_to(target_ref[...], (SLOTS, PROBES))
    pack_ref[COMPS + 3 :] = jnp.zeros((FIELDS - COMPS - 3, SLOTS, PROBES), F32)


def pair_kernel(
    packs_hbm, rows_hbm, owners_hbm, split_hbm, out_hbm, spread_hbm, sums_hbm,
    packs_ref, rows_ref, owners_ref, split_ref, sems,
    out_ref, spread_ref, sums_ref, out_sems,
):
    copies = started(
        (
            (packs_hbm, packs_ref),
            (owners_hbm, owners_ref),
            (split_hbm, split_ref),
            (rows_hbm, rows_ref),
        ),
        sems,
    )
    shards, chunk = out_ref.shape[1], out_ref.shape[3]
    out_ref[...] = jnp.zeros(out_ref.shape, F32)
    copies[0].wait()
    sub = lax.broadcasted_iota(jnp.int32, (ATOMS, PROBES), 0).astype(F32)
    dists, places = [], []
    for source in range(SOURCES):
        place, part = plane_place(DELTAS[source])
        places.append((place, part))
        if source == 1:
            copies[1].wait()
        for slot in range(SLOTS):
            start = source * SPAN + slot * PROBES

            def row(field):
                return packs_ref[place, part, field, slot : slot + 1, :]

            hot = (row(COMPS + 1) - float(source * ATOMS) == sub).astype(F32)
            if source > 0:
                hot = matmul(owners_ref[source - 1], hot.astype(BF16))
            for m in range(COMPS):
                spread_ref[m * ATOMS : (m + 1) * ATOMS, start : start + PROBES] = (
                    hot * row(m)
                ).astype(BF16)
            dists.append(row(COMPS))
    writes = started(((spread_ref, spread_hbm),), out_sems)
    dist = jnp.concatenate(dists, axis=1)
    orders = lax.broadcasted_iota(jnp.int32, (BASES, PAIRS), 0).astype(F32) + 1.0
    phase = math.pi * dist / CUTOFF
    envelope = 0.5 * (jnp.cos(phase) + 1.0) / dist
    basis = jnp.sin(phase * orders) * envelope
    basis_split = stacked(basis, (0, 1, 0, 1, 2, 0))
    sums_ref[DEGREES * CHANS :, :] = basis_split
    copies[2].wait()
    copies[3].wait()
    total = None
    for degree in range(DEGREES):
        low, high = first_rows(degree)
        radial = along_first(split_ref[:, lanes(degree)], basis_split)
        sums = along_first(rows_ref[low:high, :], spread_ref[low:high, :])
        sums_ref[lanes(degree), :] = sums.astype(BF16)
        term = radial * sums
        total = term if total is None else total + term
    for source in range(SOURCES):
        start = source * SPAN
        value = (total[:, start : start + PROBES] + total[:, start + PROBES : start + SPAN]).T
        place, part = places[source]
        for shard in range(shards):
            out_ref[place, shard, part] = value[shard * chunk : (shard + 1) * chunk, :]
    writes += started(
        ((out_ref, out_hbm), (sums_ref, sums_hbm)),
        out_sems.at[pl.ds(1, 2)],
    )
    for write in writes:
        write.wait()


def silu_slope(values):
    logistic = jax.nn.sigmoid(values)
    return logistic * (1.0 + values * (1.0 - logistic))


def sum_kernel(parts_ref, out_ref):
    total = parts_ref[0].astype(F32)
    for index in range(1, parts_ref.shape[0]):
        total = total + parts_ref[index].astype(F32)
    if len(out_ref.shape) == len(parts_ref.shape):
        for copy in range(out_ref.shape[0]):
            out_ref[copy] = total.astype(out_ref.dtype)
    else:
        out_ref[...] = total.astype(out_ref.dtype)


def readout_kernel(
    scale, mine_ref, theirs_ref, pack_ref, their_pack_ref, w_hidden_ref, b_hidden_ref, w_out_ref,
    up_ref, head_ref, column_ref,
):
    chunk = mine_ref.shape[1]
    shard = lax.axis_index("x") * lax.axis_size("c") + lax.axis_index("c")
    start = pl.multiple_of(shard * chunk, chunk)
    summed = jnp.concatenate(
        [mine_ref[0] + theirs_ref[1], theirs_ref[0] + mine_ref[1]], axis=0
    )
    targets = []
    for ref in (pack_ref, their_pack_ref):
        column_ref[...] = jnp.broadcast_to(ref[COMPS + 2, 0:1, :], (PROBES, PROBES)).T
        targets.append(column_ref[pl.ds(start, chunk), :])
    target = jnp.concatenate(targets, axis=0)
    w_hidden = w_hidden_ref[...]
    w_out = w_out_ref[...]
    hidden_pre = matmul(summed, w_hidden, PRECISE) + b_hidden_ref[...]
    activated = jax.nn.silu(hidden_pre)
    density = jnp.sum(activated * w_out, axis=1, keepdims=True)
    error = density - target
    error_grad = error * scale
    pre_grad = w_out * silu_slope(hidden_pre) * error_grad
    spot = lax.broadcasted_iota(jnp.int32, (chunk, PROBES), 0) + start
    mask = (spot == lax.broadcasted_iota(jnp.int32, (chunk, PROBES), 1)).astype(F32)
    up_ref[0 : 2 * chunk, :] = along_last(pre_grad, w_hidden, PRECISE)
    density_row = jnp.sum(mask * density[0:chunk, :], axis=0, keepdims=True)
    up_ref[2 * chunk :, :] = jnp.broadcast_to(density_row, (8, PROBES))
    mine, own_error = pre_grad[0:chunk, :], error[0:chunk, :]
    head_ref[0:CHANS, :] = along_first(summed[0:chunk, :], mine, PRECISE)
    bias = jnp.sum(mine, axis=0, keepdims=True)
    out = jnp.sum(activated[0:chunk, :] * error_grad[0:chunk, :], axis=0, keepdims=True)
    loss = jnp.sum(mask * own_error * own_error * (0.5 * scale), axis=0, keepdims=True)
    head_ref[CHANS : CHANS + 16, :] = jnp.concatenate(
        [bias, out, loss, jnp.zeros((13, CHANS), F32)], axis=0
    )


def backward_kernel(
    feats_ref, species_ref, w_deg_ref, w_gate_ref, split_ref, head_ref, up_ref,
    spread_hbm, sums_hbm, payload_ref, density_ref, spread_ref, sums_ref, sems,
):
    spreads = [pl.ds(low, high - low) for low, high in map(first_rows, range(DEGREES))]
    copies = started(
        [(sums_hbm, sums_ref)]
        + [(spread_hbm.at[part], spread_ref.at[part]) for part in spreads],
        sems,
    )
    shards = up_ref.shape[1]
    chunk = PROBES // shards
    blocks = []
    for delta in DELTAS:
        place, part = plane_place(delta)
        begin = pl.multiple_of(part * chunk, chunk)
        block = jnp.concatenate(
            [up_ref[place, shard, pl.ds(begin, chunk), :] for shard in range(shards)], axis=0
        ).T
        blocks += [block] * SLOTS
    upstream = jnp.concatenate(blocks, axis=1)
    density = None
    for shard in range(shards):
        row = up_ref[lax.axis_index("y"), shard, 2 * chunk : 2 * chunk + 1, :]
        density = row if density is None else density + row
    density_ref[...] = density
    scalar = feats_ref[:, lanes(0)]
    gates = jax.nn.sigmoid(matmul(scalar, w_gate_ref[...]))
    copies[0].wait()
    basis_split = sums_ref[DEGREES * CHANS :, :]
    radial_grads = []
    for degree in range(DEGREES):
        low, high = first_rows(degree)
        radial = along_first(split_ref[:, lanes(degree)], basis_split)
        inner = (radial * upstream).astype(BF16)
        copies[1 + degree].wait()
        grads = along_last(spread_ref[low:high, :], inner)
        product = (sums_ref[lanes(degree), :].astype(F32) * upstream).astype(BF16)
        both = along_last(product, basis_split[0 : 2 * BASES, :])
        radial_grads.append((both[:, 0:BASES] + both[:, BASES : 2 * BASES]).T)
        rows = component_rows(feats_ref, degree)
        mixed = matmul(rows, w_deg_ref[degree])
        if degree == 0:
            mixed_grad = grads * silu_slope(mixed)
            embed_grad = matmul(kind_rows(species_ref), grads, PRECISE)
        else:
            gate = gates[:, lanes(degree - 1)]
            mixed_grad = grads * over_components(gate, degree)
            product = grads * mixed
            total = product[0:ATOMS, :]
            for comp in range(1, 2 * degree + 1):
                total = total + product[comp * ATOMS : (comp + 1) * ATOMS, :]
            pre = (total * gate * (1.0 - gate)).astype(BF16)
            start = (DEGREES + degree - 1) * CHANS
            payload_ref[start : start + CHANS, :] = along_first(scalar, pre).astype(BF16)
        payload_ref[degree * CHANS : (degree + 1) * CHANS, :] = along_first(
            rows, mixed_grad.astype(BF16)
        ).astype(BF16)
    base = (2 * DEGREES - 1) * CHANS
    payload_ref[base : base + CHANS + 16, :] = head_ref[...].astype(BF16)
    base += CHANS + 16
    payload_ref[base : base + 48, :] = jnp.concatenate(
        radial_grads + [embed_grad], axis=0
    ).astype(BF16)
    base += 48
    payload_ref[base:, :] = jnp.zeros((PAYLOAD - base, CHANS), BF16)


def unpack_kernel(
    payload_ref, loss_ref, deg_ref, gate_ref, embed_ref, radial_ref, hidden_ref, bias_ref, out_ref
):
    for degree in range(DEGREES):
        deg_ref[degree] = payload_ref[lanes(degree), :].astype(F32)
    for degree in range(1, DEGREES):
        gate_ref[:, lanes(degree - 1)] = payload_ref[lanes(DEGREES + degree - 1), :].astype(F32)
    base = (2 * DEGREES - 1) * CHANS
    hidden_ref[...] = payload_ref[base : base + CHANS, :].astype(F32)
    base += CHANS
    misc = payload_ref[base : base + 16, :].astype(F32)
    bias_ref[...] = misc[0:1, :]
    out_ref[...] = misc[1:2, :]
    loss_ref[...] = jnp.sum(misc[2:3, :], axis=1, keepdims=True)
    base += 16
    small = payload_ref[base : base + 48, :].astype(F32)
    for degree in range(DEGREES):
        radial_ref[:, lanes(degree)] = small[degree * BASES : (degree + 1) * BASES, :]
    embed_ref[...] = small[DEGREES * BASES :, :]


def shape(dims, dtype=F32):
    return jax.ShapeDtypeStruct(dims, dtype)


def call(kernel, outs, name, limit=48, **options):
    return pl.pallas_call(
        kernel,
        out_shape=outs,
        name=name,
        compiler_params=pltpu.CompilerParams(vmem_limit_bytes=limit * 1024 * 1024),
        **options,
    )


def staging(arrays):
    return [pltpu.VMEM(array.shape, array.dtype) for array in arrays] + [
        pltpu.SemaphoreType.DMA((len(arrays),))
    ]


def call_apart(kernel, outs, name, *operands, outside=False):
    far = pl.BlockSpec(memory_space=pltpu.HBM)
    options = {"out_specs": [far] * len(outs)} if outside else {}
    return call(
        kernel,
        outs,
        name,
        limit=LIMIT,
        in_specs=[far] * len(operands),
        scratch_shapes=staging(operands) + (staging(outs) if outside else []),
        **options,
    )(*operands)


def to_partner(block):
    count = lax.axis_size(SLAB)
    route = [(i, (i + (2 if i % 4 >= 2 else -2)) % count) for i in range(count)]
    return lax.ppermute(block, SLAB, route)


def to_all(block, axes):
    count = lax.axis_size(axes)
    return lax.all_to_all(jnp.broadcast_to(block[None], (count,) + block.shape), axes, 0, 0)


def reduce_all(payload):
    count = lax.axis_size(PLANE)
    depth = lax.axis_size("z")
    rows = PAYLOAD // count
    parts = lax.all_to_all(payload.reshape(count, rows, CHANS), PLANE, 0, 0)
    copies = call(sum_kernel, shape((depth, rows, CHANS), BF16), "sum_plane")(parts)
    parts = lax.all_to_all(copies, "z", 0, 0)
    copies = call(sum_kernel, shape((count, rows, CHANS), BF16), "sum_depth")(parts)
    return lax.all_to_all(copies, PLANE, 0, 0).reshape(PAYLOAD, CHANS)


def on_device(
    atom_feats, species, send_rows, neighbours, harmonics, distances, target,
    w_deg, w_gate, embed, w_radial, w_hidden, b_hidden, w_out,
):
    slab_count = lax.axis_size(SLAB)
    shards = lax.axis_size(ATOM)
    chunk = PROBES // shards
    scale = 1.0 / math.sqrt(PROBES * slab_count)
    species = species.reshape(1, ATOMS)
    pack = call(
        pack_kernel,
        shape((FIELDS, SLOTS, PROBES)),
        "pack",
        limit=LIMIT,
        in_specs=[pl.BlockSpec(memory_space=pltpu.HBM)] * 4,
        scratch_shapes=[
            pltpu.VMEM((SLOTS, PROBES), jnp.int32),
            pltpu.VMEM((1, PROBES), F32),
            pltpu.SemaphoreType.DMA((4,)),
        ],
    )(harmonics, distances, neighbours, target.reshape(1, PROBES))
    with jax.named_scope("exchange_pairs"):
        their_pack = to_partner(pack)
    rows, owners, split = call_apart(
        encode_kernel,
        [
            shape((COMPS * ATOMS, CHANS), BF16),
            shape((len(OFFSETS), ATOMS, ATOMS), BF16),
            shape((6 * BASES, DEGREES * CHANS), BF16),
        ],
        "encode",
        atom_feats, species, w_deg, w_gate, embed, send_rows[0, 0], w_radial,
    )
    with jax.named_scope("gather_pairs"):
        packs = to_all(jnp.stack([pack, their_pack]), "y")
    held = [
        shape((4, shards, 2, chunk, CHANS)),
        shape((COMPS * ATOMS, PAIRS), BF16),
        shape((DEGREES * CHANS + 6 * BASES, PAIRS), BF16),
    ]
    values, spread, sums = call_apart(
        pair_kernel, held, "pair_sums", packs, rows, owners, split, outside=True
    )
    with jax.named_scope("scatter_sums"):
        parts = lax.all_to_all(values.reshape(4 * shards, 2, chunk, CHANS), PLANE, 0, 0)
    mine = call(sum_kernel, shape((2, chunk, CHANS)), "sum_sources")(parts)
    with jax.named_scope("exchange_sums"):
        theirs = to_partner(mine)
    up, head = call(
        functools.partial(readout_kernel, scale),
        [shape((2 * chunk + 8, CHANS)), shape((CHANS + 16, CHANS))],
        "readout",
        scratch_shapes=[pltpu.VMEM((PROBES, PROBES), F32)],
    )(
        mine, theirs, pack, their_pack, w_hidden, b_hidden.reshape(1, CHANS),
        w_out.reshape(1, CHANS),
    )
    with jax.named_scope("gather_grads"):
        ups = to_all(up, PLANE).reshape(4, shards, 2 * chunk + 8, CHANS)
    near, far = pl.BlockSpec(memory_space=pltpu.VMEM), pl.BlockSpec(memory_space=pltpu.HBM)
    payload, density = call(
        backward_kernel,
        [shape((PAYLOAD, CHANS), BF16), shape((1, PROBES))],
        "backward",
        in_specs=[near] * 7 + [far] * 2,
        scratch_shapes=[
            pltpu.VMEM(spread.shape, BF16),
            pltpu.VMEM(sums.shape, BF16),
            pltpu.SemaphoreType.DMA((1 + DEGREES,)),
        ],
    )(atom_feats, species, w_deg, w_gate, split, head, ups, spread, sums)
    with jax.named_scope("reduce_grads"):
        payload = reduce_all(payload)
    loss, deg, gate, embed_grad, radial_grad, hidden, bias, out = call(
        unpack_kernel,
        [
            shape((1, 1)),
            shape((DEGREES, CHANS, CHANS)),
            shape((CHANS, (DEGREES - 1) * CHANS)),
            shape((KINDS, CHANS)),
            shape((BASES, DEGREES * CHANS)),
            shape((CHANS, CHANS)),
            shape((1, CHANS)),
            shape((1, CHANS)),
        ],
        "unpack",
    )(payload)
    return (
        loss.reshape(()), density.reshape(PROBES), deg, gate, embed_grad, radial_grad, hidden,
        bias.reshape(CHANS), out.reshape(CHANS),
    )


def solution(mesh):
    slabs, shards = mesh.devices.shape
    fine = Mesh(mesh.devices.reshape(slabs // 4, 4, shards // 2, 2), ("z", "y", "x", "c"))
    in_specs = (
        P(SLAB + ATOM, None),
        P(SLAB + ATOM),
        P(SLAB, ATOM, None, None),
        P(ATOM, SLAB),
        P(None, ATOM, SLAB),
        P(ATOM, SLAB),
        P(SLAB),
        P(),
        P(),
        P(),
        P(),
        P(),
        P(),
        P(),
    )
    out_specs = (P(), P(SLAB), P(), P(), P(), P(), P(), P(), P())
    return jax.shard_map(
        on_device, mesh=fine, in_specs=in_specs, out_specs=out_specs, check_vma=False
    )
```

```python
import functools
import math

import jax
import jax.numpy as jnp
from jax import lax
from jax.experimental import pallas as pl
from jax.experimental.pallas import tpu as pltpu
from jax.sharding import Mesh, PartitionSpec as P

OFFSETS = (-2, -1, 1, 2)
CUTOFF = 4.0
PRECISE = lax.Precision.HIGHEST
F32 = jnp.float32
BF16 = jnp.bfloat16
SLAB = ("z", "y")
ATOM = ("x", "c")
PLANE = ("y", "x", "c")
DEGREES = 5
COMPS = DEGREES * DEGREES
CHANS = 128
ATOMS = 64
SLOTS = 2
PROBES = 128
DELTAS = (0,) + OFFSETS
SOURCES = len(DELTAS)
SPAN = SLOTS * PROBES
PAIRS = SOURCES * SPAN
FIELDS = 32
BASES = 8
KINDS = 8
PAYLOAD = 1536
LIMIT = 63


def first_rows(degree):
    return degree * degree * ATOMS, (degree + 1) * (degree + 1) * ATOMS


def lanes(block):
    return slice(block * CHANS, (block + 1) * CHANS)


def along_first(left, right, precision=None):
    return lax.dot_general(
        left, right, (((0,), (0,)), ((), ())), preferred_element_type=F32, precision=precision
    )


def along_last(left, right, precision=None):
    return lax.dot_general(
        left, right, (((1,), (1,)), ((), ())), preferred_element_type=F32, precision=precision
    )


def matmul(left, right, precision=None):
    return jnp.dot(left, right, preferred_element_type=F32, precision=precision)


def component_rows(feats_ref, degree):
    parts = [feats_ref[:, lanes(m)] for m in range(degree * degree, (degree + 1) * (degree + 1))]
    return parts[0] if degree == 0 else jnp.concatenate(parts, axis=0)


def over_components(gate, degree):
    return jnp.concatenate([gate] * (2 * degree + 1), axis=0)


def kind_rows(species_ref):
    ids = lax.broadcasted_iota(jnp.int32, (KINDS, ATOMS), 0)
    return (ids == species_ref[...]).astype(F32)


def started(pairs, sems):
    copies = [
        pltpu.make_async_copy(source, target, sems.at[index])
        for index, (source, target) in enumerate(pairs)
    ]
    for copy in copies:
        copy.start()
    return copies


def encode_kernel(
    feats_hbm, species_hbm, w_deg_hbm, w_gate_hbm, embed_hbm, lists_hbm, w_radial_hbm,
    rows_ref, owners_ref, split_ref,
    feats_ref, species_ref, w_deg_ref, w_gate_ref, embed_ref, lists_ref, w_radial_ref, sems,
):
    copies = started(
        (
            (feats_hbm, feats_ref),
            (species_hbm, species_ref),
            (w_deg_hbm, w_deg_ref),
            (w_gate_hbm, w_gate_ref),
            (embed_hbm, embed_ref),
            (lists_hbm, lists_ref),
            (w_radial_hbm, w_radial_ref),
        ),
        sems,
    )
    for copy in copies:
        copy.wait()
    ids = lax.broadcasted_iota(jnp.int32, (ATOMS, ATOMS), 0)
    for which in range(len(OFFSETS)):
        owners_ref[which] = (ids == lists_ref[which : which + 1, :]).astype(BF16)
    split_ref[...] = stacked(w_radial_ref[...], (0, 0, 1, 1, 0, 2))
    scalar = feats_ref[:, lanes(0)]
    gates = jax.nn.sigmoid(matmul(scalar, w_gate_ref[...]))
    for degree in range(DEGREES):
        low, high = first_rows(degree)
        rows = component_rows(feats_ref, degree)
        mixed = matmul(rows, w_deg_ref[degree])
        if degree == 0:
            added = jax.nn.silu(mixed) + along_first(
                kind_rows(species_ref), embed_ref[...], PRECISE
            )
        else:
            added = mixed * over_components(gates[:, lanes(degree - 1)], degree)
        rows_ref[low:high, :] = (rows.astype(F32) + added).astype(BF16)


def parts_of(values):
    high = values.astype(BF16)
    rest = values - high.astype(F32)
    middle = rest.astype(BF16)
    low = (rest - middle.astype(F32)).astype(BF16)
    return high, middle, low


def stacked(values, order):
    parts = [part.astype(F32) for part in parts_of(values)]
    return jnp.concatenate([parts[index] for index in order], axis=0).astype(BF16)


def plane_place(delta):
    row = lax.axis_index("y") + delta
    below, above = row < 0, row > 3
    place = jnp.where(below, row + 2, jnp.where(above, row - 2, row))
    return place, jnp.where(jnp.logical_or(below, above), 1, 0)


def pack_place(delta):
    row = lax.axis_index("y") + delta
    return jnp.where(jnp.logical_or(row < 0, row > 3), 4 if abs(delta) == 2 else 5, row)


def pack_kernel(
    harm_hbm, dist_hbm, nbr_hbm, target_hbm, pack_hbm, copies_hbm,
    pack_ref, nbr_ref, target_ref, sems, out_sems,
):
    copies = started(
        (
            (harm_hbm, pack_ref.at[pl.ds(0, COMPS)]),
            (dist_hbm, pack_ref.at[COMPS]),
            (nbr_hbm, nbr_ref),
            (target_hbm, target_ref),
        ),
        sems,
    )
    for copy in copies:
        copy.wait()
    pack_ref[COMPS + 1] = nbr_ref[...].astype(F32)
    pack_ref[COMPS + 2] = jnp.broadcast_to(target_ref[...], (SLOTS, PROBES))
    pack_ref[COMPS + 3 :] = jnp.zeros((FIELDS - COMPS - 3, SLOTS, PROBES), F32)
    targets = [pack_hbm] + [copies_hbm.at[row] for row in range(copies_hbm.shape[0])]
    for write in started([(pack_ref, target) for target in targets], out_sems):
        write.wait()


def pair_kernel(
    plane_hbm, second_hbm, first_hbm, rows_hbm, owners_hbm, split_hbm,
    out_hbm, spread_hbm, sums_hbm, packs_ref, rows_ref, owners_ref, split_ref, sems,
    out_ref, spread_ref, sums_ref, out_sems,
):
    copies = started(
        (
            (plane_hbm, packs_ref.at[pl.ds(0, 4)]),
            (second_hbm, packs_ref.at[4]),
            (first_hbm, packs_ref.at[5]),
            (owners_hbm, owners_ref),
            (split_hbm, split_ref),
            (rows_hbm, rows_ref),
        ),
        sems,
    )
    shards, chunk = out_ref.shape[1], out_ref.shape[3]
    out_ref[...] = jnp.zeros(out_ref.shape, F32)
    for copy in copies[:3]:
        copy.wait()
    sub = lax.broadcasted_iota(jnp.int32, (ATOMS, PROBES), 0).astype(F32)
    dists = []
    for source in range(SOURCES):
        where = pack_place(DELTAS[source])
        if source == 1:
            copies[3].wait()
        for slot in range(SLOTS):
            start = source * SPAN + slot * PROBES

            def row(field):
                return packs_ref[where, field, slot : slot + 1, :]

            hot = (row(COMPS + 1) - float(source * ATOMS) == sub).astype(F32)
            if source > 0:
                hot = matmul(owners_ref[source - 1], hot.astype(BF16))
            for m in range(COMPS):
                spread_ref[m * ATOMS : (m + 1) * ATOMS, start : start + PROBES] = (
                    hot * row(m)
                ).astype(BF16)
            dists.append(row(COMPS))
    writes = started(((spread_ref, spread_hbm),), out_sems)
    dist = jnp.concatenate(dists, axis=1)
    orders = lax.broadcasted_iota(jnp.int32, (BASES, PAIRS), 0).astype(F32) + 1.0
    phase = math.pi * dist / CUTOFF
    envelope = 0.5 * (jnp.cos(phase) + 1.0) / dist
    basis = jnp.sin(phase * orders) * envelope
    basis_split = stacked(basis, (0, 1, 0, 1, 2, 0))
    sums_ref[DEGREES * CHANS :, :] = basis_split
    copies[4].wait()
    copies[5].wait()
    total = None
    for degree in range(DEGREES):
        low, high = first_rows(degree)
        radial = along_first(split_ref[:, lanes(degree)], basis_split)
        sums = along_first(rows_ref[low:high, :], spread_ref[low:high, :])
        sums_ref[lanes(degree), :] = sums.astype(BF16)
        term = radial * sums
        total = term if total is None else total + term
    for source in range(SOURCES):
        start = source * SPAN
        value = (total[:, start : start + PROBES] + total[:, start + PROBES : start + SPAN]).T
        place, part = plane_place(DELTAS[source])
        for shard in range(shards):
            out_ref[place, shard, part] = value[shard * chunk : (shard + 1) * chunk, :]
    writes += started(
        ((out_ref, out_hbm), (sums_ref, sums_hbm)),
        out_sems.at[pl.ds(1, 2)],
    )
    for write in writes:
        write.wait()


def silu_slope(values):
    logistic = jax.nn.sigmoid(values)
    return logistic * (1.0 + values * (1.0 - logistic))


def sum_kernel(parts_ref, out_ref):
    total = parts_ref[0].astype(F32)
    for index in range(1, parts_ref.shape[0]):
        total = total + parts_ref[index].astype(F32)
    if len(out_ref.shape) == len(parts_ref.shape):
        for copy in range(out_ref.shape[0]):
            out_ref[copy] = total.astype(out_ref.dtype)
    else:
        out_ref[...] = total.astype(out_ref.dtype)


def readout_kernel(
    scale, mine_hbm, theirs_hbm, pack_hbm, their_pack_hbm, w_hidden_hbm, b_hidden_hbm, w_out_hbm,
    up_ref, head_ref, density_ref, column_ref,
    mine_ref, theirs_ref, target_ref, w_hidden_ref, b_hidden_ref, w_out_ref, sems,
):
    copies = started(
        (
            (mine_hbm, mine_ref),
            (theirs_hbm, theirs_ref),
            (pack_hbm.at[COMPS + 2], target_ref.at[0]),
            (their_pack_hbm.at[COMPS + 2], target_ref.at[1]),
            (w_hidden_hbm, w_hidden_ref),
            (b_hidden_hbm, b_hidden_ref),
            (w_out_hbm, w_out_ref),
        ),
        sems,
    )
    for copy in copies:
        copy.wait()
    chunk = mine_ref.shape[1]
    shard = lax.axis_index("x") * lax.axis_size("c") + lax.axis_index("c")
    start = pl.multiple_of(shard * chunk, chunk)
    summed = jnp.concatenate(
        [mine_ref[0] + theirs_ref[1], theirs_ref[0] + mine_ref[1]], axis=0
    )
    targets = []
    for side in range(2):
        column_ref[...] = jnp.broadcast_to(target_ref[side, 0:1, :], (PROBES, PROBES)).T
        targets.append(column_ref[pl.ds(start, chunk), :])
    target = jnp.concatenate(targets, axis=0)
    w_hidden = w_hidden_ref[...]
    w_out = w_out_ref[...]
    hidden_pre = matmul(summed, w_hidden, PRECISE) + b_hidden_ref[...]
    activated = jax.nn.silu(hidden_pre)
    density = jnp.sum(activated * w_out, axis=1, keepdims=True)
    error = density - target
    error_grad = error * scale
    pre_grad = w_out * silu_slope(hidden_pre) * error_grad
    spot = lax.broadcasted_iota(jnp.int32, (chunk, PROBES), 0) + start
    mask = (spot == lax.broadcasted_iota(jnp.int32, (chunk, PROBES), 1)).astype(F32)
    upstream = along_last(pre_grad, w_hidden, PRECISE)
    for copy in range(up_ref.shape[0]):
        up_ref[copy] = upstream
    density_row = jnp.sum(mask * density[0:chunk, :], axis=0, keepdims=True)
    density_ref[...] = density_row
    mine, own_error = pre_grad[0:chunk, :], error[0:chunk, :]
    head_ref[0:CHANS, :] = along_first(summed[0:chunk, :], mine, PRECISE)
    bias = jnp.sum(mine, axis=0, keepdims=True)
    out = jnp.sum(activated[0:chunk, :] * error_grad[0:chunk, :], axis=0, keepdims=True)
    loss = jnp.sum(mask * own_error * own_error * (0.5 * scale), axis=0, keepdims=True)
    head_ref[CHANS : CHANS + 16, :] = jnp.concatenate(
        [bias, out, loss, jnp.zeros((13, CHANS), F32)], axis=0
    )


def own_slab():
    return lax.axis_index("z") * 4 + lax.axis_index("y")


def backward_kernel(
    up_hbm, split_hbm, sums_hbm, feats_hbm, w_deg_hbm, w_gate_hbm, species_hbm, head_hbm,
    density_hbm, spread_hbm, payload_ref,
    up_ref, split_ref, sums_ref, feats_ref, w_deg_ref, w_gate_ref, species_ref, head_ref,
    density_ref, spread_ref, sems,
):
    spreads = [pl.ds(low, high - low) for low, high in map(first_rows, range(DEGREES))]
    copies = started(
        [
            (up_hbm, up_ref),
            (split_hbm, split_ref),
            (sums_hbm, sums_ref),
            (feats_hbm, feats_ref),
            (w_deg_hbm, w_deg_ref),
            (w_gate_hbm, w_gate_ref),
            (species_hbm, species_ref),
            (head_hbm, head_ref),
            (density_hbm, density_ref),
        ]
        + [(spread_hbm.at[part], spread_ref.at[part]) for part in spreads],
        sems,
    )
    copies[0].wait()
    shards = up_ref.shape[1]
    chunk = PROBES // shards
    blocks = []
    for delta in DELTAS:
        place, part = plane_place(delta)
        begin = pl.multiple_of(part * chunk, chunk)
        block = jnp.concatenate(
            [up_ref[place, shard, pl.ds(begin, chunk), :] for shard in range(shards)], axis=0
        ).T
        blocks += [block] * SLOTS
    upstream = jnp.concatenate(blocks, axis=1)
    for copy in copies[1:9]:
        copy.wait()
    scalar = feats_ref[:, lanes(0)]
    gates = jax.nn.sigmoid(matmul(scalar, w_gate_ref[...]))
    basis_split = sums_ref[DEGREES * CHANS :, :]
    radial_grads = []
    for degree in range(DEGREES):
        low, high = first_rows(degree)
        radial = along_first(split_ref[:, lanes(degree)], basis_split)
        inner = (radial * upstream).astype(BF16)
        copies[9 + degree].wait()
        grads = along_last(spread_ref[low:high, :], inner)
        product = (sums_ref[lanes(degree), :].astype(F32) * upstream).astype(BF16)
        both = along_last(product, basis_split[0 : 2 * BASES, :])
        radial_grads.append((both[:, 0:BASES] + both[:, BASES : 2 * BASES]).T)
        rows = component_rows(feats_ref, degree)
        mixed = matmul(rows, w_deg_ref[degree])
        if degree == 0:
            mixed_grad = grads * silu_slope(mixed)
            embed_grad = matmul(kind_rows(species_ref), grads, PRECISE)
        else:
            gate = gates[:, lanes(degree - 1)]
            mixed_grad = grads * over_components(gate, degree)
            product = grads * mixed
            total = product[0:ATOMS, :]
            for comp in range(1, 2 * degree + 1):
                total = total + product[comp * ATOMS : (comp + 1) * ATOMS, :]
            pre = (total * gate * (1.0 - gate)).astype(BF16)
            start = (DEGREES + degree - 1) * CHANS
            payload_ref[start : start + CHANS, :] = along_first(scalar, pre).astype(BF16)
        payload_ref[degree * CHANS : (degree + 1) * CHANS, :] = along_first(
            rows, mixed_grad.astype(BF16)
        ).astype(BF16)
    base = (2 * DEGREES - 1) * CHANS
    payload_ref[base : base + CHANS + 16, :] = head_ref[...].astype(BF16)
    base += CHANS + 16
    payload_ref[base : base + 48, :] = jnp.concatenate(
        radial_grads + [embed_grad], axis=0
    ).astype(BF16)
    base += 48
    slabs = (PAYLOAD - base) // 3
    here = lax.broadcasted_iota(jnp.int32, (slabs, PROBES), 0) == own_slab()
    for part in parts_of(jnp.where(here, density_ref[...], 0.0)):
        payload_ref[base : base + slabs, :] = part
        base += slabs


def unpack_kernel(
    payload_ref, loss_ref, density_ref, deg_ref, gate_ref, embed_ref, radial_ref, hidden_ref,
    bias_ref, out_ref,
):
    for degree in range(DEGREES):
        deg_ref[degree] = payload_ref[lanes(degree), :].astype(F32)
    for degree in range(1, DEGREES):
        gate_ref[:, lanes(degree - 1)] = payload_ref[lanes(DEGREES + degree - 1), :].astype(F32)
    base = (2 * DEGREES - 1) * CHANS
    hidden_ref[...] = payload_ref[base : base + CHANS, :].astype(F32)
    base += CHANS
    misc = payload_ref[base : base + 16, :].astype(F32)
    bias_ref[...] = misc[0:1, :]
    out_ref[...] = misc[1:2, :]
    loss_ref[...] = jnp.sum(misc[2:3, :], axis=1, keepdims=True)
    base += 16
    small = payload_ref[base : base + 48, :].astype(F32)
    for degree in range(DEGREES):
        radial_ref[:, lanes(degree)] = small[degree * BASES : (degree + 1) * BASES, :]
    embed_ref[...] = small[DEGREES * BASES :, :]
    base += 48
    slabs = (PAYLOAD - base) // 3
    total = None
    for _ in range(3):
        part = payload_ref[base : base + slabs, :].astype(F32)
        total = part if total is None else total + part
        base += slabs
    here = lax.broadcasted_iota(jnp.int32, (slabs, PROBES), 0) == own_slab()
    density_ref[...] = jnp.sum(jnp.where(here, total, 0.0), axis=0, keepdims=True)


def shape(dims, dtype=F32):
    return jax.ShapeDtypeStruct(dims, dtype)


def call(kernel, outs, name, limit=48, **options):
    return pl.pallas_call(
        kernel,
        out_shape=outs,
        name=name,
        compiler_params=pltpu.CompilerParams(vmem_limit_bytes=limit * 1024 * 1024),
        **options,
    )


def staging(arrays):
    return [pltpu.VMEM(array.shape, array.dtype) for array in arrays] + [
        pltpu.SemaphoreType.DMA((len(arrays),))
    ]


def call_apart(kernel, outs, name, *operands):
    return call(
        kernel,
        outs,
        name,
        limit=LIMIT,
        in_specs=[pl.BlockSpec(memory_space=pl.ANY)] * len(operands),
        scratch_shapes=staging(operands),
    )(*operands)


def to_partner(block, distance=2):
    count = lax.axis_size(SLAB)
    steps = (-2, -2, 2, 2) if distance == 2 else (-1, 1, -1, 1)
    route = [(i, (i + steps[i % 4]) % count) for i in range(count)]
    return lax.ppermute(block, SLAB, route)


def reduce_all(payload):
    count = lax.axis_size(PLANE)
    depth = lax.axis_size("z")
    rows = PAYLOAD // count
    parts = lax.all_to_all(payload.reshape(count, rows, CHANS), PLANE, 0, 0)
    copies = call(sum_kernel, shape((depth, rows, CHANS), BF16), "sum_plane")(parts)
    parts = lax.all_to_all(copies, "z", 0, 0)
    copies = call(sum_kernel, shape((count, rows, CHANS), BF16), "sum_depth")(parts)
    return lax.all_to_all(copies, PLANE, 0, 0).reshape(PAYLOAD, CHANS)


def on_device(
    atom_feats, species, send_rows, neighbours, harmonics, distances, target,
    w_deg, w_gate, embed, w_radial, w_hidden, b_hidden, w_out,
):
    slab_count = lax.axis_size(SLAB)
    shards = lax.axis_size(ATOM)
    chunk = PROBES // shards
    scale = 1.0 / math.sqrt(PROBES * slab_count)
    species = species.reshape(1, ATOMS)
    far = pl.BlockSpec(memory_space=pl.ANY)
    field_shape = (FIELDS, SLOTS, PROBES)
    pack, copies = call(
        pack_kernel,
        [shape(field_shape), shape((4,) + field_shape)],
        "pack",
        limit=LIMIT,
        in_specs=[far] * 4,
        out_specs=[far] * 2,
        scratch_shapes=[
            pltpu.VMEM(field_shape, F32),
            pltpu.VMEM((SLOTS, PROBES), jnp.int32),
            pltpu.VMEM((1, PROBES), F32),
            pltpu.SemaphoreType.DMA((4,)),
            pltpu.SemaphoreType.DMA((5,)),
        ],
    )(harmonics, distances, neighbours, target.reshape(1, PROBES))
    with jax.named_scope("gather_pairs"):
        packs = lax.all_to_all(copies, "y", 0, 0)
    with jax.named_scope("exchange_pairs"):
        their_pack = to_partner(pack, 2)
        next_pack = to_partner(pack, 1)
    rows, owners, split = call_apart(
        encode_kernel,
        [
            shape((COMPS * ATOMS, CHANS), BF16),
            shape((len(OFFSETS), ATOMS, ATOMS), BF16),
            shape((6 * BASES, DEGREES * CHANS), BF16),
        ],
        "encode",
        atom_feats, species, w_deg, w_gate, embed, send_rows[0, 0], w_radial,
    )
    held = [
        shape((4, shards, 2, chunk, CHANS)),
        shape((COMPS * ATOMS, PAIRS), BF16),
        shape((DEGREES * CHANS + 6 * BASES, PAIRS), BF16),
    ]
    operands = (packs, their_pack, next_pack, rows, owners, split)
    values, spread, sums = call(
        pair_kernel,
        held,
        "pair_sums",
        limit=LIMIT,
        in_specs=[far] * len(operands),
        out_specs=[far] * len(held),
        scratch_shapes=[pltpu.VMEM((6,) + field_shape, F32)]
        + [pltpu.VMEM(operand.shape, operand.dtype) for operand in (rows, owners, split)]
        + [pltpu.SemaphoreType.DMA((len(operands),))]
        + staging(held),
    )(*operands)
    with jax.named_scope("scatter_sums"):
        parts = lax.all_to_all(values.reshape(4 * shards, 2, chunk, CHANS), PLANE, 0, 0)
    mine = call(sum_kernel, shape((2, chunk, CHANS)), "sum_sources")(parts)
    with jax.named_scope("exchange_sums"):
        theirs = to_partner(mine)
    operands = (
        mine, theirs, pack, their_pack, w_hidden, b_hidden.reshape(1, CHANS),
        w_out.reshape(1, CHANS),
    )
    up, head, density_row = call(
        functools.partial(readout_kernel, scale),
        [
            shape((4 * shards, 2 * chunk, CHANS)),
            shape((CHANS + 16, CHANS)),
            shape((1, PROBES)),
        ],
        "readout",
        limit=LIMIT,
        in_specs=[far] * len(operands),
        scratch_shapes=[
            pltpu.VMEM((PROBES, PROBES), F32),
            pltpu.VMEM(mine.shape, F32),
            pltpu.VMEM(theirs.shape, F32),
            pltpu.VMEM((2, SLOTS, PROBES), F32),
            pltpu.VMEM((CHANS, CHANS), F32),
            pltpu.VMEM((1, CHANS), F32),
            pltpu.VMEM((1, CHANS), F32),
            pltpu.SemaphoreType.DMA((len(operands),)),
        ],
    )(*operands)
    with jax.named_scope("gather_grads"):
        ups = lax.all_to_all(up, PLANE, 0, 0).reshape(4, shards, 2 * chunk, CHANS)
    operands = (
        ups, split, sums, atom_feats, w_deg, w_gate, species, head, density_row, spread
    )
    payload = call(
        backward_kernel,
        shape((PAYLOAD, CHANS), BF16),
        "backward",
        limit=LIMIT,
        in_specs=[far] * len(operands),
        scratch_shapes=[pltpu.VMEM(operand.shape, operand.dtype) for operand in operands]
        + [pltpu.SemaphoreType.DMA((len(operands) - 1 + DEGREES,))],
    )(*operands)
    with jax.named_scope("reduce_grads"):
        payload = reduce_all(payload)
    loss, density, deg, gate, embed_grad, radial_grad, hidden, bias, out = call(
        unpack_kernel,
        [
            shape((1, 1)),
            shape((1, PROBES)),
            shape((DEGREES, CHANS, CHANS)),
            shape((CHANS, (DEGREES - 1) * CHANS)),
            shape((KINDS, CHANS)),
            shape((BASES, DEGREES * CHANS)),
            shape((CHANS, CHANS)),
            shape((1, CHANS)),
            shape((1, CHANS)),
        ],
        "unpack",
    )(payload)
    return (
        loss.reshape(()), density.reshape(PROBES), deg, gate, embed_grad, radial_grad, hidden,
        bias.reshape(CHANS), out.reshape(CHANS),
    )


def solution(mesh):
    slabs, shards = mesh.devices.shape
    fine = Mesh(mesh.devices.reshape(slabs // 4, 4, shards // 2, 2), ("z", "y", "x", "c"))
    in_specs = (
        P(SLAB + ATOM, None),
        P(SLAB + ATOM),
        P(SLAB, ATOM, None, None),
        P(ATOM, SLAB),
        P(None, ATOM, SLAB),
        P(ATOM, SLAB),
        P(SLAB),
        P(),
        P(),
        P(),
        P(),
        P(),
        P(),
        P(),
    )
    out_specs = (P(), P(SLAB), P(), P(), P(), P(), P(), P(), P())
    return jax.shard_map(
        on_device, mesh=fine, in_specs=in_specs, out_specs=out_specs, check_vma=False
    )
```

```python
import functools
import math

import jax
import jax.numpy as jnp
from jax import lax
from jax.experimental import pallas as pl
from jax.experimental.pallas import tpu as pltpu
from jax.sharding import Mesh, PartitionSpec as P

OFFSETS = (-2, -1, 1, 2)
CUTOFF = 4.0
PRECISE = lax.Precision.HIGHEST
F32 = jnp.float32
BF16 = jnp.bfloat16
SLAB = ("z", "y")
ATOM = ("x", "c")
PLANE = ("y", "x", "c")
DEGREES = 5
COMPS = DEGREES * DEGREES
CHANS = 128
ATOMS = 64
SLOTS = 2
PROBES = 128
SPAN = SLOTS * PROBES
ROWS = 4
HALO = 2
OWN_PAIRS = ROWS * SPAN
HALO_PAIRS = HALO * SPAN
PAIRS = OWN_PAIRS + HALO_PAIRS
FIELDS = 32
BASES = 8
KINDS = 8
PAYLOAD = 1536
LIMIT = 63


def first_rows(degree):
    return degree * degree * ATOMS, (degree + 1) * (degree + 1) * ATOMS


def lanes(block):
    return slice(block * CHANS, (block + 1) * CHANS)


def along_first(left, right, precision=None):
    return lax.dot_general(
        left, right, (((0,), (0,)), ((), ())), preferred_element_type=F32, precision=precision
    )


def along_last(left, right, precision=None):
    return lax.dot_general(
        left, right, (((1,), (1,)), ((), ())), preferred_element_type=F32, precision=precision
    )


def matmul(left, right, precision=None):
    return jnp.dot(left, right, preferred_element_type=F32, precision=precision)


def component_rows(feats_ref, degree):
    parts = [feats_ref[:, lanes(m)] for m in range(degree * degree, (degree + 1) * (degree + 1))]
    return parts[0] if degree == 0 else jnp.concatenate(parts, axis=0)


def over_components(gate, degree):
    return jnp.concatenate([gate] * (2 * degree + 1), axis=0)


def kind_rows(species):
    ids = lax.broadcasted_iota(jnp.int32, (KINDS, ATOMS), 0).astype(F32)
    return (ids == species).astype(F32)


def owner_tables(lists, owners_ref):
    ids = lax.broadcasted_iota(jnp.int32, (ATOMS, ATOMS), 0).astype(F32)
    same = lax.broadcasted_iota(jnp.int32, (ATOMS, ATOMS), 1).astype(F32)
    for index in range(1 + len(OFFSETS)):
        row = same if index == 2 else lists[index - (index > 2)]
        owners_ref[index] = (ids == row).astype(BF16)


def started(pairs, sems):
    copies = [
        pltpu.make_async_copy(source, target, sems.at[index])
        for index, (source, target) in enumerate(pairs)
    ]
    for copy in copies:
        copy.start()
    return copies


def encode_rows(feats_ref, species, w_deg_ref, w_gate_ref, embed_ref, rows_ref):
    scalar = feats_ref[:, lanes(0)]
    gates = jax.nn.sigmoid(matmul(scalar, w_gate_ref[...]))
    for degree in range(DEGREES):
        low, high = first_rows(degree)
        rows = component_rows(feats_ref, degree)
        mixed = matmul(rows, w_deg_ref[degree])
        if degree == 0:
            added = jax.nn.silu(mixed) + along_first(
                kind_rows(species), embed_ref[...], PRECISE
            )
        else:
            added = mixed * over_components(gates[:, lanes(degree - 1)], degree)
        rows_ref[low:high, :] = (rows.astype(F32) + added).astype(BF16)


def encode_kernel(
    feats_ref, species_ref, w_deg_ref, w_gate_ref, embed_ref, lists_ref, w_radial_ref,
    rows_ref, owners_ref, split_ref, w_deg_out_ref, w_gate_out_ref,
):
    w_deg_out_ref[...] = w_deg_ref[...]
    w_gate_out_ref[...] = w_gate_ref[...]
    lists = [lists_ref[which : which + 1, :].astype(F32) for which in range(len(OFFSETS))]
    owner_tables(lists, owners_ref)
    split_ref[...] = stacked(w_radial_ref[...], (0, 0, 1, 1, 0, 2))
    encode_rows(
        feats_ref, species_ref[...].astype(F32), w_deg_ref, w_gate_ref, embed_ref, rows_ref
    )


def parts_of(values):
    high = values.astype(BF16)
    rest = values - high.astype(F32)
    middle = rest.astype(BF16)
    low = (rest - middle.astype(F32)).astype(BF16)
    return high, middle, low


def stacked(values, order):
    parts = [part.astype(F32) for part in parts_of(values)]
    return jnp.concatenate([parts[index] for index in order], axis=0).astype(BF16)


def pack_kernel(
    harm_hbm, dist_hbm, nbr_hbm, feats_hbm, lists_hbm, species_hbm, copies_hbm, atoms_hbm,
    pack_ref, nbr_ref, lists_ref, species_ref, extra_ref, sems, out_sems,
):
    far = atoms_hbm.at[:, pl.ds(0, COMPS * CHANS)]
    copies = started(
        (
            (harm_hbm, pack_ref.at[pl.ds(0, COMPS)]),
            (dist_hbm, pack_ref.at[COMPS]),
            (nbr_hbm, nbr_ref),
            (lists_hbm, lists_ref),
            (species_hbm, species_ref),
            (feats_hbm, far),
        ),
        sems,
    )
    for copy in copies[:5]:
        copy.wait()
    extra = jnp.concatenate(
        [
            lists_ref[...].astype(F32),
            species_ref[...].astype(F32),
            jnp.zeros((CHANS - 1 - len(OFFSETS), ATOMS), F32),
        ],
        axis=0,
    )
    extra_ref[...] = extra.T.astype(BF16)
    pack_ref[COMPS + 1] = nbr_ref[...].astype(F32)
    pack_ref[COMPS + 2 :] = jnp.zeros((FIELDS - COMPS - 2, SLOTS, PROBES), F32)
    writes = started(
        [(extra_ref, atoms_hbm.at[:, pl.ds(COMPS * CHANS, CHANS)])]
        + [(pack_ref, copies_hbm.at[row]) for row in range(ROWS)],
        out_sems,
    )
    for copy in copies[5:] + writes:
        copy.wait()


def plane_halves():
    row = lax.axis_index("y")
    upper = jnp.where(row > 1, 1, 0)
    partner = row + 4 * upper - 2
    return row, 2 * upper, partner


def pair_kernel(
    packs_ref, theirs_ref, rows_ref, owners_ref, split_ref, w_deg_ref, w_gate_ref, embed_ref,
    out_ref, spread_ref, halo_ref, sums_ref, their_rows_ref, their_owners_ref,
):
    shards, chunk = out_ref.shape[1], out_ref.shape[2]
    own_row, first, partner_row = plane_halves()
    sub = lax.broadcasted_iota(jnp.int32, (ATOMS, PROBES), 0).astype(F32)

    def spread_pairs(target_ref, tables_ref, begin, probe_row, atom_row):
        delta = probe_row - atom_row
        valid = jnp.logical_and(delta >= -2, delta <= 2)
        table = jnp.clip(delta + 2, 0, 4)
        block = jnp.where(delta < 0, delta + 3, jnp.where(delta > 0, delta + 2, 0))
        base = jnp.where(valid, block * ATOMS, 1 << 20).astype(F32)
        for slot in range(SLOTS):
            start = begin + slot * PROBES

            def row(field):
                return packs_ref[probe_row, field, slot : slot + 1, :]

            hot = (row(COMPS + 1) - base == sub).astype(BF16)
            hot = matmul(tables_ref[table], hot)
            for m in range(COMPS):
                target_ref[m * ATOMS : (m + 1) * ATOMS, start : start + PROBES] = (
                    hot * row(m)
                ).astype(BF16)

    for row in range(ROWS):
        spread_pairs(spread_ref, owners_ref, row * SPAN, row, own_row)
    extra = theirs_ref[:, lanes(COMPS)].astype(F32).T
    count = len(OFFSETS)
    owner_tables([extra[which : which + 1, :] for which in range(count)], their_owners_ref)
    encode_rows(
        theirs_ref, extra[count : count + 1, :], w_deg_ref, w_gate_ref, embed_ref, their_rows_ref
    )
    for row in range(HALO):
        spread_pairs(halo_ref, their_owners_ref, row * SPAN, first + row, partner_row)
    dists = [packs_ref[row, COMPS, slot : slot + 1, :] for row in range(ROWS) for slot in range(SLOTS)]
    dists += [
        packs_ref[first + row, COMPS, slot : slot + 1, :]
        for row in range(HALO)
        for slot in range(SLOTS)
    ]
    dist = jnp.concatenate(dists, axis=1)
    orders = lax.broadcasted_iota(jnp.int32, (BASES, PAIRS), 0).astype(F32) + 1.0
    phase = math.pi * dist / CUTOFF
    envelope = 0.5 * (jnp.cos(phase) + 1.0) / dist
    basis_split = stacked(jnp.sin(phase * orders) * envelope, (0, 1, 0, 1, 2, 0))
    sums_ref[DEGREES * CHANS :, :] = basis_split
    total = None
    for degree in range(DEGREES):
        low, high = first_rows(degree)
        radial = along_first(split_ref[:, lanes(degree)], basis_split)
        sums = jnp.concatenate(
            [
                along_first(rows_ref[low:high, :], spread_ref[low:high, :]),
                along_first(their_rows_ref[low:high, :], halo_ref[low:high, :]),
            ],
            axis=1,
        )
        sums_ref[lanes(degree), :] = sums.astype(BF16)
        term = radial * sums
        total = term if total is None else total + term

    def value_of(block):
        start = block * SPAN
        both = total[:, start : start + PROBES] + total[:, start + PROBES : start + SPAN]
        return both.T

    for row in range(ROWS):
        value = value_of(row)
        for shard in range(shards):
            out_ref[row, shard] = value[shard * chunk : (shard + 1) * chunk, :]
    for row in range(HALO):
        value = value_of(ROWS + row)
        for shard in range(shards):
            out_ref[first + row, shard] += value[shard * chunk : (shard + 1) * chunk, :]


def silu_slope(values):
    logistic = jax.nn.sigmoid(values)
    return logistic * (1.0 + values * (1.0 - logistic))


def sum_kernel(parts_ref, out_ref):
    total = parts_ref[0].astype(F32)
    for index in range(1, parts_ref.shape[0]):
        total = total + parts_ref[index].astype(F32)
    if len(out_ref.shape) == len(parts_ref.shape):
        for copy in range(out_ref.shape[0]):
            out_ref[copy] = total.astype(out_ref.dtype)
    else:
        out_ref[...] = total.astype(out_ref.dtype)


def readout_kernel(
    scale, parts_ref, target_ref, w_hidden_ref, b_hidden_ref, w_out_ref,
    up_ref, head_ref, density_ref, column_ref,
):
    chunk = parts_ref.shape[1]
    shard = lax.axis_index("x") * lax.axis_size("c") + lax.axis_index("c")
    start = pl.multiple_of(shard * chunk, chunk)
    column_ref[...] = jnp.broadcast_to(target_ref[...], (PROBES, PROBES)).T
    target = column_ref[pl.ds(start, chunk), :]
    summed = parts_ref[0]
    for index in range(1, parts_ref.shape[0]):
        summed = summed + parts_ref[index]
    w_hidden = w_hidden_ref[...]
    w_out = w_out_ref[...]
    hidden_pre = matmul(summed, w_hidden, PRECISE) + b_hidden_ref[...]
    activated = jax.nn.silu(hidden_pre)
    density = jnp.sum(activated * w_out, axis=1, keepdims=True)
    error = density - target
    error_grad = error * scale
    pre_grad = w_out * silu_slope(hidden_pre) * error_grad
    spot = lax.broadcasted_iota(jnp.int32, (chunk, PROBES), 0) + start
    mask = (spot == lax.broadcasted_iota(jnp.int32, (chunk, PROBES), 1)).astype(F32)
    upstream = along_last(pre_grad, w_hidden, PRECISE)
    for copy in range(up_ref.shape[0]):
        up_ref[copy] = upstream
    density_ref[...] = jnp.sum(mask * density, axis=0, keepdims=True)
    head_ref[0:CHANS, :] = along_first(summed, pre_grad, PRECISE)
    bias = jnp.sum(pre_grad, axis=0, keepdims=True)
    out = jnp.sum(activated * error_grad, axis=0, keepdims=True)
    loss = jnp.sum(mask * error * error * (0.5 * scale), axis=0, keepdims=True)
    head_ref[CHANS : CHANS + 16, :] = jnp.concatenate(
        [bias, out, loss, jnp.zeros((13, CHANS), F32)], axis=0
    )


def own_slab():
    return lax.axis_index("z") * ROWS + lax.axis_index("y")


def backward_kernel(
    feats_ref, theirs_ref, species_ref, w_deg_ref, w_gate_ref, split_ref, head_ref, density_ref,
    up_ref, sums_ref, spread_ref, halo_ref, payload_ref,
):
    shards = up_ref.shape[1]
    first = plane_halves()[1]

    def block_of(row):
        parts = [up_ref[row, shard] for shard in range(shards)]
        return [jnp.concatenate(parts, axis=0).T] * SLOTS

    blocks = []
    for row in list(range(ROWS)) + [first + row for row in range(HALO)]:
        blocks += block_of(row)
    upstream = jnp.concatenate(blocks, axis=1)
    scalar = jnp.concatenate([feats_ref[:, lanes(0)], theirs_ref[:, lanes(0)]], axis=0)
    gates = jax.nn.sigmoid(matmul(scalar, w_gate_ref[...]))
    their_species = theirs_ref[:, lanes(COMPS)].astype(F32).T[len(OFFSETS) : len(OFFSETS) + 1, :]
    kinds = jnp.concatenate(
        [kind_rows(species_ref[...].astype(F32)), kind_rows(their_species)], axis=1
    )
    basis_split = sums_ref[DEGREES * CHANS :, :]
    radial_grads = []
    for degree in range(DEGREES):
        low, high = first_rows(degree)
        size = high - low
        radial = along_first(split_ref[:, lanes(degree)], basis_split)
        inner = (radial * upstream).astype(BF16)
        grads = jnp.concatenate(
            [
                along_last(spread_ref[low:high, :], inner[:, 0:OWN_PAIRS]),
                along_last(halo_ref[low:high, :], inner[:, OWN_PAIRS:]),
            ],
            axis=0,
        )
        product = (sums_ref[lanes(degree), :].astype(F32) * upstream).astype(BF16)
        both = along_last(product, basis_split[0 : 2 * BASES, :])
        radial_grads.append((both[:, 0:BASES] + both[:, BASES : 2 * BASES]).T)
        rows = jnp.concatenate(
            [component_rows(feats_ref, degree), component_rows(theirs_ref, degree)], axis=0
        )
        mixed = matmul(rows, w_deg_ref[degree])
        if degree == 0:
            mixed_grad = grads * silu_slope(mixed)
            embed_grad = matmul(kinds, grads, PRECISE)
        else:
            gate = gates[:, lanes(degree - 1)]
            spread_gate = jnp.concatenate(
                [over_components(gate[0:ATOMS, :], degree), over_components(gate[ATOMS:, :], degree)],
                axis=0,
            )
            mixed_grad = grads * spread_gate
            product = grads * mixed
            totals = []
            for side in range(2):
                total = product[side * size : side * size + ATOMS, :]
                for comp in range(1, 2 * degree + 1):
                    begin = side * size + comp * ATOMS
                    total = total + product[begin : begin + ATOMS, :]
                totals.append(total)
            total = jnp.concatenate(totals, axis=0)
            pre = (total * gate * (1.0 - gate)).astype(BF16)
            start = (DEGREES + degree - 1) * CHANS
            payload_ref[start : start + CHANS, :] = along_first(scalar, pre).astype(BF16)
        payload_ref[degree * CHANS : (degree + 1) * CHANS, :] = along_first(
            rows, mixed_grad.astype(BF16)
        ).astype(BF16)
    base = (2 * DEGREES - 1) * CHANS
    payload_ref[base : base + CHANS + 16, :] = head_ref[...].astype(BF16)
    base += CHANS + 16
    payload_ref[base : base + 48, :] = jnp.concatenate(
        radial_grads + [embed_grad], axis=0
    ).astype(BF16)
    base += 48
    slabs = (PAYLOAD - base) // 3
    here = lax.broadcasted_iota(jnp.int32, (slabs, PROBES), 0) == own_slab()
    for part in parts_of(jnp.where(here, density_ref[...], 0.0)):
        payload_ref[base : base + slabs, :] = part
        base += slabs


def unpack_kernel(
    payload_ref, loss_ref, density_ref, deg_ref, gate_ref, embed_ref, radial_ref, hidden_ref,
    bias_ref, out_ref,
):
    for degree in range(DEGREES):
        deg_ref[degree] = payload_ref[lanes(degree), :].astype(F32)
    for degree in range(1, DEGREES):
        gate_ref[:, lanes(degree - 1)] = payload_ref[lanes(DEGREES + degree - 1), :].astype(F32)
    base = (2 * DEGREES - 1) * CHANS
    hidden_ref[...] = payload_ref[base : base + CHANS, :].astype(F32)
    base += CHANS
    misc = payload_ref[base : base + 16, :].astype(F32)
    bias_ref[...] = misc[0:1, :]
    out_ref[...] = misc[1:2, :]
    loss_ref[...] = jnp.sum(misc[2:3, :], axis=1, keepdims=True)
    base += 16
    small = payload_ref[base : base + 48, :].astype(F32)
    for degree in range(DEGREES):
        radial_ref[:, lanes(degree)] = small[degree * BASES : (degree + 1) * BASES, :]
    embed_ref[...] = small[DEGREES * BASES :, :]
    base += 48
    slabs = (PAYLOAD - base) // 3
    total = None
    for _ in range(3):
        part = payload_ref[base : base + slabs, :].astype(F32)
        total = part if total is None else total + part
        base += slabs
    here = lax.broadcasted_iota(jnp.int32, (slabs, PROBES), 0) == own_slab()
    density_ref[...] = jnp.sum(jnp.where(here, total, 0.0), axis=0, keepdims=True)


def shape(dims, dtype=F32):
    return jax.ShapeDtypeStruct(dims, dtype)


def call(kernel, outs, name, limit=32, **options):
    return pl.pallas_call(
        kernel,
        out_shape=outs,
        name=name,
        compiler_params=pltpu.CompilerParams(vmem_limit_bytes=limit * 1024 * 1024),
        **options,
    )


def to_partner(block):
    count = lax.axis_size(SLAB)
    route = [(i, (i + (2 if i % 4 >= 2 else -2)) % count) for i in range(count)]
    return lax.ppermute(block, SLAB, route)


def reduce_all(payload):
    count = lax.axis_size(PLANE)
    depth = lax.axis_size("z")
    rows = PAYLOAD // count
    parts = lax.all_to_all(payload.reshape(count, rows, CHANS), PLANE, 0, 0)
    copies = call(sum_kernel, shape((depth, rows, CHANS), BF16), "sum_plane")(parts)
    parts = lax.all_to_all(copies, "z", 0, 0)
    copies = call(sum_kernel, shape((count, rows, CHANS), BF16), "sum_depth")(parts)
    return lax.all_to_all(copies, PLANE, 0, 0).reshape(PAYLOAD, CHANS)


def on_device(
    atom_feats, species, send_rows, neighbours, harmonics, distances, target,
    w_deg, w_gate, embed, w_radial, w_hidden, b_hidden, w_out,
):
    slab_count = lax.axis_size(SLAB)
    shards = lax.axis_size(ATOM)
    chunk = PROBES // shards
    scale = 1.0 / math.sqrt(PROBES * slab_count)
    species = species.reshape(1, ATOMS)
    lists = send_rows[0, 0]
    far = pl.BlockSpec(memory_space=pl.ANY)
    field_shape = (FIELDS, SLOTS, PROBES)
    operands = (harmonics, distances, neighbours, atom_feats, lists, species)
    copies, atoms = call(
        pack_kernel,
        [shape((ROWS,) + field_shape), shape((ATOMS, (COMPS + 1) * CHANS), BF16)],
        "pack",
        limit=LIMIT,
        in_specs=[far] * len(operands),
        out_specs=[far] * 2,
        scratch_shapes=[
            pltpu.VMEM(field_shape, F32),
            pltpu.VMEM((SLOTS, PROBES), jnp.int32),
            pltpu.VMEM(lists.shape, jnp.int32),
            pltpu.VMEM(species.shape, jnp.int32),
            pltpu.VMEM((ATOMS, CHANS), BF16),
            pltpu.SemaphoreType.DMA((len(operands),)),
            pltpu.SemaphoreType.DMA((1 + ROWS,)),
        ],
    )(*operands)
    with jax.named_scope("exchange_atoms"):
        theirs = to_partner(atoms)
    with jax.named_scope("gather_pairs"):
        packs = lax.all_to_all(copies, "y", 0, 0)
    rows, owners, split, w_deg_near, w_gate_near = call(
        encode_kernel,
        [
            shape((COMPS * ATOMS, CHANS), BF16),
            shape((1 + len(OFFSETS), ATOMS, ATOMS), BF16),
            shape((6 * BASES, DEGREES * CHANS), BF16),
            shape(w_deg.shape, BF16),
            shape(w_gate.shape, BF16),
        ],
        "encode",
    )(atom_feats, species, w_deg, w_gate, embed, lists, w_radial)
    values, spread, halo, sums = call(
        pair_kernel,
        [
            shape((ROWS, shards, chunk, CHANS)),
            shape((COMPS * ATOMS, OWN_PAIRS), BF16),
            shape((COMPS * ATOMS, HALO_PAIRS), BF16),
            shape((DEGREES * CHANS + 6 * BASES, PAIRS), BF16),
        ],
        "pair_sums",
        scratch_shapes=[pltpu.VMEM(rows.shape, BF16), pltpu.VMEM(owners.shape, BF16)],
    )(packs, theirs, rows, owners, split, w_deg_near, w_gate_near, embed)
    with jax.named_scope("scatter_sums"):
        parts = lax.all_to_all(values.reshape(ROWS * shards, chunk, CHANS), PLANE, 0, 0)
    up, head, density_row = call(
        functools.partial(readout_kernel, scale),
        [
            shape((ROWS * shards, chunk, CHANS)),
            shape((CHANS + 16, CHANS)),
            shape((1, PROBES)),
        ],
        "readout",
        scratch_shapes=[pltpu.VMEM((PROBES, PROBES), F32)],
    )(
        parts, target.reshape(1, PROBES), w_hidden, b_hidden.reshape(1, CHANS),
        w_out.reshape(1, CHANS),
    )
    with jax.named_scope("gather_grads"):
        ups = lax.all_to_all(up, PLANE, 0, 0).reshape(ROWS, shards, chunk, CHANS)
    operands = (
        atom_feats, theirs, species, w_deg_near, w_gate_near, split, head, density_row, ups, sums,
        spread, halo,
    )
    payload = call(backward_kernel, shape((PAYLOAD, CHANS), BF16), "backward")(*operands)
    with jax.named_scope("reduce_grads"):
        payload = reduce_all(payload)
    loss, density, deg, gate, embed_grad, radial_grad, hidden, bias, out = call(
        unpack_kernel,
        [
            shape((1, 1)),
            shape((1, PROBES)),
            shape((DEGREES, CHANS, CHANS)),
            shape((CHANS, (DEGREES - 1) * CHANS)),
            shape((KINDS, CHANS)),
            shape((BASES, DEGREES * CHANS)),
            shape((CHANS, CHANS)),
            shape((1, CHANS)),
            shape((1, CHANS)),
        ],
        "unpack",
    )(payload)
    return (
        loss.reshape(()), density.reshape(PROBES), deg, gate, embed_grad, radial_grad, hidden,
        bias.reshape(CHANS), out.reshape(CHANS),
    )


def solution(mesh):
    slabs, shards = mesh.devices.shape
    fine = Mesh(mesh.devices.reshape(slabs // 4, 4, shards // 2, 2), ("z", "y", "x", "c"))
    in_specs = (
        P(SLAB + ATOM, None),
        P(SLAB + ATOM),
        P(SLAB, ATOM, None, None),
        P(ATOM, SLAB),
        P(None, ATOM, SLAB),
        P(ATOM, SLAB),
        P(SLAB),
        P(),
        P(),
        P(),
        P(),
        P(),
        P(),
        P(),
    )
    out_specs = (P(), P(SLAB), P(), P(), P(), P(), P(), P(), P())
    return jax.shard_map(
        on_device, mesh=fine, in_specs=in_specs, out_specs=out_specs, check_vma=False
    )
```

```python
import functools
import math

import jax
import jax.numpy as jnp
from jax import lax
from jax.experimental import pallas as pl
from jax.experimental.pallas import tpu as pltpu
from jax.sharding import Mesh, PartitionSpec as P

OFFSETS = (-2, -1, 1, 2)
CUTOFF = 4.0
PRECISE = lax.Precision.HIGHEST
F32 = jnp.float32
BF16 = jnp.bfloat16
SLAB = ("z", "y")
ATOM = ("x", "c")
PLANE = ("y", "x", "c")
DEGREES = 5
COMPS = DEGREES * DEGREES
CHANS = 128
ATOMS = 64
SLOTS = 2
PROBES = 128
SPAN = SLOTS * PROBES
ROWS = 4
HALO = 2
OWN_PAIRS = ROWS * SPAN
HALO_PAIRS = HALO * SPAN
PAIRS = OWN_PAIRS + HALO_PAIRS
FIELDS = 32
BASES = 8
KINDS = 8
PAYLOAD = 1536


def first_rows(degree):
    return degree * degree * ATOMS, (degree + 1) * (degree + 1) * ATOMS


def lanes(block):
    return slice(block * CHANS, (block + 1) * CHANS)


def along_first(left, right, precision=None):
    return lax.dot_general(
        left, right, (((0,), (0,)), ((), ())), preferred_element_type=F32, precision=precision
    )


def along_last(left, right, precision=None):
    return lax.dot_general(
        left, right, (((1,), (1,)), ((), ())), preferred_element_type=F32, precision=precision
    )


def matmul(left, right, precision=None):
    return jnp.dot(left, right, preferred_element_type=F32, precision=precision)


def component_rows(feats_ref, degree):
    parts = [feats_ref[:, lanes(m)] for m in range(degree * degree, (degree + 1) * (degree + 1))]
    return parts[0] if degree == 0 else jnp.concatenate(parts, axis=0)


def over_components(gate, degree):
    return jnp.concatenate([gate] * (2 * degree + 1), axis=0)


def kind_rows(species):
    ids = lax.broadcasted_iota(jnp.int32, (KINDS, ATOMS), 0).astype(F32)
    return (ids == species).astype(F32)


def owner_tables(lists, owners_ref):
    ids = lax.broadcasted_iota(jnp.int32, (ATOMS, ATOMS), 0).astype(F32)
    same = lax.broadcasted_iota(jnp.int32, (ATOMS, ATOMS), 1).astype(F32)
    for index in range(1 + len(OFFSETS)):
        row = same if index == 2 else lists[index - (index > 2)]
        owners_ref[index] = (ids == row).astype(BF16)


def started(pairs, sems):
    copies = [
        pltpu.make_async_copy(source, target, sems.at[index])
        for index, (source, target) in enumerate(pairs)
    ]
    for copy in copies:
        copy.start()
    return copies


def encode_rows(feats_ref, species, w_deg_ref, w_gate_ref, embed_ref, rows_ref):
    scalar = feats_ref[:, lanes(0)]
    gates = jax.nn.sigmoid(matmul(scalar, w_gate_ref[...]))
    for degree in range(DEGREES):
        low, high = first_rows(degree)
        rows = component_rows(feats_ref, degree)
        mixed = matmul(rows, w_deg_ref[degree])
        if degree == 0:
            added = jax.nn.silu(mixed) + along_first(
                kind_rows(species), embed_ref[...], PRECISE
            )
        else:
            added = mixed * over_components(gates[:, lanes(degree - 1)], degree)
        rows_ref[low:high, :] = (rows.astype(F32) + added).astype(BF16)


def lists_of(atoms_ref):
    extra = atoms_ref[:, lanes(COMPS)].astype(F32).T
    count = len(OFFSETS)
    return [extra[which : which + 1, :] for which in range(count)], extra[count : count + 1, :]


def encode_kernel(
    atoms_ref, w_deg_ref, w_gate_ref, small_ref,
    rows_ref, owners_ref, split_ref, w_deg_out_ref, w_gate_out_ref, embed_ref,
):
    w_deg_out_ref[...] = w_deg_ref[...]
    w_gate_out_ref[...] = w_gate_ref[...]
    embed_ref[...] = small_ref[BASES:, lanes(0)]
    lists, species = lists_of(atoms_ref)
    owner_tables(lists, owners_ref)
    split_ref[...] = stacked(small_ref[0:BASES, :], (0, 0, 1, 1, 0, 2))
    encode_rows(atoms_ref, species, w_deg_ref, w_gate_ref, embed_ref, rows_ref)


def parts_of(values):
    high = values.astype(BF16)
    rest = values - high.astype(F32)
    middle = rest.astype(BF16)
    low = (rest - middle.astype(F32)).astype(BF16)
    return high, middle, low


def stacked(values, order):
    parts = [part.astype(F32) for part in parts_of(values)]
    return jnp.concatenate([parts[index] for index in order], axis=0).astype(BF16)


def pack_kernel(
    harm_hbm, dist_hbm, nbr_hbm, feats_hbm, lists_hbm, species_hbm, w_radial_hbm, embed_hbm,
    copies_hbm, atoms_hbm, small_hbm,
    pack_ref, atoms_ref, small_ref, nbr_ref, lists_ref, species_ref, sems, out_sems,
):
    small_ref[...] = jnp.zeros(small_ref.shape, F32)
    copies = started(
        (
            (feats_hbm, atoms_ref.at[:, pl.ds(0, COMPS * CHANS)]),
            (harm_hbm, pack_ref.at[pl.ds(0, COMPS)]),
            (dist_hbm, pack_ref.at[COMPS]),
            (nbr_hbm, nbr_ref),
            (lists_hbm, lists_ref),
            (species_hbm, species_ref),
            (w_radial_hbm, small_ref.at[pl.ds(0, BASES)]),
            (embed_hbm, small_ref.at[pl.ds(BASES, KINDS), pl.ds(0, CHANS)]),
        ),
        sems,
    )
    for copy in copies[1:]:
        copy.wait()
    extra = jnp.concatenate(
        [
            lists_ref[...].astype(F32),
            species_ref[...].astype(F32),
            jnp.zeros((CHANS - 1 - len(OFFSETS), ATOMS), F32),
        ],
        axis=0,
    )
    atoms_ref[:, lanes(COMPS)] = extra.T.astype(BF16)
    pack_ref[COMPS + 1] = nbr_ref[...].astype(F32)
    pack_ref[COMPS + 2 :] = jnp.zeros((FIELDS - COMPS - 2, SLOTS, PROBES), F32)
    copies[0].wait()
    writes = started(
        [(atoms_ref, atoms_hbm), (small_ref, small_hbm)]
        + [(pack_ref, copies_hbm.at[row]) for row in range(ROWS)],
        out_sems,
    )
    for write in writes:
        write.wait()


def plane_halves():
    row = lax.axis_index("y")
    upper = jnp.where(row > 1, 1, 0)
    return row, HALO - HALO * upper, row + ROWS - 2 * ROWS * upper


def pair_kernel(
    packs_ref, theirs_ref, rows_ref, owners_ref, split_ref, w_deg_ref, w_gate_ref, embed_ref,
    out_ref, spread_ref, halo_ref, sums_ref, their_rows_ref, their_owners_ref,
):
    shards, chunk = out_ref.shape[1], out_ref.shape[2]
    own_row, first, partner_row = plane_halves()
    sub = lax.broadcasted_iota(jnp.int32, (ATOMS, PROBES), 0).astype(F32)

    def spread_pairs(target_ref, tables_ref, begin, probe_row, atom_row):
        delta = probe_row - atom_row
        valid = jnp.logical_and(delta >= -2, delta <= 2)
        table = jnp.clip(delta + 2, 0, 4)
        block = jnp.where(delta < 0, delta + 3, jnp.where(delta > 0, delta + 2, 0))
        base = jnp.where(valid, block * ATOMS, 1 << 20).astype(F32)
        for slot in range(SLOTS):
            start = begin + slot * PROBES

            def row(field):
                return packs_ref[probe_row, field, slot : slot + 1, :]

            hot = (row(COMPS + 1) - base == sub).astype(BF16)
            hot = matmul(tables_ref[table], hot)
            for m in range(COMPS):
                target_ref[m * ATOMS : (m + 1) * ATOMS, start : start + PROBES] = (
                    hot * row(m)
                ).astype(BF16)

    for row in range(ROWS):
        spread_pairs(spread_ref, owners_ref, row * SPAN, row, own_row)
    their_lists, their_species = lists_of(theirs_ref)
    owner_tables(their_lists, their_owners_ref)
    encode_rows(
        theirs_ref, their_species, w_deg_ref, w_gate_ref, embed_ref, their_rows_ref
    )
    for row in range(HALO):
        spread_pairs(halo_ref, their_owners_ref, row * SPAN, first + row, partner_row)
    dists = [packs_ref[row, COMPS, slot : slot + 1, :] for row in range(ROWS) for slot in range(SLOTS)]
    dists += [
        packs_ref[first + row, COMPS, slot : slot + 1, :]
        for row in range(HALO)
        for slot in range(SLOTS)
    ]
    dist = jnp.concatenate(dists, axis=1)
    orders = lax.broadcasted_iota(jnp.int32, (BASES, PAIRS), 0).astype(F32) + 1.0
    phase = math.pi * dist / CUTOFF
    envelope = 0.5 * (jnp.cos(phase) + 1.0) / dist
    basis_split = stacked(jnp.sin(phase * orders) * envelope, (0, 1, 0, 1, 2, 0))
    sums_ref[DEGREES * CHANS :, :] = basis_split
    total = None
    for degree in range(DEGREES):
        low, high = first_rows(degree)
        radial = along_first(split_ref[:, lanes(degree)], basis_split)
        sums = jnp.concatenate(
            [
                along_first(rows_ref[low:high, :], spread_ref[low:high, :]),
                along_first(their_rows_ref[low:high, :], halo_ref[low:high, :]),
            ],
            axis=1,
        )
        sums_ref[lanes(degree), :] = sums.astype(BF16)
        term = radial * sums
        total = term if total is None else total + term

    def value_of(block):
        start = block * SPAN
        both = total[:, start : start + PROBES] + total[:, start + PROBES : start + SPAN]
        return both.T

    for row in range(ROWS):
        value = value_of(row)
        for shard in range(shards):
            out_ref[row, shard] = value[shard * chunk : (shard + 1) * chunk, :]
    for row in range(HALO):
        value = value_of(ROWS + row)
        for shard in range(shards):
            out_ref[first + row, shard] += value[shard * chunk : (shard + 1) * chunk, :]


def silu_slope(values):
    logistic = jax.nn.sigmoid(values)
    return logistic * (1.0 + values * (1.0 - logistic))


def sum_kernel(parts_ref, out_ref):
    total = parts_ref[0].astype(F32)
    for index in range(1, parts_ref.shape[0]):
        total = total + parts_ref[index].astype(F32)
    if len(out_ref.shape) == len(parts_ref.shape):
        for copy in range(out_ref.shape[0]):
            out_ref[copy] = total.astype(out_ref.dtype)
    else:
        out_ref[...] = total.astype(out_ref.dtype)


def readout_kernel(
    scale, parts_ref, target_ref, w_hidden_ref, b_hidden_ref, w_out_ref,
    up_ref, head_ref, density_ref, column_ref,
):
    chunk = parts_ref.shape[1]
    shard = lax.axis_index("x") * lax.axis_size("c") + lax.axis_index("c")
    start = pl.multiple_of(shard * chunk, chunk)
    column_ref[...] = jnp.broadcast_to(target_ref[...], (PROBES, PROBES)).T
    target = column_ref[pl.ds(start, chunk), :]
    summed = parts_ref[0]
    for index in range(1, parts_ref.shape[0]):
        summed = summed + parts_ref[index]
    w_hidden = w_hidden_ref[...]
    w_out = w_out_ref[...]
    hidden_pre = matmul(summed, w_hidden, PRECISE) + b_hidden_ref[...]
    activated = jax.nn.silu(hidden_pre)
    density = jnp.sum(activated * w_out, axis=1, keepdims=True)
    error = density - target
    error_grad = error * scale
    pre_grad = w_out * silu_slope(hidden_pre) * error_grad
    spot = lax.broadcasted_iota(jnp.int32, (chunk, PROBES), 0) + start
    mask = (spot == lax.broadcasted_iota(jnp.int32, (chunk, PROBES), 1)).astype(F32)
    upstream = along_last(pre_grad, w_hidden, PRECISE)
    for copy in range(up_ref.shape[0]):
        up_ref[copy] = upstream
    density_ref[...] = jnp.sum(mask * density, axis=0, keepdims=True)
    head_ref[0:CHANS, :] = along_first(summed, pre_grad, PRECISE)
    bias = jnp.sum(pre_grad, axis=0, keepdims=True)
    out = jnp.sum(activated * error_grad, axis=0, keepdims=True)
    loss = jnp.sum(mask * error * error * (0.5 * scale), axis=0, keepdims=True)
    head_ref[CHANS : CHANS + 16, :] = jnp.concatenate(
        [bias, out, loss, jnp.zeros((13, CHANS), F32)], axis=0
    )


def own_slab():
    return lax.axis_index("z") * ROWS + lax.axis_index("y")


def backward_kernel(
    atoms_ref, theirs_ref, w_deg_ref, w_gate_ref, split_ref, head_ref, density_ref, up_ref,
    sums_ref, spread_ref, halo_ref, payload_ref,
):
    shards = up_ref.shape[1]
    first = plane_halves()[1]

    def block_of(row):
        parts = [up_ref[row, shard] for shard in range(shards)]
        return [jnp.concatenate(parts, axis=0).T] * SLOTS

    blocks = []
    for row in list(range(ROWS)) + [first + row for row in range(HALO)]:
        blocks += block_of(row)
    upstream = jnp.concatenate(blocks, axis=1)
    scalar = jnp.concatenate([atoms_ref[:, lanes(0)], theirs_ref[:, lanes(0)]], axis=0)
    gates = jax.nn.sigmoid(matmul(scalar, w_gate_ref[...]))
    kinds = jnp.concatenate(
        [kind_rows(lists_of(ref)[1]) for ref in (atoms_ref, theirs_ref)], axis=1
    )
    basis_split = sums_ref[DEGREES * CHANS :, :]
    radial_grads = []
    for degree in range(DEGREES):
        low, high = first_rows(degree)
        size = high - low
        radial = along_first(split_ref[:, lanes(degree)], basis_split)
        inner = (radial * upstream).astype(BF16)
        grads = jnp.concatenate(
            [
                along_last(spread_ref[low:high, :], inner[:, 0:OWN_PAIRS]),
                along_last(halo_ref[low:high, :], inner[:, OWN_PAIRS:]),
            ],
            axis=0,
        )
        product = (sums_ref[lanes(degree), :].astype(F32) * upstream).astype(BF16)
        both = along_last(product, basis_split[0 : 2 * BASES, :])
        radial_grads.append((both[:, 0:BASES] + both[:, BASES : 2 * BASES]).T)
        rows = jnp.concatenate(
            [component_rows(atoms_ref, degree), component_rows(theirs_ref, degree)], axis=0
        )
        mixed = matmul(rows, w_deg_ref[degree])
        if degree == 0:
            mixed_grad = grads * silu_slope(mixed)
            embed_grad = matmul(kinds, grads, PRECISE)
        else:
            gate = gates[:, lanes(degree - 1)]
            spread_gate = jnp.concatenate(
                [over_components(gate[0:ATOMS, :], degree), over_components(gate[ATOMS:, :], degree)],
                axis=0,
            )
            mixed_grad = grads * spread_gate
            product = grads * mixed
            totals = []
            for side in range(2):
                total = product[side * size : side * size + ATOMS, :]
                for comp in range(1, 2 * degree + 1):
                    begin = side * size + comp * ATOMS
                    total = total + product[begin : begin + ATOMS, :]
                totals.append(total)
            total = jnp.concatenate(totals, axis=0)
            pre = (total * gate * (1.0 - gate)).astype(BF16)
            start = (DEGREES + degree - 1) * CHANS
            payload_ref[start : start + CHANS, :] = along_first(scalar, pre).astype(BF16)
        payload_ref[degree * CHANS : (degree + 1) * CHANS, :] = along_first(
            rows, mixed_grad.astype(BF16)
        ).astype(BF16)
    base = (2 * DEGREES - 1) * CHANS
    payload_ref[base : base + CHANS + 16, :] = head_ref[...].astype(BF16)
    base += CHANS + 16
    payload_ref[base : base + 48, :] = jnp.concatenate(
        radial_grads + [embed_grad], axis=0
    ).astype(BF16)
    base += 48
    slabs = (PAYLOAD - base) // 3
    here = lax.broadcasted_iota(jnp.int32, (slabs, PROBES), 0) == own_slab()
    for part in parts_of(jnp.where(here, density_ref[...], 0.0)):
        payload_ref[base : base + slabs, :] = part
        base += slabs


def unpack_kernel(
    payload_ref, loss_ref, density_ref, deg_ref, gate_ref, embed_ref, radial_ref, hidden_ref,
    bias_ref, out_ref,
):
    for degree in range(DEGREES):
        deg_ref[degree] = payload_ref[lanes(degree), :].astype(F32)
    for degree in range(1, DEGREES):
        gate_ref[:, lanes(degree - 1)] = payload_ref[lanes(DEGREES + degree - 1), :].astype(F32)
    base = (2 * DEGREES - 1) * CHANS
    hidden_ref[...] = payload_ref[base : base + CHANS, :].astype(F32)
    base += CHANS
    misc = payload_ref[base : base + 16, :].astype(F32)
    bias_ref[...] = misc[0:1, :]
    out_ref[...] = misc[1:2, :]
    loss_ref[...] = jnp.sum(misc[2:3, :], axis=1, keepdims=True)
    base += 16
    small = payload_ref[base : base + 48, :].astype(F32)
    for degree in range(DEGREES):
        radial_ref[:, lanes(degree)] = small[degree * BASES : (degree + 1) * BASES, :]
    embed_ref[...] = small[DEGREES * BASES :, :]
    base += 48
    slabs = (PAYLOAD - base) // 3
    total = None
    for _ in range(3):
        part = payload_ref[base : base + slabs, :].astype(F32)
        total = part if total is None else total + part
        base += slabs
    here = lax.broadcasted_iota(jnp.int32, (slabs, PROBES), 0) == own_slab()
    density_ref[...] = jnp.sum(jnp.where(here, total, 0.0), axis=0, keepdims=True)


def shape(dims, dtype=F32):
    return jax.ShapeDtypeStruct(dims, dtype)


def call(kernel, outs, name, limit=32, **options):
    return pl.pallas_call(
        kernel,
        out_shape=outs,
        name=name,
        compiler_params=pltpu.CompilerParams(vmem_limit_bytes=limit * 1024 * 1024),
        **options,
    )


def to_partner(block):
    count = lax.axis_size(SLAB)
    route = [(i, (i + (ROWS if i % ROWS >= HALO else -ROWS)) % count) for i in range(count)]
    return lax.ppermute(block, SLAB, route)


def reduce_all(payload):
    count = lax.axis_size(PLANE)
    depth = lax.axis_size("z")
    rows = PAYLOAD // count
    parts = lax.all_to_all(payload.reshape(count, rows, CHANS), PLANE, 0, 0)
    copies = call(sum_kernel, shape((depth, rows, CHANS), BF16), "sum_plane")(parts)
    parts = lax.all_to_all(copies, "z", 0, 0)
    copies = call(sum_kernel, shape((count, rows, CHANS), BF16), "sum_depth")(parts)
    return lax.all_to_all(copies, PLANE, 0, 0).reshape(PAYLOAD, CHANS)


def on_device(
    atom_feats, species, send_rows, neighbours, harmonics, distances, target,
    w_deg, w_gate, embed, w_radial, w_hidden, b_hidden, w_out,
):
    slab_count = lax.axis_size(SLAB)
    shards = lax.axis_size(ATOM)
    chunk = PROBES // shards
    scale = 1.0 / math.sqrt(PROBES * slab_count)
    species = species.reshape(1, ATOMS)
    lists = send_rows[0, 0]
    far = pl.BlockSpec(memory_space=pl.ANY)
    field_shape = (FIELDS, SLOTS, PROBES)
    operands = (
        harmonics, distances, neighbours, atom_feats, lists, species, w_radial, embed
    )
    held = [
        shape((ROWS,) + field_shape),
        shape((ATOMS, (COMPS + 1) * CHANS), BF16),
        shape((BASES + KINDS, DEGREES * CHANS)),
    ]
    copies, atoms, small = call(
        pack_kernel,
        held,
        "pack",
        limit=63,
        in_specs=[far] * len(operands),
        out_specs=[far] * len(held),
        scratch_shapes=[
            pltpu.VMEM(field_shape, F32),
            pltpu.VMEM(held[1].shape, BF16),
            pltpu.VMEM(held[2].shape, F32),
            pltpu.VMEM((SLOTS, PROBES), jnp.int32),
            pltpu.VMEM(lists.shape, jnp.int32),
            pltpu.VMEM(species.shape, jnp.int32),
            pltpu.SemaphoreType.DMA((len(operands),)),
            pltpu.SemaphoreType.DMA((2 + ROWS,)),
        ],
    )(*operands)
    with jax.named_scope("exchange_atoms"):
        theirs = to_partner(atoms)
    with jax.named_scope("gather_pairs"):
        packs = lax.all_to_all(copies, "y", 0, 0)
    rows, owners, split, w_deg_near, w_gate_near, embed_near = call(
        encode_kernel,
        [
            shape((COMPS * ATOMS, CHANS), BF16),
            shape((1 + len(OFFSETS), ATOMS, ATOMS), BF16),
            shape((6 * BASES, DEGREES * CHANS), BF16),
            shape(w_deg.shape, BF16),
            shape(w_gate.shape, BF16),
            shape(embed.shape),
        ],
        "encode",
    )(atoms, w_deg, w_gate, small)
    values, spread, halo, sums = call(
        pair_kernel,
        [
            shape((ROWS, shards, chunk, CHANS)),
            shape((COMPS * ATOMS, OWN_PAIRS), BF16),
            shape((COMPS * ATOMS, HALO_PAIRS), BF16),
            shape((DEGREES * CHANS + 6 * BASES, PAIRS), BF16),
        ],
        "pair_sums",
        scratch_shapes=[pltpu.VMEM(rows.shape, BF16), pltpu.VMEM(owners.shape, BF16)],
    )(packs, theirs, rows, owners, split, w_deg_near, w_gate_near, embed_near)
    with jax.named_scope("scatter_sums"):
        parts = lax.all_to_all(values.reshape(ROWS * shards, chunk, CHANS), PLANE, 0, 0)
    up, head, density_row = call(
        functools.partial(readout_kernel, scale),
        [
            shape((ROWS * shards, chunk, CHANS)),
            shape((CHANS + 16, CHANS)),
            shape((1, PROBES)),
        ],
        "readout",
        scratch_shapes=[pltpu.VMEM((PROBES, PROBES), F32)],
    )(
        parts, target.reshape(1, PROBES), w_hidden, b_hidden.reshape(1, CHANS),
        w_out.reshape(1, CHANS),
    )
    with jax.named_scope("gather_grads"):
        ups = lax.all_to_all(up, PLANE, 0, 0).reshape(ROWS, shards, chunk, CHANS)
    operands = (
        atoms, theirs, w_deg_near, w_gate_near, split, head, density_row, ups, sums,
        spread, halo,
    )
    payload = call(backward_kernel, shape((PAYLOAD, CHANS), BF16), "backward")(*operands)
    with jax.named_scope("reduce_grads"):
        payload = reduce_all(payload)
    loss, density, deg, gate, embed_grad, radial_grad, hidden, bias, out = call(
        unpack_kernel,
        [
            shape((1, 1)),
            shape((1, PROBES)),
            shape((DEGREES, CHANS, CHANS)),
            shape((CHANS, (DEGREES - 1) * CHANS)),
            shape((KINDS, CHANS)),
            shape((BASES, DEGREES * CHANS)),
            shape((CHANS, CHANS)),
            shape((1, CHANS)),
            shape((1, CHANS)),
        ],
        "unpack",
    )(payload)
    return (
        loss.reshape(()), density.reshape(PROBES), deg, gate, embed_grad, radial_grad, hidden,
        bias.reshape(CHANS), out.reshape(CHANS),
    )


def solution(mesh):
    slabs, shards = mesh.devices.shape
    fine = Mesh(mesh.devices.reshape(slabs // 4, 4, shards // 2, 2), ("z", "y", "x", "c"))
    in_specs = (
        P(SLAB + ATOM, None),
        P(SLAB + ATOM),
        P(SLAB, ATOM, None, None),
        P(ATOM, SLAB),
        P(None, ATOM, SLAB),
        P(ATOM, SLAB),
        P(SLAB),
        P(),
        P(),
        P(),
        P(),
        P(),
        P(),
        P(),
    )
    out_specs = (P(), P(SLAB), P(), P(), P(), P(), P(), P(), P())
    return jax.shard_map(
        on_device, mesh=fine, in_specs=in_specs, out_specs=out_specs, check_vma=False
    )
```

```python
import functools
import math

import jax
import jax.numpy as jnp
from jax import lax
from jax.experimental import pallas as pl
from jax.experimental.pallas import tpu as pltpu
from jax.sharding import Mesh, PartitionSpec as P

OFFSETS = (-2, -1, 1, 2)
CUTOFF = 4.0
PRECISE = lax.Precision.HIGHEST
F32 = jnp.float32
BF16 = jnp.bfloat16
SLAB = ("zh", "zl", "y")
ATOM = ("x", "c")
PLANE = ("y", "x", "c")
NEAR = ("zl", "y", "x", "c")
DEGREES = 5
COMPS = DEGREES * DEGREES
CHANS = 128
ATOMS = 64
SLOTS = 2
PROBES = 128
SPAN = SLOTS * PROBES
ROWS = 4
HALO = 2
OWN_PAIRS = ROWS * SPAN
HALO_PAIRS = HALO * SPAN
PAIRS = OWN_PAIRS + HALO_PAIRS
FIELDS = 32
BASES = 8
KINDS = 8
PAYLOAD = 1536


def first_rows(degree):
    return degree * degree * ATOMS, (degree + 1) * (degree + 1) * ATOMS


def lanes(block):
    return slice(block * CHANS, (block + 1) * CHANS)


def along_first(left, right, precision=None):
    return lax.dot_general(
        left, right, (((0,), (0,)), ((), ())), preferred_element_type=F32, precision=precision
    )


def along_last(left, right, precision=None):
    return lax.dot_general(
        left, right, (((1,), (1,)), ((), ())), preferred_element_type=F32, precision=precision
    )


def matmul(left, right, precision=None):
    return jnp.dot(left, right, preferred_element_type=F32, precision=precision)


def component_rows(feats_ref, degree):
    parts = [feats_ref[:, lanes(m)] for m in range(degree * degree, (degree + 1) * (degree + 1))]
    return parts[0] if degree == 0 else jnp.concatenate(parts, axis=0)


def over_components(gate, degree):
    return jnp.concatenate([gate] * (2 * degree + 1), axis=0)


def kind_rows(species):
    ids = lax.broadcasted_iota(jnp.int32, (KINDS, ATOMS), 0).astype(F32)
    return (ids == species).astype(F32)


def owner_tables(lists, owners_ref):
    ids = lax.broadcasted_iota(jnp.int32, (ATOMS, ATOMS), 0).astype(F32)
    same = lax.broadcasted_iota(jnp.int32, (ATOMS, ATOMS), 1).astype(F32)
    for index in range(1 + len(OFFSETS)):
        row = same if index == 2 else lists[index - (index > 2)]
        owners_ref[index] = (ids == row).astype(BF16)


def started(pairs, sems):
    copies = [
        pltpu.make_async_copy(source, target, sems.at[index])
        for index, (source, target) in enumerate(pairs)
    ]
    for copy in copies:
        copy.start()
    return copies


def encode_rows(
    feats_ref, species, w_deg_ref, w_gate_ref, embed_ref, rows_ref, mixed_ref, gates_ref
):
    scalar = feats_ref[:, lanes(0)]
    gates = jax.nn.sigmoid(matmul(scalar, w_gate_ref[...]))
    gates_ref[...] = gates
    for degree in range(DEGREES):
        low, high = first_rows(degree)
        rows = component_rows(feats_ref, degree)
        mixed = matmul(rows, w_deg_ref[degree])
        mixed_ref[low:high, :] = mixed
        if degree == 0:
            added = jax.nn.silu(mixed) + along_first(
                kind_rows(species), embed_ref[...], PRECISE
            )
        else:
            added = mixed * over_components(gates[:, lanes(degree - 1)], degree)
        rows_ref[low:high, :] = (rows.astype(F32) + added).astype(BF16)


def lists_of(atoms_ref):
    extra = atoms_ref[:, lanes(COMPS)].astype(F32).T
    count = len(OFFSETS)
    return [extra[which : which + 1, :] for which in range(count)], extra[count : count + 1, :]


def encode_kernel(
    atoms_ref, w_deg_ref, w_gate_ref, small_ref,
    rows_ref, owners_ref, split_ref, w_deg_out_ref, w_gate_out_ref, embed_ref, mixed_ref,
    gates_ref,
):
    w_deg_out_ref[...] = w_deg_ref[...]
    w_gate_out_ref[...] = w_gate_ref[...]
    embed_ref[...] = small_ref[BASES:, lanes(0)]
    lists, species = lists_of(atoms_ref)
    owner_tables(lists, owners_ref)
    split_ref[...] = stacked(small_ref[0:BASES, :], (0, 0, 1, 1, 0, 2))
    encode_rows(
        atoms_ref, species, w_deg_ref, w_gate_ref, embed_ref, rows_ref, mixed_ref, gates_ref
    )


def parts_of(values):
    high = values.astype(BF16)
    rest = values - high.astype(F32)
    middle = rest.astype(BF16)
    low = (rest - middle.astype(F32)).astype(BF16)
    return high, middle, low


def stacked(values, order):
    parts = [part.astype(F32) for part in parts_of(values)]
    return jnp.concatenate([parts[index] for index in order], axis=0).astype(BF16)


def pack_kernel(
    harm_hbm, dist_hbm, nbr_hbm, feats_hbm, lists_hbm, species_hbm, w_radial_hbm, embed_hbm,
    copies_hbm, atoms_hbm, small_hbm,
    pack_ref, atoms_ref, small_ref, nbr_ref, lists_ref, species_ref, sems, out_sems,
):
    small_ref[...] = jnp.zeros(small_ref.shape, F32)
    copies = started(
        (
            (feats_hbm, atoms_ref.at[:, pl.ds(0, COMPS * CHANS)]),
            (harm_hbm, pack_ref.at[pl.ds(0, COMPS)]),
            (dist_hbm, pack_ref.at[COMPS]),
            (nbr_hbm, nbr_ref),
            (lists_hbm, lists_ref),
            (species_hbm, species_ref),
            (w_radial_hbm, small_ref.at[pl.ds(0, BASES)]),
            (embed_hbm, small_ref.at[pl.ds(BASES, KINDS), pl.ds(0, CHANS)]),
        ),
        sems,
    )
    for copy in copies[1:]:
        copy.wait()
    extra = jnp.concatenate(
        [
            lists_ref[...].astype(F32),
            species_ref[...].astype(F32),
            jnp.zeros((CHANS - 1 - len(OFFSETS), ATOMS), F32),
        ],
        axis=0,
    )
    atoms_ref[:, lanes(COMPS)] = extra.T.astype(BF16)
    pack_ref[COMPS + 1] = nbr_ref[...].astype(F32)
    pack_ref[COMPS + 2 :] = jnp.zeros((FIELDS - COMPS - 2, SLOTS, PROBES), F32)
    copies[0].wait()
    writes = started(
        [(atoms_ref, atoms_hbm), (small_ref, small_hbm)]
        + [(pack_ref, copies_hbm.at[row]) for row in range(ROWS)],
        out_sems,
    )
    for write in writes:
        write.wait()


def plane_halves():
    row = lax.axis_index("y")
    upper = jnp.where(row > 1, 1, 0)
    return row, HALO - HALO * upper, row + ROWS - 2 * ROWS * upper


def pair_kernel(
    packs_ref, theirs_ref, rows_ref, owners_ref, split_ref, w_deg_ref, w_gate_ref, embed_ref,
    out_ref, spread_ref, halo_ref, sums_ref, radial_ref, their_mixed_ref, their_gates_ref,
    their_rows_ref, their_owners_ref,
):
    shards, chunk = out_ref.shape[1], out_ref.shape[2]
    own_row, first, partner_row = plane_halves()
    sub = lax.broadcasted_iota(jnp.int32, (ATOMS, PROBES), 0).astype(F32)

    def spread_pairs(target_ref, tables_ref, begin, probe_row, atom_row):
        delta = probe_row - atom_row
        valid = jnp.logical_and(delta >= -2, delta <= 2)
        table = jnp.clip(delta + 2, 0, 4)
        block = jnp.where(delta < 0, delta + 3, jnp.where(delta > 0, delta + 2, 0))
        base = jnp.where(valid, block * ATOMS, 1 << 20).astype(F32)
        for slot in range(SLOTS):
            start = begin + slot * PROBES

            def row(field):
                return packs_ref[probe_row, field, slot : slot + 1, :]

            hot = (row(COMPS + 1) - base == sub).astype(BF16)
            hot = matmul(tables_ref[table], hot)
            for m in range(COMPS):
                target_ref[m * ATOMS : (m + 1) * ATOMS, start : start + PROBES] = (
                    hot * row(m)
                ).astype(BF16)

    for row in range(ROWS):
        spread_pairs(spread_ref, owners_ref, row * SPAN, row, own_row)
    their_lists, their_species = lists_of(theirs_ref)
    owner_tables(their_lists, their_owners_ref)
    encode_rows(
        theirs_ref, their_species, w_deg_ref, w_gate_ref, embed_ref, their_rows_ref,
        their_mixed_ref, their_gates_ref,
    )
    for row in range(HALO):
        spread_pairs(halo_ref, their_owners_ref, row * SPAN, first + row, partner_row)
    dists = [packs_ref[row, COMPS, slot : slot + 1, :] for row in range(ROWS) for slot in range(SLOTS)]
    dists += [
        packs_ref[first + row, COMPS, slot : slot + 1, :]
        for row in range(HALO)
        for slot in range(SLOTS)
    ]
    dist = jnp.concatenate(dists, axis=1)
    orders = lax.broadcasted_iota(jnp.int32, (BASES, PAIRS), 0).astype(F32) + 1.0
    phase = math.pi * dist / CUTOFF
    envelope = 0.5 * (jnp.cos(phase) + 1.0) / dist
    basis_split = stacked(jnp.sin(phase * orders) * envelope, (0, 1, 0, 1, 2, 0))
    sums_ref[DEGREES * CHANS :, :] = basis_split[0 : 2 * BASES, :]
    total = None
    for degree in range(DEGREES):
        low, high = first_rows(degree)
        radial = along_first(split_ref[:, lanes(degree)], basis_split)
        radial_ref[lanes(degree), :] = radial
        sums = jnp.concatenate(
            [
                along_first(rows_ref[low:high, :], spread_ref[low:high, :]),
                along_first(their_rows_ref[low:high, :], halo_ref[low:high, :]),
            ],
            axis=1,
        )
        sums_ref[lanes(degree), :] = sums.astype(BF16)
        term = radial * sums
        total = term if total is None else total + term

    def value_of(block):
        start = block * SPAN
        both = total[:, start : start + PROBES] + total[:, start + PROBES : start + SPAN]
        return both.T

    for row in range(ROWS):
        value = value_of(row)
        for shard in range(shards):
            out_ref[row, shard] = value[shard * chunk : (shard + 1) * chunk, :]
    for row in range(HALO):
        value = value_of(ROWS + row)
        for shard in range(shards):
            out_ref[first + row, shard] += value[shard * chunk : (shard + 1) * chunk, :]


def silu_slope(values):
    logistic = jax.nn.sigmoid(values)
    return logistic * (1.0 + values * (1.0 - logistic))


def sum_kernel(parts_ref, out_ref):
    total = parts_ref[0].astype(F32)
    for index in range(1, parts_ref.shape[0]):
        total = total + parts_ref[index].astype(F32)
    if len(out_ref.shape) == len(parts_ref.shape):
        for copy in range(out_ref.shape[0]):
            out_ref[copy] = total.astype(out_ref.dtype)
    else:
        out_ref[...] = total.astype(out_ref.dtype)


def readout_kernel(
    scale, parts_ref, target_ref, w_hidden_ref, b_hidden_ref, w_out_ref,
    up_ref, head_ref, density_ref, column_ref,
):
    chunk = parts_ref.shape[1]
    shard = lax.axis_index("x") * lax.axis_size("c") + lax.axis_index("c")
    start = pl.multiple_of(shard * chunk, chunk)
    column_ref[...] = jnp.broadcast_to(target_ref[...], (PROBES, PROBES)).T
    target = column_ref[pl.ds(start, chunk), :]
    summed = parts_ref[0]
    for index in range(1, parts_ref.shape[0]):
        summed = summed + parts_ref[index]
    w_hidden = w_hidden_ref[...]
    w_out = w_out_ref[...]
    hidden_pre = matmul(summed, w_hidden, PRECISE) + b_hidden_ref[...]
    activated = jax.nn.silu(hidden_pre)
    density = jnp.sum(activated * w_out, axis=1, keepdims=True)
    error = density - target
    error_grad = error * scale
    pre_grad = w_out * silu_slope(hidden_pre) * error_grad
    spot = lax.broadcasted_iota(jnp.int32, (chunk, PROBES), 0) + start
    mask = (spot == lax.broadcasted_iota(jnp.int32, (chunk, PROBES), 1)).astype(F32)
    upstream = along_last(pre_grad, w_hidden, PRECISE)
    for copy in range(up_ref.shape[0]):
        up_ref[copy] = upstream
    density_ref[...] = jnp.sum(mask * density, axis=0, keepdims=True)
    head_ref[0:CHANS, :] = along_first(summed, pre_grad, PRECISE)
    bias = jnp.sum(pre_grad, axis=0, keepdims=True)
    out = jnp.sum(activated * error_grad, axis=0, keepdims=True)
    loss = jnp.sum(mask * error * error * (0.5 * scale), axis=0, keepdims=True)
    head_ref[CHANS : CHANS + 16, :] = jnp.concatenate(
        [bias, out, loss, jnp.zeros((13, CHANS), F32)], axis=0
    )


def own_slab():
    depth = lax.axis_index("zh") * lax.axis_size("zl") + lax.axis_index("zl")
    return depth * ROWS + lax.axis_index("y")


def backward_kernel(
    atoms_ref, theirs_ref, mixed_ref, their_mixed_ref, gates_ref, their_gates_ref, radial_ref,
    head_ref, density_ref, up_ref, sums_ref, spread_ref, halo_ref, payload_ref,
):
    shards = up_ref.shape[1]
    first = plane_halves()[1]

    def block_of(row):
        parts = [up_ref[row, shard] for shard in range(shards)]
        return [jnp.concatenate(parts, axis=0).T] * SLOTS

    blocks = []
    for row in list(range(ROWS)) + [first + row for row in range(HALO)]:
        blocks += block_of(row)
    upstream = jnp.concatenate(blocks, axis=1)
    scalar = jnp.concatenate([atoms_ref[:, lanes(0)], theirs_ref[:, lanes(0)]], axis=0)
    gates = jnp.concatenate([gates_ref[...], their_gates_ref[...]], axis=0)
    kinds = jnp.concatenate(
        [kind_rows(lists_of(ref)[1]) for ref in (atoms_ref, theirs_ref)], axis=1
    )
    basis_split = sums_ref[DEGREES * CHANS :, :]
    radial_grads = []
    for degree in range(DEGREES):
        low, high = first_rows(degree)
        size = high - low
        inner = (radial_ref[lanes(degree), :] * upstream).astype(BF16)
        grads = jnp.concatenate(
            [
                along_last(spread_ref[low:high, :], inner[:, 0:OWN_PAIRS]),
                along_last(halo_ref[low:high, :], inner[:, OWN_PAIRS:]),
            ],
            axis=0,
        )
        product = (sums_ref[lanes(degree), :].astype(F32) * upstream).astype(BF16)
        both = along_last(product, basis_split)
        radial_grads.append((both[:, 0:BASES] + both[:, BASES : 2 * BASES]).T)
        rows = jnp.concatenate(
            [component_rows(atoms_ref, degree), component_rows(theirs_ref, degree)], axis=0
        )
        mixed = jnp.concatenate([mixed_ref[low:high, :], their_mixed_ref[low:high, :]], axis=0)
        if degree == 0:
            mixed_grad = grads * silu_slope(mixed)
            embed_grad = matmul(kinds, grads, PRECISE)
        else:
            gate = gates[:, lanes(degree - 1)]
            spread_gate = jnp.concatenate(
                [over_components(gate[0:ATOMS, :], degree), over_components(gate[ATOMS:, :], degree)],
                axis=0,
            )
            mixed_grad = grads * spread_gate
            product = grads * mixed
            totals = []
            for side in range(2):
                total = product[side * size : side * size + ATOMS, :]
                for comp in range(1, 2 * degree + 1):
                    begin = side * size + comp * ATOMS
                    total = total + product[begin : begin + ATOMS, :]
                totals.append(total)
            total = jnp.concatenate(totals, axis=0)
            pre = (total * gate * (1.0 - gate)).astype(BF16)
            start = (DEGREES + degree - 1) * CHANS
            payload_ref[start : start + CHANS, :] = along_first(scalar, pre).astype(BF16)
        payload_ref[degree * CHANS : (degree + 1) * CHANS, :] = along_first(
            rows, mixed_grad.astype(BF16)
        ).astype(BF16)
    base = (2 * DEGREES - 1) * CHANS
    payload_ref[base : base + CHANS + 16, :] = head_ref[...].astype(BF16)
    base += CHANS + 16
    payload_ref[base : base + 48, :] = jnp.concatenate(
        radial_grads + [embed_grad], axis=0
    ).astype(BF16)
    base += 48
    slabs = (PAYLOAD - base) // 3
    here = lax.broadcasted_iota(jnp.int32, (slabs, PROBES), 0) == own_slab()
    for part in parts_of(jnp.where(here, density_ref[...], 0.0)):
        payload_ref[base : base + slabs, :] = part
        base += slabs


def unpack_kernel(
    payload_ref, loss_ref, density_ref, deg_ref, gate_ref, embed_ref, radial_ref, hidden_ref,
    bias_ref, out_ref,
):
    for degree in range(DEGREES):
        deg_ref[degree] = payload_ref[lanes(degree), :].astype(F32)
    for degree in range(1, DEGREES):
        gate_ref[:, lanes(degree - 1)] = payload_ref[lanes(DEGREES + degree - 1), :].astype(F32)
    base = (2 * DEGREES - 1) * CHANS
    hidden_ref[...] = payload_ref[base : base + CHANS, :].astype(F32)
    base += CHANS
    misc = payload_ref[base : base + 16, :].astype(F32)
    bias_ref[...] = misc[0:1, :]
    out_ref[...] = misc[1:2, :]
    loss_ref[...] = jnp.sum(misc[2:3, :], axis=1, keepdims=True)
    base += 16
    small = payload_ref[base : base + 48, :].astype(F32)
    for degree in range(DEGREES):
        radial_ref[:, lanes(degree)] = small[degree * BASES : (degree + 1) * BASES, :]
    embed_ref[...] = small[DEGREES * BASES :, :]
    base += 48
    slabs = (PAYLOAD - base) // 3
    total = None
    for _ in range(3):
        part = payload_ref[base : base + slabs, :].astype(F32)
        total = part if total is None else total + part
        base += slabs
    here = lax.broadcasted_iota(jnp.int32, (slabs, PROBES), 0) == own_slab()
    density_ref[...] = jnp.sum(jnp.where(here, total, 0.0), axis=0, keepdims=True)


def shape(dims, dtype=F32):
    return jax.ShapeDtypeStruct(dims, dtype)


def call(kernel, outs, name, limit=32, **options):
    return pl.pallas_call(
        kernel,
        out_shape=outs,
        name=name,
        compiler_params=pltpu.CompilerParams(vmem_limit_bytes=limit * 1024 * 1024),
        **options,
    )


def to_partner(block):
    count = lax.axis_size(SLAB)
    route = [(i, (i + (ROWS if i % ROWS >= HALO else -ROWS)) % count) for i in range(count)]
    return lax.ppermute(block, SLAB, route)


def reduce_all(payload):
    count, depth = lax.axis_size(NEAR), lax.axis_size("zh")
    rows = PAYLOAD // count
    parts = lax.all_to_all(payload.reshape(count, rows, CHANS), NEAR, 0, 0)
    copies = call(sum_kernel, shape((depth, rows, CHANS), BF16), "sum_near")(parts)
    parts = lax.all_to_all(copies, "zh", 0, 0)
    copies = call(sum_kernel, shape((count, rows, CHANS), BF16), "sum_depth")(parts)
    return lax.all_to_all(copies, NEAR, 0, 0).reshape(PAYLOAD, CHANS)


def on_device(
    atom_feats, species, send_rows, neighbours, harmonics, distances, target,
    w_deg, w_gate, embed, w_radial, w_hidden, b_hidden, w_out,
):
    slab_count = lax.axis_size(SLAB)
    shards = lax.axis_size(ATOM)
    chunk = PROBES // shards
    scale = 1.0 / math.sqrt(PROBES * slab_count)
    species = species.reshape(1, ATOMS)
    lists = send_rows[0, 0]
    far = pl.BlockSpec(memory_space=pl.ANY)
    field_shape = (FIELDS, SLOTS, PROBES)
    operands = (
        harmonics, distances, neighbours, atom_feats, lists, species, w_radial, embed
    )
    held = [
        shape((ROWS,) + field_shape),
        shape((ATOMS, (COMPS + 1) * CHANS), BF16),
        shape((BASES + KINDS, DEGREES * CHANS)),
    ]
    copies, atoms, small = call(
        pack_kernel,
        held,
        "pack",
        limit=63,
        in_specs=[far] * len(operands),
        out_specs=[far] * len(held),
        scratch_shapes=[
            pltpu.VMEM(field_shape, F32),
            pltpu.VMEM(held[1].shape, BF16),
            pltpu.VMEM(held[2].shape, F32),
            pltpu.VMEM((SLOTS, PROBES), jnp.int32),
            pltpu.VMEM(lists.shape, jnp.int32),
            pltpu.VMEM(species.shape, jnp.int32),
            pltpu.SemaphoreType.DMA((len(operands),)),
            pltpu.SemaphoreType.DMA((2 + ROWS,)),
        ],
    )(*operands)
    with jax.named_scope("exchange_atoms"):
        theirs = to_partner(atoms)
    with jax.named_scope("gather_pairs"):
        packs = lax.all_to_all(copies, "y", 0, 0)
    mixed_shapes = [shape((COMPS * ATOMS, CHANS)), shape((ATOMS, (DEGREES - 1) * CHANS))]
    rows, owners, split, w_deg_near, w_gate_near, embed_near, mixed, gates = call(
        encode_kernel,
        [
            shape((COMPS * ATOMS, CHANS), BF16),
            shape((1 + len(OFFSETS), ATOMS, ATOMS), BF16),
            shape((6 * BASES, DEGREES * CHANS), BF16),
            shape(w_deg.shape, BF16),
            shape(w_gate.shape, BF16),
            shape(embed.shape),
        ]
        + mixed_shapes,
        "encode",
    )(atoms, w_deg, w_gate, small)
    values, spread, halo, sums, radial, their_mixed, their_gates = call(
        pair_kernel,
        [
            shape((ROWS, shards, chunk, CHANS)),
            shape((COMPS * ATOMS, OWN_PAIRS), BF16),
            shape((COMPS * ATOMS, HALO_PAIRS), BF16),
            shape((DEGREES * CHANS + 2 * BASES, PAIRS), BF16),
            shape((DEGREES * CHANS, PAIRS)),
        ]
        + mixed_shapes,
        "pair_sums",
        scratch_shapes=[pltpu.VMEM(rows.shape, BF16), pltpu.VMEM(owners.shape, BF16)],
    )(packs, theirs, rows, owners, split, w_deg_near, w_gate_near, embed_near)
    with jax.named_scope("scatter_sums"):
        parts = lax.all_to_all(values.reshape(ROWS * shards, chunk, CHANS), PLANE, 0, 0)
    up, head, density_row = call(
        functools.partial(readout_kernel, scale),
        [
            shape((ROWS * shards, chunk, CHANS)),
            shape((CHANS + 16, CHANS)),
            shape((1, PROBES)),
        ],
        "readout",
        scratch_shapes=[pltpu.VMEM((PROBES, PROBES), F32)],
    )(
        parts, target.reshape(1, PROBES), w_hidden, b_hidden.reshape(1, CHANS),
        w_out.reshape(1, CHANS),
    )
    with jax.named_scope("gather_grads"):
        ups = lax.all_to_all(up, PLANE, 0, 0).reshape(ROWS, shards, chunk, CHANS)
    operands = (
        atoms, theirs, mixed, their_mixed, gates, their_gates, radial, head, density_row, ups,
        sums, spread, halo,
    )
    payload = call(backward_kernel, shape((PAYLOAD, CHANS), BF16), "backward")(*operands)
    with jax.named_scope("reduce_grads"):
        payload = reduce_all(payload)
    loss, density, deg, gate, embed_grad, radial_grad, hidden, bias, out = call(
        unpack_kernel,
        [
            shape((1, 1)),
            shape((1, PROBES)),
            shape((DEGREES, CHANS, CHANS)),
            shape((CHANS, (DEGREES - 1) * CHANS)),
            shape((KINDS, CHANS)),
            shape((BASES, DEGREES * CHANS)),
            shape((CHANS, CHANS)),
            shape((1, CHANS)),
            shape((1, CHANS)),
        ],
        "unpack",
    )(payload)
    return (
        loss.reshape(()), density.reshape(PROBES), deg, gate, embed_grad, radial_grad, hidden,
        bias.reshape(CHANS), out.reshape(CHANS),
    )


def solution(mesh):
    slabs, shards = mesh.devices.shape
    fine = mesh.devices.reshape(slabs // 8, 2, 4, shards // 2, 2)
    fine = Mesh(fine, ("zh", "zl", "y", "x", "c"))
    in_specs = (
        P(SLAB + ATOM, None),
        P(SLAB + ATOM),
        P(SLAB, ATOM, None, None),
        P(ATOM, SLAB),
        P(None, ATOM, SLAB),
        P(ATOM, SLAB),
        P(SLAB),
        P(),
        P(),
        P(),
        P(),
        P(),
        P(),
        P(),
    )
    out_specs = (P(), P(SLAB), P(), P(), P(), P(), P(), P(), P())
    return jax.shard_map(
        on_device, mesh=fine, in_specs=in_specs, out_specs=out_specs, check_vma=False
    )
```

```python
import functools
import math

import jax
import jax.numpy as jnp
from jax import lax
from jax.experimental import pallas as pl
from jax.experimental.pallas import tpu as pltpu
from jax.sharding import Mesh, PartitionSpec as P

OFFSETS = (-2, -1, 1, 2)
CUTOFF = 4.0
PRECISE = lax.Precision.HIGHEST
F32 = jnp.float32
BF16 = jnp.bfloat16
SLAB = ("zh", "zl", "y")
ATOM = ("x", "c")
PLANE = ("y", "x", "c")
NEAR = ("zl", "y", "x", "c")
DEGREES = 5
COMPS = DEGREES * DEGREES
CHANS = 128
ATOMS = 64
SLOTS = 2
PROBES = 128
SPAN = SLOTS * PROBES
ROWS = 4
HALO = 2
OWN_PAIRS = ROWS * SPAN
HALO_PAIRS = HALO * SPAN
PAIRS = OWN_PAIRS + HALO_PAIRS
FIELDS = 32
BASES = 8
KINDS = 8
PAYLOAD = 1536
EMBED_ROW = DEGREES * BASES
INTS_ROW = EMBED_ROW + KINDS
CONST_ROW = INTS_ROW + 8
SMALL_ROWS = CONST_ROW + 8 + CHANS


def first_rows(degree):
    return degree * degree * ATOMS, (degree + 1) * (degree + 1) * ATOMS


def lanes(block):
    return slice(block * CHANS, (block + 1) * CHANS)


def along_first(left, right, precision=None):
    return lax.dot_general(
        left, right, (((0,), (0,)), ((), ())), preferred_element_type=F32, precision=precision
    )


def along_last(left, right, precision=None):
    return lax.dot_general(
        left, right, (((1,), (1,)), ((), ())), preferred_element_type=F32, precision=precision
    )


def matmul(left, right, precision=None):
    return jnp.dot(left, right, preferred_element_type=F32, precision=precision)


def component_rows(feats_ref, degree):
    parts = [feats_ref[:, lanes(m)] for m in range(degree * degree, (degree + 1) * (degree + 1))]
    return parts[0] if degree == 0 else jnp.concatenate(parts, axis=0)


def over_components(gate, degree):
    return jnp.concatenate([gate] * (2 * degree + 1), axis=0)


def kind_rows(species):
    ids = lax.broadcasted_iota(jnp.int32, (KINDS, ATOMS), 0).astype(F32)
    return (ids == species).astype(F32)


def owner_tables(lists, owners_ref):
    ids = lax.broadcasted_iota(jnp.int32, (ATOMS, ATOMS), 0).astype(F32)
    same = lax.broadcasted_iota(jnp.int32, (ATOMS, ATOMS), 1).astype(F32)
    for index in range(1 + len(OFFSETS)):
        row = same if index == 2 else lists[index - (index > 2)]
        owners_ref[index] = (ids == row).astype(BF16)


def started(pairs, sems):
    copies = [
        pltpu.make_async_copy(source, target, sems.at[index])
        for index, (source, target) in enumerate(pairs)
    ]
    for copy in copies:
        copy.start()
    return copies


def encode_rows(
    feats_ref, species, w_deg_ref, w_gate_ref, embed_ref, rows_ref, mixed_ref, gates_ref
):
    scalar = feats_ref[:, lanes(0)]
    gates = jax.nn.sigmoid(matmul(scalar, w_gate_ref[...]))
    gates_ref[...] = gates
    for degree in range(DEGREES):
        low, high = first_rows(degree)
        rows = component_rows(feats_ref, degree)
        mixed = matmul(rows, w_deg_ref[degree])
        mixed_ref[low:high, :] = mixed
        if degree == 0:
            added = jax.nn.silu(mixed) + along_first(
                kind_rows(species), embed_ref[...], PRECISE
            )
        else:
            added = mixed * over_components(gates[:, lanes(degree - 1)], degree)
        rows_ref[low:high, :] = (rows.astype(F32) + added).astype(BF16)


def lists_of(ints_ref):
    count = len(OFFSETS)
    lists = [ints_ref[which : which + 1, 0:ATOMS] for which in range(count)]
    return lists, ints_ref[count : count + 1, 0:ATOMS]


def encode_kernel(
    feats_ref, w_deg_ref, w_gate_ref, small_ref,
    rows_ref, owners_ref, split_ref, w_deg_out_ref, w_gate_out_ref, embed_ref, ints_ref,
    const_ref, mixed_ref, gates_ref,
):
    w_deg_out_ref[...] = w_deg_ref[...]
    w_gate_out_ref[...] = w_gate_ref[...]
    embed_ref[...] = small_ref[EMBED_ROW:INTS_ROW, :]
    ints_ref[...] = small_ref[INTS_ROW:CONST_ROW, :]
    const_ref[...] = small_ref[CONST_ROW:, :]
    lists, species = lists_of(ints_ref)
    owner_tables(lists, owners_ref)
    w_radial = jnp.concatenate(
        [small_ref[degree * BASES : (degree + 1) * BASES, :] for degree in range(DEGREES)], axis=1
    )
    split_ref[...] = stacked(w_radial, (0, 0, 1, 1, 0, 2))
    encode_rows(
        feats_ref, species, w_deg_ref, w_gate_ref, embed_ref, rows_ref, mixed_ref, gates_ref
    )


def parts_of(values):
    high = values.astype(BF16)
    rest = values - high.astype(F32)
    middle = rest.astype(BF16)
    low = (rest - middle.astype(F32)).astype(BF16)
    return high, middle, low


def stacked(values, order):
    parts = [part.astype(F32) for part in parts_of(values)]
    return jnp.concatenate([parts[index] for index in order], axis=0).astype(BF16)


def pack_kernel(
    harm_hbm, dist_hbm, nbr_hbm, lists_hbm, species_hbm, w_radial_hbm, embed_hbm, w_hidden_hbm,
    b_hidden_hbm, w_out_hbm, target_hbm, copies_hbm, ints_hbm, small_hbm,
    pack_ref, small_ref, nbr_ref, lists_ref, species_ref, b_hidden_ref, w_out_ref, target_ref,
    sems, out_sems,
):
    copies = started(
        [
            (harm_hbm, pack_ref.at[pl.ds(0, COMPS)]),
            (dist_hbm, pack_ref.at[COMPS]),
            (nbr_hbm, nbr_ref),
            (lists_hbm, lists_ref),
            (species_hbm, species_ref),
            (embed_hbm, small_ref.at[pl.ds(EMBED_ROW, KINDS)]),
            (w_hidden_hbm, small_ref.at[pl.ds(CONST_ROW + 8, CHANS)]),
            (b_hidden_hbm, b_hidden_ref),
            (w_out_hbm, w_out_ref),
            (target_hbm, target_ref),
        ]
        + [
            (
                w_radial_hbm.at[:, pl.ds(degree * CHANS, CHANS)],
                small_ref.at[pl.ds(degree * BASES, BASES)],
            )
            for degree in range(DEGREES)
        ],
        sems,
    )
    pack_ref[COMPS + 2 :] = jnp.zeros((FIELDS - COMPS - 2, SLOTS, PROBES), F32)
    small_ref[INTS_ROW : CONST_ROW + 8, :] = jnp.zeros((16, CHANS), F32)
    for copy in copies:
        copy.wait()
    count = len(OFFSETS)
    small_ref[INTS_ROW : INTS_ROW + count, 0:ATOMS] = lists_ref[...].astype(F32)
    small_ref[INTS_ROW + count : INTS_ROW + count + 1, 0:ATOMS] = species_ref[...].astype(F32)
    small_ref[CONST_ROW : CONST_ROW + 3, :] = jnp.concatenate(
        [b_hidden_ref[...], w_out_ref[...], target_ref[...]], axis=0
    )
    pack_ref[COMPS + 1] = nbr_ref[...].astype(F32)
    writes = started(
        [(small_ref.at[pl.ds(INTS_ROW, 8)], ints_hbm), (small_ref, small_hbm)]
        + [(pack_ref, copies_hbm.at[row]) for row in range(ROWS)],
        out_sems,
    )
    for write in writes:
        write.wait()


def plane_halves():
    row = lax.axis_index("y")
    upper = jnp.where(row > 1, 1, 0)
    return row, HALO - HALO * upper, row + ROWS - 2 * ROWS * upper


def pair_kernel(
    packs_ref, theirs_ref, their_ints_ref, rows_ref, owners_ref, split_ref, w_deg_ref,
    w_gate_ref, embed_ref, out_ref, spread_ref, halo_ref, sums_ref, radial_ref, their_mixed_ref, their_gates_ref,
    their_rows_ref, their_owners_ref,
):
    shards, chunk = out_ref.shape[1], out_ref.shape[2]
    own_row, first, partner_row = plane_halves()
    sub = lax.broadcasted_iota(jnp.int32, (ATOMS, PROBES), 0).astype(F32)

    def spread_pairs(target_ref, tables_ref, begin, probe_row, atom_row):
        delta = probe_row - atom_row
        valid = jnp.logical_and(delta >= -2, delta <= 2)
        table = jnp.clip(delta + 2, 0, 4)
        block = jnp.where(delta < 0, delta + 3, jnp.where(delta > 0, delta + 2, 0))
        base = jnp.where(valid, block * ATOMS, 1 << 20).astype(F32)
        for slot in range(SLOTS):
            start = begin + slot * PROBES

            def row(field):
                return packs_ref[probe_row, field, slot : slot + 1, :]

            hot = (row(COMPS + 1) - base == sub).astype(BF16)
            hot = matmul(tables_ref[table], hot)
            for m in range(COMPS):
                target_ref[m * ATOMS : (m + 1) * ATOMS, start : start + PROBES] = (
                    hot * row(m)
                ).astype(BF16)

    for row in range(ROWS):
        spread_pairs(spread_ref, owners_ref, row * SPAN, row, own_row)
    their_lists, their_species = lists_of(their_ints_ref)
    owner_tables(their_lists, their_owners_ref)
    encode_rows(
        theirs_ref, their_species, w_deg_ref, w_gate_ref, embed_ref, their_rows_ref,
        their_mixed_ref, their_gates_ref,
    )
    for row in range(HALO):
        spread_pairs(halo_ref, their_owners_ref, row * SPAN, first + row, partner_row)
    dists = [packs_ref[row, COMPS, slot : slot + 1, :] for row in range(ROWS) for slot in range(SLOTS)]
    dists += [
        packs_ref[first + row, COMPS, slot : slot + 1, :]
        for row in range(HALO)
        for slot in range(SLOTS)
    ]
    dist = jnp.concatenate(dists, axis=1)
    orders = lax.broadcasted_iota(jnp.int32, (BASES, PAIRS), 0).astype(F32) + 1.0
    phase = math.pi * dist / CUTOFF
    envelope = 0.5 * (jnp.cos(phase) + 1.0) / dist
    basis_split = stacked(jnp.sin(phase * orders) * envelope, (0, 1, 0, 1, 2, 0))
    sums_ref[DEGREES * CHANS :, :] = basis_split[0 : 2 * BASES, :]
    total = None
    for degree in range(DEGREES):
        low, high = first_rows(degree)
        radial = along_first(split_ref[:, lanes(degree)], basis_split)
        radial_ref[lanes(degree), :] = radial
        sums = jnp.concatenate(
            [
                along_first(rows_ref[low:high, :], spread_ref[low:high, :]),
                along_first(their_rows_ref[low:high, :], halo_ref[low:high, :]),
            ],
            axis=1,
        )
        sums_ref[lanes(degree), :] = sums.astype(BF16)
        term = radial * sums
        total = term if total is None else total + term

    def value_of(block):
        start = block * SPAN
        both = total[:, start : start + PROBES] + total[:, start + PROBES : start + SPAN]
        return both.T

    for row in range(ROWS):
        value = value_of(row)
        for shard in range(shards):
            out_ref[row, shard] = value[shard * chunk : (shard + 1) * chunk, :]
    for row in range(HALO):
        value = value_of(ROWS + row)
        for shard in range(shards):
            out_ref[first + row, shard] += value[shard * chunk : (shard + 1) * chunk, :]


def silu_slope(values):
    logistic = jax.nn.sigmoid(values)
    return logistic * (1.0 + values * (1.0 - logistic))


def sum_kernel(parts_ref, out_ref):
    total = parts_ref[0].astype(F32)
    for index in range(1, parts_ref.shape[0]):
        total = total + parts_ref[index].astype(F32)
    if len(out_ref.shape) == len(parts_ref.shape):
        for copy in range(out_ref.shape[0]):
            out_ref[copy] = total.astype(out_ref.dtype)
    else:
        out_ref[...] = total.astype(out_ref.dtype)


def readout_kernel(
    scale, parts_ref, const_ref, up_ref, head_ref, density_ref, column_ref
):
    chunk = parts_ref.shape[1]
    shard = lax.axis_index("x") * lax.axis_size("c") + lax.axis_index("c")
    start = pl.multiple_of(shard * chunk, chunk)
    column_ref[...] = jnp.broadcast_to(const_ref[2:3, :], (PROBES, PROBES)).T
    target = column_ref[pl.ds(start, chunk), :]
    summed = parts_ref[0]
    for index in range(1, parts_ref.shape[0]):
        summed = summed + parts_ref[index]
    w_hidden = const_ref[8:, :]
    w_out = const_ref[1:2, :]
    hidden_pre = matmul(summed, w_hidden, PRECISE) + const_ref[0:1, :]
    activated = jax.nn.silu(hidden_pre)
    density = jnp.sum(activated * w_out, axis=1, keepdims=True)
    error = density - target
    error_grad = error * scale
    pre_grad = w_out * silu_slope(hidden_pre) * error_grad
    spot = lax.broadcasted_iota(jnp.int32, (chunk, PROBES), 0) + start
    mask = (spot == lax.broadcasted_iota(jnp.int32, (chunk, PROBES), 1)).astype(F32)
    upstream = along_last(pre_grad, w_hidden, PRECISE)
    for copy in range(up_ref.shape[0]):
        up_ref[copy] = upstream
    density_ref[...] = jnp.sum(mask * density, axis=0, keepdims=True)
    head_ref[0:CHANS, :] = along_first(summed, pre_grad, PRECISE)
    bias = jnp.sum(pre_grad, axis=0, keepdims=True)
    out = jnp.sum(activated * error_grad, axis=0, keepdims=True)
    loss = jnp.sum(mask * error * error * (0.5 * scale), axis=0, keepdims=True)
    head_ref[CHANS : CHANS + 16, :] = jnp.concatenate(
        [bias, out, loss, jnp.zeros((13, CHANS), F32)], axis=0
    )


def own_slab():
    depth = lax.axis_index("zh") * lax.axis_size("zl") + lax.axis_index("zl")
    return depth * ROWS + lax.axis_index("y")


def backward_kernel(
    atoms_ref, theirs_ref, ints_ref, their_ints_ref, mixed_ref, their_mixed_ref, gates_ref, their_gates_ref,
    radial_ref, head_ref, density_ref, up_ref, sums_ref, spread_ref, halo_ref, payload_ref,
):
    shards = up_ref.shape[1]
    first = plane_halves()[1]

    def block_of(row):
        parts = [up_ref[row, shard] for shard in range(shards)]
        return [jnp.concatenate(parts, axis=0).T] * SLOTS

    blocks = []
    for row in list(range(ROWS)) + [first + row for row in range(HALO)]:
        blocks += block_of(row)
    upstream = jnp.concatenate(blocks, axis=1)
    scalar = jnp.concatenate([atoms_ref[:, lanes(0)], theirs_ref[:, lanes(0)]], axis=0)
    gates = jnp.concatenate([gates_ref[...], their_gates_ref[...]], axis=0)
    kinds = jnp.concatenate(
        [kind_rows(lists_of(ref)[1]) for ref in (ints_ref, their_ints_ref)], axis=1
    )
    basis_split = sums_ref[DEGREES * CHANS :, :]
    radial_grads = []
    for degree in range(DEGREES):
        low, high = first_rows(degree)
        size = high - low
        inner = (radial_ref[lanes(degree), :] * upstream).astype(BF16)
        grads = jnp.concatenate(
            [
                along_last(spread_ref[low:high, :], inner[:, 0:OWN_PAIRS]),
                along_last(halo_ref[low:high, :], inner[:, OWN_PAIRS:]),
            ],
            axis=0,
        )
        product = (sums_ref[lanes(degree), :].astype(F32) * upstream).astype(BF16)
        both = along_last(product, basis_split)
        radial_grads.append((both[:, 0:BASES] + both[:, BASES : 2 * BASES]).T)
        rows = jnp.concatenate(
            [component_rows(atoms_ref, degree), component_rows(theirs_ref, degree)], axis=0
        )
        mixed = jnp.concatenate([mixed_ref[low:high, :], their_mixed_ref[low:high, :]], axis=0)
        if degree == 0:
            mixed_grad = grads * silu_slope(mixed)
            embed_grad = matmul(kinds, grads, PRECISE)
        else:
            gate = gates[:, lanes(degree - 1)]
            spread_gate = jnp.concatenate(
                [over_components(gate[0:ATOMS, :], degree), over_components(gate[ATOMS:, :], degree)],
                axis=0,
            )
            mixed_grad = grads * spread_gate
            product = grads * mixed
            totals = []
            for side in range(2):
                total = product[side * size : side * size + ATOMS, :]
                for comp in range(1, 2 * degree + 1):
                    begin = side * size + comp * ATOMS
                    total = total + product[begin : begin + ATOMS, :]
                totals.append(total)
            total = jnp.concatenate(totals, axis=0)
            pre = (total * gate * (1.0 - gate)).astype(BF16)
            start = (DEGREES + degree - 1) * CHANS
            payload_ref[start : start + CHANS, :] = along_first(scalar, pre).astype(BF16)
        payload_ref[degree * CHANS : (degree + 1) * CHANS, :] = along_first(
            rows, mixed_grad.astype(BF16)
        ).astype(BF16)
    base = (2 * DEGREES - 1) * CHANS
    payload_ref[base : base + CHANS + 16, :] = head_ref[...].astype(BF16)
    base += CHANS + 16
    payload_ref[base : base + 48, :] = jnp.concatenate(
        radial_grads + [embed_grad], axis=0
    ).astype(BF16)
    base += 48
    slabs = (PAYLOAD - base) // 3
    here = lax.broadcasted_iota(jnp.int32, (slabs, PROBES), 0) == own_slab()
    for part in parts_of(jnp.where(here, density_ref[...], 0.0)):
        payload_ref[base : base + slabs, :] = part
        base += slabs


def unpack_kernel(
    payload_ref, loss_ref, density_ref, deg_ref, gate_ref, embed_ref, radial_ref, hidden_ref,
    bias_ref, out_ref,
):
    for degree in range(DEGREES):
        deg_ref[degree] = payload_ref[lanes(degree), :].astype(F32)
    for degree in range(1, DEGREES):
        gate_ref[:, lanes(degree - 1)] = payload_ref[lanes(DEGREES + degree - 1), :].astype(F32)
    base = (2 * DEGREES - 1) * CHANS
    hidden_ref[...] = payload_ref[base : base + CHANS, :].astype(F32)
    base += CHANS
    misc = payload_ref[base : base + 16, :].astype(F32)
    bias_ref[...] = misc[0:1, :]
    out_ref[...] = misc[1:2, :]
    loss_ref[...] = jnp.sum(misc[2:3, :], axis=1, keepdims=True)
    base += 16
    small = payload_ref[base : base + 48, :].astype(F32)
    for degree in range(DEGREES):
        radial_ref[:, lanes(degree)] = small[degree * BASES : (degree + 1) * BASES, :]
    embed_ref[...] = small[DEGREES * BASES :, :]
    base += 48
    slabs = (PAYLOAD - base) // 3
    total = None
    for _ in range(3):
        part = payload_ref[base : base + slabs, :].astype(F32)
        total = part if total is None else total + part
        base += slabs
    here = lax.broadcasted_iota(jnp.int32, (slabs, PROBES), 0) == own_slab()
    density_ref[...] = jnp.sum(jnp.where(here, total, 0.0), axis=0, keepdims=True)


def shape(dims, dtype=F32):
    return jax.ShapeDtypeStruct(dims, dtype)


def call(kernel, outs, name, limit=32, **options):
    return pl.pallas_call(
        kernel,
        out_shape=outs,
        name=name,
        compiler_params=pltpu.CompilerParams(vmem_limit_bytes=limit * 1024 * 1024),
        **options,
    )


def to_partner(block):
    count = lax.axis_size(SLAB)
    route = [(i, (i + (ROWS if i % ROWS >= HALO else -ROWS)) % count) for i in range(count)]
    return lax.ppermute(block, SLAB, route)


def reduce_all(payload):
    count, depth = lax.axis_size(NEAR), lax.axis_size("zh")
    rows = PAYLOAD // count
    parts = lax.all_to_all(payload.reshape(count, rows, CHANS), NEAR, 0, 0)
    copies = call(sum_kernel, shape((depth, rows, CHANS), BF16), "sum_near")(parts)
    parts = lax.all_to_all(copies, "zh", 0, 0)
    copies = call(sum_kernel, shape((count, rows, CHANS), BF16), "sum_depth")(parts)
    return lax.all_to_all(copies, NEAR, 0, 0).reshape(PAYLOAD, CHANS)


def on_device(
    atom_feats, species, send_rows, neighbours, harmonics, distances, target,
    w_deg, w_gate, embed, w_radial, w_hidden, b_hidden, w_out,
):
    slab_count = lax.axis_size(SLAB)
    shards = lax.axis_size(ATOM)
    chunk = PROBES // shards
    scale = 1.0 / math.sqrt(PROBES * slab_count)
    species = species.reshape(1, ATOMS)
    lists = send_rows[0, 0]
    far = pl.BlockSpec(memory_space=pl.ANY)
    field_shape = (FIELDS, SLOTS, PROBES)
    with jax.named_scope("exchange_atoms"):
        theirs = to_partner(atom_feats)
    rows_of = [row.reshape(1, CHANS) for row in (b_hidden, w_out, target)]
    operands = (
        harmonics, distances, neighbours, lists, species, w_radial, embed, w_hidden, *rows_of
    )
    held = [
        shape((ROWS,) + field_shape),
        shape((8, CHANS)),
        shape((SMALL_ROWS, CHANS)),
    ]
    copies, ints, small = call(
        pack_kernel,
        held,
        "pack",
        limit=63,
        in_specs=[far] * len(operands),
        out_specs=[far] * len(held),
        scratch_shapes=[
            pltpu.VMEM(field_shape, F32),
            pltpu.VMEM(held[2].shape, F32),
            pltpu.VMEM((SLOTS, PROBES), jnp.int32),
            pltpu.VMEM(lists.shape, jnp.int32),
            pltpu.VMEM(species.shape, jnp.int32),
        ]
        + [pltpu.VMEM((1, CHANS), F32)] * 3
        + [
            pltpu.SemaphoreType.DMA((len(operands) - 1 + DEGREES,)),
            pltpu.SemaphoreType.DMA((2 + ROWS,)),
        ],
    )(*operands)
    with jax.named_scope("exchange_lists"):
        their_ints = to_partner(ints)
    with jax.named_scope("gather_pairs"):
        packs = lax.all_to_all(copies, "y", 0, 0)
    mixed_shapes = [shape((COMPS * ATOMS, CHANS)), shape((ATOMS, (DEGREES - 1) * CHANS))]
    rows, owners, split, w_deg_near, w_gate_near, embed_near, own_ints, consts, mixed, gates = call(
        encode_kernel,
        [
            shape((COMPS * ATOMS, CHANS), BF16),
            shape((1 + len(OFFSETS), ATOMS, ATOMS), BF16),
            shape((6 * BASES, DEGREES * CHANS), BF16),
            shape(w_deg.shape, BF16),
            shape(w_gate.shape, BF16),
            shape(embed.shape),
            shape(ints.shape),
            shape((SMALL_ROWS - CONST_ROW, CHANS)),
        ]
        + mixed_shapes,
        "encode",
    )(atom_feats, w_deg, w_gate, small)
    values, spread, halo, sums, radial, their_mixed, their_gates = call(
        pair_kernel,
        [
            shape((ROWS, shards, chunk, CHANS)),
            shape((COMPS * ATOMS, OWN_PAIRS), BF16),
            shape((COMPS * ATOMS, HALO_PAIRS), BF16),
            shape((DEGREES * CHANS + 2 * BASES, PAIRS), BF16),
            shape((DEGREES * CHANS, PAIRS)),
        ]
        + mixed_shapes,
        "pair_sums",
        scratch_shapes=[pltpu.VMEM(rows.shape, BF16), pltpu.VMEM(owners.shape, BF16)],
    )(
        packs, theirs, their_ints, rows, owners, split, w_deg_near, w_gate_near, embed_near
    )
    with jax.named_scope("scatter_sums"):
        parts = lax.all_to_all(values.reshape(ROWS * shards, chunk, CHANS), PLANE, 0, 0)
    up, head, density_row = call(
        functools.partial(readout_kernel, scale),
        [
            shape((ROWS * shards, chunk, CHANS)),
            shape((CHANS + 16, CHANS)),
            shape((1, PROBES)),
        ],
        "readout",
        scratch_shapes=[pltpu.VMEM((PROBES, PROBES), F32)],
    )(parts, consts)
    with jax.named_scope("gather_grads"):
        ups = lax.all_to_all(up, PLANE, 0, 0).reshape(ROWS, shards, chunk, CHANS)
    operands = (
        atom_feats, theirs, own_ints, their_ints, mixed, their_mixed, gates, their_gates, radial,
        head, density_row, ups, sums, spread, halo,
    )
    payload = call(backward_kernel, shape((PAYLOAD, CHANS), BF16), "backward")(*operands)
    with jax.named_scope("reduce_grads"):
        payload = reduce_all(payload)
    loss, density, deg, gate, embed_grad, radial_grad, hidden, bias, out = call(
        unpack_kernel,
        [
            shape((1, 1)),
            shape((1, PROBES)),
            shape((DEGREES, CHANS, CHANS)),
            shape((CHANS, (DEGREES - 1) * CHANS)),
            shape((KINDS, CHANS)),
            shape((BASES, DEGREES * CHANS)),
            shape((CHANS, CHANS)),
            shape((1, CHANS)),
            shape((1, CHANS)),
        ],
        "unpack",
    )(payload)
    return (
        loss.reshape(()), density.reshape(PROBES), deg, gate, embed_grad, radial_grad, hidden,
        bias.reshape(CHANS), out.reshape(CHANS),
    )


def solution(mesh):
    slabs, shards = mesh.devices.shape
    fine = mesh.devices.reshape(slabs // 8, 2, 4, shards // 2, 2)
    fine = Mesh(fine, ("zh", "zl", "y", "x", "c"))
    in_specs = (
        P(SLAB + ATOM, None),
        P(SLAB + ATOM),
        P(SLAB, ATOM, None, None),
        P(ATOM, SLAB),
        P(None, ATOM, SLAB),
        P(ATOM, SLAB),
        P(SLAB),
        P(),
        P(),
        P(),
        P(),
        P(),
        P(),
        P(),
    )
    out_specs = (P(), P(SLAB), P(), P(), P(), P(), P(), P(), P())
    return jax.shard_map(
        on_device, mesh=fine, in_specs=in_specs, out_specs=out_specs, check_vma=False
    )
```

```python
import functools
import math

import jax
import jax.numpy as jnp
from jax import lax
from jax.experimental import pallas as pl
from jax.experimental.pallas import tpu as pltpu
from jax.sharding import Mesh, PartitionSpec as P

OFFSETS = (-2, -1, 1, 2)
CUTOFF = 4.0
PRECISE = lax.Precision.HIGHEST
F32 = jnp.float32
BF16 = jnp.bfloat16
SLAB = ("zh", "zl", "y")
ATOM = ("x", "c")
PLANE = ("y", "x", "c")
NEAR = ("zl", "y", "x", "c")
DEGREES = 5
COMPS = DEGREES * DEGREES
CHANS = 128
ATOMS = 64
SLOTS = 2
PROBES = 128
SPAN = SLOTS * PROBES
ROWS = 4
HALO = 2
OWN_PAIRS = ROWS * SPAN
HALO_PAIRS = HALO * SPAN
PAIRS = OWN_PAIRS + HALO_PAIRS
FIELDS = 32
BASES = 8
KINDS = 8
PAYLOAD = 1536
EMBED_ROW = DEGREES * BASES
INTS_ROW = EMBED_ROW + KINDS
CONST_ROW = INTS_ROW + 8
SMALL_ROWS = CONST_ROW + 8 + CHANS


def first_rows(degree):
    return degree * degree * ATOMS, (degree + 1) * (degree + 1) * ATOMS


def lanes(block):
    return slice(block * CHANS, (block + 1) * CHANS)


def along_first(left, right, precision=None):
    return lax.dot_general(
        left, right, (((0,), (0,)), ((), ())), preferred_element_type=F32, precision=precision
    )


def along_last(left, right, precision=None):
    return lax.dot_general(
        left, right, (((1,), (1,)), ((), ())), preferred_element_type=F32, precision=precision
    )


def matmul(left, right, precision=None):
    return jnp.dot(left, right, preferred_element_type=F32, precision=precision)


def component_rows(feats_ref, degree):
    parts = [feats_ref[:, lanes(m)] for m in range(degree * degree, (degree + 1) * (degree + 1))]
    return parts[0] if degree == 0 else jnp.concatenate(parts, axis=0)


def over_components(gate, degree):
    return jnp.concatenate([gate] * (2 * degree + 1), axis=0)


def kind_rows(species):
    ids = lax.broadcasted_iota(jnp.int32, (KINDS, ATOMS), 0).astype(F32)
    return (ids == species).astype(F32)


def owner_tables(lists, owners_ref):
    ids = lax.broadcasted_iota(jnp.int32, (ATOMS, ATOMS), 0).astype(F32)
    same = lax.broadcasted_iota(jnp.int32, (ATOMS, ATOMS), 1).astype(F32)
    for index in range(1 + len(OFFSETS)):
        row = same if index == 2 else lists[index - (index > 2)]
        owners_ref[index] = (ids == row).astype(BF16)


def started(pairs, sems):
    copies = [
        pltpu.make_async_copy(source, target, sems.at[index])
        for index, (source, target) in enumerate(pairs)
    ]
    for copy in copies:
        copy.start()
    return copies


def encode_rows(
    feats_ref, species, w_deg_ref, w_gate_ref, embed_ref, rows_ref, mixed_ref, gates_ref
):
    scalar = feats_ref[:, lanes(0)]
    gates = jax.nn.sigmoid(matmul(scalar, w_gate_ref[...]))
    gates_ref[...] = gates
    for degree in range(DEGREES):
        low, high = first_rows(degree)
        rows = component_rows(feats_ref, degree)
        mixed = matmul(rows, w_deg_ref[degree])
        mixed_ref[low:high, :] = mixed
        if degree == 0:
            added = jax.nn.silu(mixed) + along_first(
                kind_rows(species), embed_ref[...], PRECISE
            )
        else:
            added = mixed * over_components(gates[:, lanes(degree - 1)], degree)
        rows_ref[low:high, :] = (rows.astype(F32) + added).astype(BF16)


def lists_of(ints_ref):
    count = len(OFFSETS)
    lists = [ints_ref[which : which + 1, 0:ATOMS] for which in range(count)]
    return lists, ints_ref[count : count + 1, 0:ATOMS]


def parts_of(values):
    high = values.astype(BF16)
    rest = values - high.astype(F32)
    middle = rest.astype(BF16)
    low = (rest - middle.astype(F32)).astype(BF16)
    return high, middle, low


def stacked(values, order):
    parts = [part.astype(F32) for part in parts_of(values)]
    return jnp.concatenate([parts[index] for index in order], axis=0).astype(BF16)


def pack_kernel(
    harm_hbm, dist_hbm, nbr_hbm, lists_hbm, species_hbm, w_radial_hbm, embed_hbm, w_hidden_hbm,
    b_hidden_hbm, w_out_hbm, target_hbm, copies_hbm, ints_hbm, small_hbm,
    pack_ref, small_ref, nbr_ref, lists_ref, species_ref, b_hidden_ref, w_out_ref, target_ref,
    sems, out_sems,
):
    copies = started(
        [
            (harm_hbm, pack_ref.at[pl.ds(0, COMPS)]),
            (dist_hbm, pack_ref.at[COMPS]),
            (nbr_hbm, nbr_ref),
            (lists_hbm, lists_ref),
            (species_hbm, species_ref),
            (embed_hbm, small_ref.at[pl.ds(EMBED_ROW, KINDS)]),
            (w_hidden_hbm, small_ref.at[pl.ds(CONST_ROW + 8, CHANS)]),
            (b_hidden_hbm, b_hidden_ref),
            (w_out_hbm, w_out_ref),
            (target_hbm, target_ref),
        ]
        + [
            (
                w_radial_hbm.at[:, pl.ds(degree * CHANS, CHANS)],
                small_ref.at[pl.ds(degree * BASES, BASES)],
            )
            for degree in range(DEGREES)
        ],
        sems,
    )
    pack_ref[COMPS + 2 :] = jnp.zeros((FIELDS - COMPS - 2, SLOTS, PROBES), F32)
    small_ref[INTS_ROW : CONST_ROW + 8, :] = jnp.zeros((16, CHANS), F32)
    for copy in copies:
        copy.wait()
    count = len(OFFSETS)
    small_ref[INTS_ROW : INTS_ROW + count, 0:ATOMS] = lists_ref[...].astype(F32)
    small_ref[INTS_ROW + count : INTS_ROW + count + 1, 0:ATOMS] = species_ref[...].astype(F32)
    small_ref[CONST_ROW : CONST_ROW + 3, :] = jnp.concatenate(
        [b_hidden_ref[...], w_out_ref[...], target_ref[...]], axis=0
    )
    pack_ref[COMPS + 1] = nbr_ref[...].astype(F32)
    writes = started(
        [(small_ref.at[pl.ds(INTS_ROW, 8)], ints_hbm), (small_ref, small_hbm)]
        + [(pack_ref, copies_hbm.at[row]) for row in range(ROWS)],
        out_sems,
    )
    for write in writes:
        write.wait()


def stage_kernel(*refs):
    half = len(refs) // 2
    for source, target in zip(refs[:half], refs[half:]):
        target[...] = source[...]


def plane_halves():
    row = lax.axis_index("y")
    upper = jnp.where(row > 1, 1, 0)
    return row, HALO - HALO * upper, row + ROWS - 2 * ROWS * upper


def pair_kernel(
    packs_ref, theirs_ref, their_ints_ref, feats_ref, w_deg_ref, w_gate_ref, small_ref,
    out_ref, spread_ref, halo_ref, sums_ref, radial_ref, ints_ref, const_ref,
    mixed_ref, gates_ref, their_mixed_ref, their_gates_ref,
    rows_ref, owners_ref, their_rows_ref, their_owners_ref, embed_ref,
):
    embed_ref[...] = small_ref[EMBED_ROW:INTS_ROW, :]
    ints_ref[...] = small_ref[INTS_ROW:CONST_ROW, :]
    const_ref[...] = small_ref[CONST_ROW:, :]
    w_radial = jnp.concatenate(
        [small_ref[degree * BASES : (degree + 1) * BASES, :] for degree in range(DEGREES)], axis=1
    )
    radial_split = stacked(w_radial, (0, 0, 1, 1, 0, 2))
    lists, species = lists_of(ints_ref)
    owner_tables(lists, owners_ref)
    encode_rows(
        feats_ref, species, w_deg_ref, w_gate_ref, embed_ref, rows_ref, mixed_ref, gates_ref
    )
    shards, chunk = out_ref.shape[1], out_ref.shape[2]
    own_row, first, partner_row = plane_halves()
    sub = lax.broadcasted_iota(jnp.int32, (ATOMS, PROBES), 0).astype(F32)

    def spread_pairs(target_ref, tables_ref, begin, probe_row, atom_row):
        delta = probe_row - atom_row
        valid = jnp.logical_and(delta >= -2, delta <= 2)
        table = jnp.clip(delta + 2, 0, 4)
        block = jnp.where(delta < 0, delta + 3, jnp.where(delta > 0, delta + 2, 0))
        base = jnp.where(valid, block * ATOMS, 1 << 20).astype(F32)
        for slot in range(SLOTS):
            start = begin + slot * PROBES

            def row(field):
                return packs_ref[probe_row, field, slot : slot + 1, :]

            hot = (row(COMPS + 1) - base == sub).astype(BF16)
            hot = matmul(tables_ref[table], hot)
            for m in range(COMPS):
                target_ref[m * ATOMS : (m + 1) * ATOMS, start : start + PROBES] = (
                    hot * row(m)
                ).astype(BF16)

    for row in range(ROWS):
        spread_pairs(spread_ref, owners_ref, row * SPAN, row, own_row)
    their_lists, their_species = lists_of(their_ints_ref)
    owner_tables(their_lists, their_owners_ref)
    encode_rows(
        theirs_ref, their_species, w_deg_ref, w_gate_ref, embed_ref, their_rows_ref,
        their_mixed_ref, their_gates_ref,
    )
    for row in range(HALO):
        spread_pairs(halo_ref, their_owners_ref, row * SPAN, first + row, partner_row)
    dists = [packs_ref[row, COMPS, slot : slot + 1, :] for row in range(ROWS) for slot in range(SLOTS)]
    dists += [
        packs_ref[first + row, COMPS, slot : slot + 1, :]
        for row in range(HALO)
        for slot in range(SLOTS)
    ]
    dist = jnp.concatenate(dists, axis=1)
    orders = lax.broadcasted_iota(jnp.int32, (BASES, PAIRS), 0).astype(F32) + 1.0
    phase = math.pi * dist / CUTOFF
    envelope = 0.5 * (jnp.cos(phase) + 1.0) / dist
    basis_split = stacked(jnp.sin(phase * orders) * envelope, (0, 1, 0, 1, 2, 0))
    sums_ref[DEGREES * CHANS :, :] = basis_split[0 : 2 * BASES, :]
    total = None
    for degree in range(DEGREES):
        low, high = first_rows(degree)
        radial = along_first(radial_split[:, lanes(degree)], basis_split)
        radial_ref[lanes(degree), :] = radial
        sums = jnp.concatenate(
            [
                along_first(rows_ref[low:high, :], spread_ref[low:high, :]),
                along_first(their_rows_ref[low:high, :], halo_ref[low:high, :]),
            ],
            axis=1,
        )
        sums_ref[lanes(degree), :] = sums.astype(BF16)
        term = radial * sums
        total = term if total is None else total + term

    def value_of(block):
        start = block * SPAN
        both = total[:, start : start + PROBES] + total[:, start + PROBES : start + SPAN]
        return both.T

    for row in range(ROWS):
        value = value_of(row)
        for shard in range(shards):
            out_ref[row, shard] = value[shard * chunk : (shard + 1) * chunk, :]
    for row in range(HALO):
        value = value_of(ROWS + row)
        for shard in range(shards):
            out_ref[first + row, shard] += value[shard * chunk : (shard + 1) * chunk, :]


def silu_slope(values):
    logistic = jax.nn.sigmoid(values)
    return logistic * (1.0 + values * (1.0 - logistic))


def sum_kernel(parts_ref, out_ref):
    total = parts_ref[0].astype(F32)
    for index in range(1, parts_ref.shape[0]):
        total = total + parts_ref[index].astype(F32)
    if len(out_ref.shape) == len(parts_ref.shape):
        for copy in range(out_ref.shape[0]):
            out_ref[copy] = total.astype(out_ref.dtype)
    else:
        out_ref[...] = total.astype(out_ref.dtype)


def readout_kernel(
    scale, parts_ref, const_ref, up_ref, head_ref, density_ref, column_ref
):
    chunk = parts_ref.shape[1]
    shard = lax.axis_index("x") * lax.axis_size("c") + lax.axis_index("c")
    start = pl.multiple_of(shard * chunk, chunk)
    column_ref[...] = jnp.broadcast_to(const_ref[2:3, :], (PROBES, PROBES)).T
    target = column_ref[pl.ds(start, chunk), :]
    summed = parts_ref[0]
    for index in range(1, parts_ref.shape[0]):
        summed = summed + parts_ref[index]
    w_hidden = const_ref[8:, :]
    w_out = const_ref[1:2, :]
    hidden_pre = matmul(summed, w_hidden, PRECISE) + const_ref[0:1, :]
    activated = jax.nn.silu(hidden_pre)
    density = jnp.sum(activated * w_out, axis=1, keepdims=True)
    error = density - target
    error_grad = error * scale
    pre_grad = w_out * silu_slope(hidden_pre) * error_grad
    spot = lax.broadcasted_iota(jnp.int32, (chunk, PROBES), 0) + start
    mask = (spot == lax.broadcasted_iota(jnp.int32, (chunk, PROBES), 1)).astype(F32)
    upstream = along_last(pre_grad, w_hidden, PRECISE)
    for copy in range(up_ref.shape[0]):
        up_ref[copy] = upstream
    density_ref[...] = jnp.sum(mask * density, axis=0, keepdims=True)
    head_ref[0:CHANS, :] = along_first(summed, pre_grad, PRECISE)
    bias = jnp.sum(pre_grad, axis=0, keepdims=True)
    out = jnp.sum(activated * error_grad, axis=0, keepdims=True)
    loss = jnp.sum(mask * error * error * (0.5 * scale), axis=0, keepdims=True)
    head_ref[CHANS : CHANS + 16, :] = jnp.concatenate(
        [bias, out, loss, jnp.zeros((13, CHANS), F32)], axis=0
    )


def own_slab():
    depth = lax.axis_index("zh") * lax.axis_size("zl") + lax.axis_index("zl")
    return depth * ROWS + lax.axis_index("y")


def backward_kernel(
    atoms_ref, theirs_ref, ints_ref, their_ints_ref, mixed_ref, their_mixed_ref, gates_ref, their_gates_ref,
    radial_ref, head_ref, density_ref, up_ref, sums_ref, spread_ref, halo_ref, payload_ref,
):
    shards = up_ref.shape[1]
    first = plane_halves()[1]

    def block_of(row):
        parts = [up_ref[row, shard] for shard in range(shards)]
        return [jnp.concatenate(parts, axis=0).T] * SLOTS

    blocks = []
    for row in list(range(ROWS)) + [first + row for row in range(HALO)]:
        blocks += block_of(row)
    upstream = jnp.concatenate(blocks, axis=1)
    scalar = jnp.concatenate([atoms_ref[:, lanes(0)], theirs_ref[:, lanes(0)]], axis=0)
    gates = jnp.concatenate([gates_ref[...], their_gates_ref[...]], axis=0)
    kinds = jnp.concatenate(
        [kind_rows(lists_of(ref)[1]) for ref in (ints_ref, their_ints_ref)], axis=1
    )
    basis_split = sums_ref[DEGREES * CHANS :, :]
    radial_grads = []
    for degree in range(DEGREES):
        low, high = first_rows(degree)
        size = high - low
        inner = (radial_ref[lanes(degree), :] * upstream).astype(BF16)
        grads = jnp.concatenate(
            [
                along_last(spread_ref[low:high, :], inner[:, 0:OWN_PAIRS]),
                along_last(halo_ref[low:high, :], inner[:, OWN_PAIRS:]),
            ],
            axis=0,
        )
        product = (sums_ref[lanes(degree), :].astype(F32) * upstream).astype(BF16)
        both = along_last(product, basis_split)
        radial_grads.append((both[:, 0:BASES] + both[:, BASES : 2 * BASES]).T)
        rows = jnp.concatenate(
            [component_rows(atoms_ref, degree), component_rows(theirs_ref, degree)], axis=0
        )
        mixed = jnp.concatenate([mixed_ref[low:high, :], their_mixed_ref[low:high, :]], axis=0)
        if degree == 0:
            mixed_grad = grads * silu_slope(mixed)
            embed_grad = matmul(kinds, grads, PRECISE)
        else:
            gate = gates[:, lanes(degree - 1)]
            spread_gate = jnp.concatenate(
                [over_components(gate[0:ATOMS, :], degree), over_components(gate[ATOMS:, :], degree)],
                axis=0,
            )
            mixed_grad = grads * spread_gate
            product = grads * mixed
            totals = []
            for side in range(2):
                total = product[side * size : side * size + ATOMS, :]
                for comp in range(1, 2 * degree + 1):
                    begin = side * size + comp * ATOMS
                    total = total + product[begin : begin + ATOMS, :]
                totals.append(total)
            total = jnp.concatenate(totals, axis=0)
            pre = (total * gate * (1.0 - gate)).astype(BF16)
            start = (DEGREES + degree - 1) * CHANS
            payload_ref[start : start + CHANS, :] = along_first(scalar, pre).astype(BF16)
        payload_ref[degree * CHANS : (degree + 1) * CHANS, :] = along_first(
            rows, mixed_grad.astype(BF16)
        ).astype(BF16)
    base = (2 * DEGREES - 1) * CHANS
    payload_ref[base : base + CHANS + 16, :] = head_ref[...].astype(BF16)
    base += CHANS + 16
    payload_ref[base : base + 48, :] = jnp.concatenate(
        radial_grads + [embed_grad], axis=0
    ).astype(BF16)
    base += 48
    slabs = (PAYLOAD - base) // 3
    here = lax.broadcasted_iota(jnp.int32, (slabs, PROBES), 0) == own_slab()
    for part in parts_of(jnp.where(here, density_ref[...], 0.0)):
        payload_ref[base : base + slabs, :] = part
        base += slabs


def unpack_kernel(
    payload_ref, loss_ref, density_ref, deg_ref, gate_ref, embed_ref, radial_ref, hidden_ref,
    bias_ref, out_ref,
):
    for degree in range(DEGREES):
        deg_ref[degree] = payload_ref[lanes(degree), :].astype(F32)
    for degree in range(1, DEGREES):
        gate_ref[:, lanes(degree - 1)] = payload_ref[lanes(DEGREES + degree - 1), :].astype(F32)
    base = (2 * DEGREES - 1) * CHANS
    hidden_ref[...] = payload_ref[base : base + CHANS, :].astype(F32)
    base += CHANS
    misc = payload_ref[base : base + 16, :].astype(F32)
    bias_ref[...] = misc[0:1, :]
    out_ref[...] = misc[1:2, :]
    loss_ref[...] = jnp.sum(misc[2:3, :], axis=1, keepdims=True)
    base += 16
    small = payload_ref[base : base + 48, :].astype(F32)
    for degree in range(DEGREES):
        radial_ref[:, lanes(degree)] = small[degree * BASES : (degree + 1) * BASES, :]
    embed_ref[...] = small[DEGREES * BASES :, :]
    base += 48
    slabs = (PAYLOAD - base) // 3
    total = None
    for _ in range(3):
        part = payload_ref[base : base + slabs, :].astype(F32)
        total = part if total is None else total + part
        base += slabs
    here = lax.broadcasted_iota(jnp.int32, (slabs, PROBES), 0) == own_slab()
    density_ref[...] = jnp.sum(jnp.where(here, total, 0.0), axis=0, keepdims=True)


def shape(dims, dtype=F32):
    return jax.ShapeDtypeStruct(dims, dtype)


def call(kernel, outs, name, limit=32, **options):
    return pl.pallas_call(
        kernel,
        out_shape=outs,
        name=name,
        compiler_params=pltpu.CompilerParams(vmem_limit_bytes=limit * 1024 * 1024),
        **options,
    )


def to_partner(block):
    count = lax.axis_size(SLAB)
    route = [(i, (i + (ROWS if i % ROWS >= HALO else -ROWS)) % count) for i in range(count)]
    return lax.ppermute(block, SLAB, route)


def reduce_all(payload):
    count, depth = lax.axis_size(NEAR), lax.axis_size("zh")
    rows = PAYLOAD // count
    parts = lax.all_to_all(payload.reshape(count, rows, CHANS), NEAR, 0, 0)
    copies = call(sum_kernel, shape((depth, rows, CHANS), BF16), "sum_near")(parts)
    parts = lax.all_to_all(copies, "zh", 0, 0)
    copies = call(sum_kernel, shape((count, rows, CHANS), BF16), "sum_depth")(parts)
    return lax.all_to_all(copies, NEAR, 0, 0).reshape(PAYLOAD, CHANS)


def on_device(
    atom_feats, species, send_rows, neighbours, harmonics, distances, target,
    w_deg, w_gate, embed, w_radial, w_hidden, b_hidden, w_out,
):
    slab_count = lax.axis_size(SLAB)
    shards = lax.axis_size(ATOM)
    chunk = PROBES // shards
    scale = 1.0 / math.sqrt(PROBES * slab_count)
    species = species.reshape(1, ATOMS)
    lists = send_rows[0, 0]
    far = pl.BlockSpec(memory_space=pl.ANY)
    field_shape = (FIELDS, SLOTS, PROBES)
    with jax.named_scope("exchange_atoms"):
        theirs = to_partner(atom_feats)
    rows_of = [row.reshape(1, CHANS) for row in (b_hidden, w_out, target)]
    operands = (
        harmonics, distances, neighbours, lists, species, w_radial, embed, w_hidden, *rows_of
    )
    held = [
        shape((ROWS,) + field_shape),
        shape((8, CHANS)),
        shape((SMALL_ROWS, CHANS)),
    ]
    copies, ints, small = call(
        pack_kernel,
        held,
        "pack",
        limit=63,
        in_specs=[far] * len(operands),
        out_specs=[far] * len(held),
        scratch_shapes=[
            pltpu.VMEM(field_shape, F32),
            pltpu.VMEM(held[2].shape, F32),
            pltpu.VMEM((SLOTS, PROBES), jnp.int32),
            pltpu.VMEM(lists.shape, jnp.int32),
            pltpu.VMEM(species.shape, jnp.int32),
        ]
        + [pltpu.VMEM((1, CHANS), F32)] * 3
        + [
            pltpu.SemaphoreType.DMA((len(operands) - 1 + DEGREES,)),
            pltpu.SemaphoreType.DMA((2 + ROWS,)),
        ],
    )(*operands)
    with jax.named_scope("exchange_lists"):
        their_ints = to_partner(ints)
    with jax.named_scope("gather_pairs"):
        packs = lax.all_to_all(copies, "y", 0, 0)
    mixed_shapes = [shape((COMPS * ATOMS, CHANS)), shape((ATOMS, (DEGREES - 1) * CHANS))]
    tables = [
        pltpu.VMEM((COMPS * ATOMS, CHANS), BF16),
        pltpu.VMEM((1 + len(OFFSETS), ATOMS, ATOMS), BF16),
    ]
    operands = (atom_feats, w_deg, w_gate, small)
    feats, *weights = call(
        stage_kernel, [shape(operand.shape, operand.dtype) for operand in operands], "stage"
    )(*operands)
    (
        values, spread, halo, sums, radial, own_ints, consts,
        mixed, gates, their_mixed, their_gates,
    ) = call(
        pair_kernel,
        [
            shape((ROWS, shards, chunk, CHANS)),
            shape((COMPS * ATOMS, OWN_PAIRS), BF16),
            shape((COMPS * ATOMS, HALO_PAIRS), BF16),
            shape((DEGREES * CHANS + 2 * BASES, PAIRS), BF16),
            shape((DEGREES * CHANS, PAIRS)),
            shape(ints.shape),
            shape((SMALL_ROWS - CONST_ROW, CHANS)),
        ]
        + mixed_shapes * 2,
        "pair_sums",
        scratch_shapes=tables * 2 + [pltpu.VMEM(embed.shape, F32)],
    )(packs, theirs, their_ints, feats, *weights)
    with jax.named_scope("scatter_sums"):
        parts = lax.all_to_all(values.reshape(ROWS * shards, chunk, CHANS), PLANE, 0, 0)
    up, head, density_row = call(
        functools.partial(readout_kernel, scale),
        [
            shape((ROWS * shards, chunk, CHANS)),
            shape((CHANS + 16, CHANS)),
            shape((1, PROBES)),
        ],
        "readout",
        scratch_shapes=[pltpu.VMEM((PROBES, PROBES), F32)],
    )(parts, consts)
    with jax.named_scope("gather_grads"):
        ups = lax.all_to_all(up, PLANE, 0, 0).reshape(ROWS, shards, chunk, CHANS)
    operands = (
        feats, theirs, own_ints, their_ints, mixed, their_mixed, gates, their_gates, radial,
        head, density_row, ups, sums, spread, halo,
    )
    payload = call(backward_kernel, shape((PAYLOAD, CHANS), BF16), "backward")(*operands)
    with jax.named_scope("reduce_grads"):
        payload = reduce_all(payload)
    loss, density, deg, gate, embed_grad, radial_grad, hidden, bias, out = call(
        unpack_kernel,
        [
            shape((1, 1)),
            shape((1, PROBES)),
            shape((DEGREES, CHANS, CHANS)),
            shape((CHANS, (DEGREES - 1) * CHANS)),
            shape((KINDS, CHANS)),
            shape((BASES, DEGREES * CHANS)),
            shape((CHANS, CHANS)),
            shape((1, CHANS)),
            shape((1, CHANS)),
        ],
        "unpack",
    )(payload)
    return (
        loss.reshape(()), density.reshape(PROBES), deg, gate, embed_grad, radial_grad, hidden,
        bias.reshape(CHANS), out.reshape(CHANS),
    )


def solution(mesh):
    slabs, shards = mesh.devices.shape
    fine = mesh.devices.reshape(slabs // 8, 2, 4, shards // 2, 2)
    fine = Mesh(fine, ("zh", "zl", "y", "x", "c"))
    in_specs = (
        P(SLAB + ATOM, None),
        P(SLAB + ATOM),
        P(SLAB, ATOM, None, None),
        P(ATOM, SLAB),
        P(None, ATOM, SLAB),
        P(ATOM, SLAB),
        P(SLAB),
        P(),
        P(),
        P(),
        P(),
        P(),
        P(),
        P(),
    )
    out_specs = (P(), P(SLAB), P(), P(), P(), P(), P(), P(), P())
    return jax.shard_map(
        on_device, mesh=fine, in_specs=in_specs, out_specs=out_specs, check_vma=False
    )
```

```python
import functools
import math

import jax
import jax.numpy as jnp
from jax import lax
from jax.experimental import pallas as pl
from jax.experimental.pallas import tpu as pltpu
from jax.sharding import Mesh, PartitionSpec as P

OFFSETS = (-2, -1, 1, 2)
CUTOFF = 4.0
PRECISE = lax.Precision.HIGHEST
F32 = jnp.float32
BF16 = jnp.bfloat16
SLAB = ("zh", "zl", "y")
ATOM = ("x", "c")
PLANE = ("y", "x", "c")
NEAR = ("zl", "y", "x", "c")
DEGREES = 5
COMPS = DEGREES * DEGREES
CHANS = 128
ATOMS = 64
SLOTS = 2
PROBES = 128
SPAN = SLOTS * PROBES
ROWS = 4
HALO = 2
OWN_PAIRS = ROWS * SPAN
HALO_PAIRS = HALO * SPAN
PAIRS = OWN_PAIRS + HALO_PAIRS
FIELDS = 32
BASES = 8
KINDS = 8
PAYLOAD = 1536
EMBED_ROW = DEGREES * BASES
INTS_ROW = EMBED_ROW + KINDS
CONST_ROW = INTS_ROW + 8
SMALL_ROWS = CONST_ROW + 8 + CHANS


def first_rows(degree):
    return degree * degree * ATOMS, (degree + 1) * (degree + 1) * ATOMS


def lanes(block):
    return slice(block * CHANS, (block + 1) * CHANS)


def along_first(left, right, precision=None):
    return lax.dot_general(
        left, right, (((0,), (0,)), ((), ())), preferred_element_type=F32, precision=precision
    )


def along_last(left, right, precision=None):
    return lax.dot_general(
        left, right, (((1,), (1,)), ((), ())), preferred_element_type=F32, precision=precision
    )


def matmul(left, right, precision=None):
    return jnp.dot(left, right, preferred_element_type=F32, precision=precision)


def component_rows(feats_ref, degree):
    parts = [feats_ref[:, lanes(m)] for m in range(degree * degree, (degree + 1) * (degree + 1))]
    return parts[0] if degree == 0 else jnp.concatenate(parts, axis=0)


def over_components(gate, degree):
    return jnp.concatenate([gate] * (2 * degree + 1), axis=0)


def kind_rows(species):
    ids = lax.broadcasted_iota(jnp.int32, (KINDS, ATOMS), 0).astype(F32)
    return (ids == species).astype(F32)


def owner_tables(lists, owners_ref):
    ids = lax.broadcasted_iota(jnp.int32, (ATOMS, ATOMS), 0).astype(F32)
    same = lax.broadcasted_iota(jnp.int32, (ATOMS, ATOMS), 1).astype(F32)
    for index in range(1 + len(OFFSETS)):
        row = same if index == 2 else lists[index - (index > 2)]
        owners_ref[index] = (ids == row).astype(BF16)


def started(pairs, sems):
    copies = [
        pltpu.make_async_copy(source, target, sems.at[index])
        for index, (source, target) in enumerate(pairs)
    ]
    for copy in copies:
        copy.start()
    return copies


def encode_rows(
    feats_ref, species, w_deg_ref, w_gate_ref, embed_ref, rows_ref, mixed_ref, gates_ref
):
    scalar = feats_ref[:, lanes(0)]
    gates = jax.nn.sigmoid(matmul(scalar, w_gate_ref[...]))
    gates_ref[...] = gates
    for degree in range(DEGREES):
        low, high = first_rows(degree)
        rows = component_rows(feats_ref, degree)
        mixed = matmul(rows, w_deg_ref[degree])
        mixed_ref[low:high, :] = mixed
        if degree == 0:
            added = jax.nn.silu(mixed) + along_first(
                kind_rows(species), embed_ref[...], PRECISE
            )
        else:
            added = mixed * over_components(gates[:, lanes(degree - 1)], degree)
        rows_ref[low:high, :] = (rows.astype(F32) + added).astype(BF16)


def lists_of(ints_ref):
    count = len(OFFSETS)
    lists = [ints_ref[which : which + 1, 0:ATOMS] for which in range(count)]
    return lists, ints_ref[count : count + 1, 0:ATOMS]


def parts_of(values):
    high = values.astype(BF16)
    rest = values - high.astype(F32)
    middle = rest.astype(BF16)
    low = (rest - middle.astype(F32)).astype(BF16)
    return high, middle, low


def halves(values, axis):
    return jnp.concatenate(parts_of(values)[0:2], axis=axis)


def folded(values):
    return values[:, 0:CHANS] + values[:, CHANS:]


def stacked(values, order):
    parts = [part.astype(F32) for part in parts_of(values)]
    return jnp.concatenate([parts[index] for index in order], axis=0).astype(BF16)


def pack_kernel(
    harm_hbm, dist_hbm, nbr_hbm, lists_hbm, species_hbm, w_radial_hbm, embed_hbm, w_hidden_hbm,
    b_hidden_hbm, w_out_hbm, target_hbm, copies_hbm, ints_hbm, small_hbm,
    pack_ref, small_ref, nbr_ref, lists_ref, species_ref, b_hidden_ref, w_out_ref, target_ref,
    sems, out_sems,
):
    copies = started(
        [
            (harm_hbm, pack_ref.at[pl.ds(0, COMPS)]),
            (dist_hbm, pack_ref.at[COMPS]),
            (nbr_hbm, nbr_ref),
            (lists_hbm, lists_ref),
            (species_hbm, species_ref),
            (embed_hbm, small_ref.at[pl.ds(EMBED_ROW, KINDS)]),
            (w_hidden_hbm, small_ref.at[pl.ds(CONST_ROW + 8, CHANS)]),
            (b_hidden_hbm, b_hidden_ref),
            (w_out_hbm, w_out_ref),
            (target_hbm, target_ref),
        ]
        + [
            (
                w_radial_hbm.at[:, pl.ds(degree * CHANS, CHANS)],
                small_ref.at[pl.ds(degree * BASES, BASES)],
            )
            for degree in range(DEGREES)
        ],
        sems,
    )
    pack_ref[COMPS + 2 :] = jnp.zeros((FIELDS - COMPS - 2, SLOTS, PROBES), F32)
    small_ref[INTS_ROW : CONST_ROW + 8, :] = jnp.zeros((16, CHANS), F32)
    for copy in copies:
        copy.wait()
    count = len(OFFSETS)
    small_ref[INTS_ROW : INTS_ROW + count, 0:ATOMS] = lists_ref[...].astype(F32)
    small_ref[INTS_ROW + count : INTS_ROW + count + 1, 0:ATOMS] = species_ref[...].astype(F32)
    small_ref[CONST_ROW : CONST_ROW + 3, :] = jnp.concatenate(
        [b_hidden_ref[...], w_out_ref[...], target_ref[...]], axis=0
    )
    pack_ref[COMPS + 1] = nbr_ref[...].astype(F32)
    writes = started(
        [(small_ref.at[pl.ds(INTS_ROW, 8)], ints_hbm), (small_ref, small_hbm)]
        + [(pack_ref, copies_hbm.at[row]) for row in range(ROWS)],
        out_sems,
    )
    for write in writes:
        write.wait()


def stage_kernel(*refs):
    half = len(refs) // 2
    for source, target in zip(refs[:half], refs[half:]):
        target[...] = source[...]


def plane_halves():
    row = lax.axis_index("y")
    upper = jnp.where(row > 1, 1, 0)
    return row, HALO - HALO * upper, row + ROWS - 2 * ROWS * upper


def pair_kernel(
    packs_ref, theirs_ref, their_ints_ref, feats_ref, w_deg_ref, w_gate_ref, small_ref,
    out_ref, spread_ref, halo_ref, sums_ref, radial_ref, ints_ref, const_ref,
    mixed_ref, gates_ref, their_mixed_ref, their_gates_ref,
    rows_ref, owners_ref, their_rows_ref, their_owners_ref, embed_ref, values_ref,
):
    embed_ref[...] = small_ref[EMBED_ROW:INTS_ROW, :]
    ints_ref[...] = small_ref[INTS_ROW:CONST_ROW, :]
    const_ref[...] = small_ref[CONST_ROW:, :]
    w_radial = jnp.concatenate(
        [small_ref[degree * BASES : (degree + 1) * BASES, :] for degree in range(DEGREES)], axis=1
    )
    radial_split = stacked(w_radial, (0, 0, 1, 1, 0, 2))
    lists, species = lists_of(ints_ref)
    owner_tables(lists, owners_ref)
    encode_rows(
        feats_ref, species, w_deg_ref, w_gate_ref, embed_ref, rows_ref, mixed_ref, gates_ref
    )
    shards, chunk = out_ref.shape[1], out_ref.shape[2]
    own_row, first, partner_row = plane_halves()
    sub = lax.broadcasted_iota(jnp.int32, (ATOMS, PROBES), 0).astype(F32)

    def spread_pairs(target_ref, tables_ref, begin, probe_row, atom_row):
        delta = probe_row - atom_row
        valid = jnp.logical_and(delta >= -2, delta <= 2)
        table = jnp.clip(delta + 2, 0, 4)
        block = jnp.where(delta < 0, delta + 3, jnp.where(delta > 0, delta + 2, 0))
        base = jnp.where(valid, block * ATOMS, 1 << 20).astype(F32)
        for slot in range(SLOTS):
            start = begin + slot * PROBES

            def row(field):
                return packs_ref[probe_row, field, slot : slot + 1, :]

            hot = (row(COMPS + 1) - base == sub).astype(BF16)
            hot = matmul(tables_ref[table], hot)
            for m in range(COMPS):
                target_ref[m * ATOMS : (m + 1) * ATOMS, start : start + PROBES] = (
                    hot * row(m)
                ).astype(BF16)

    for row in range(ROWS):
        spread_pairs(spread_ref, owners_ref, row * SPAN, row, own_row)
    their_lists, their_species = lists_of(their_ints_ref)
    owner_tables(their_lists, their_owners_ref)
    encode_rows(
        theirs_ref, their_species, w_deg_ref, w_gate_ref, embed_ref, their_rows_ref,
        their_mixed_ref, their_gates_ref,
    )
    for row in range(HALO):
        spread_pairs(halo_ref, their_owners_ref, row * SPAN, first + row, partner_row)
    dists = [packs_ref[row, COMPS, slot : slot + 1, :] for row in range(ROWS) for slot in range(SLOTS)]
    dists += [
        packs_ref[first + row, COMPS, slot : slot + 1, :]
        for row in range(HALO)
        for slot in range(SLOTS)
    ]
    dist = jnp.concatenate(dists, axis=1)
    orders = lax.broadcasted_iota(jnp.int32, (BASES, PAIRS), 0).astype(F32) + 1.0
    phase = math.pi * dist / CUTOFF
    envelope = 0.5 * (jnp.cos(phase) + 1.0) / dist
    basis_split = stacked(jnp.sin(phase * orders) * envelope, (0, 1, 0, 1, 2, 0))
    sums_ref[DEGREES * CHANS :, :] = basis_split[0 : 2 * BASES, :]
    total = None
    for degree in range(DEGREES):
        low, high = first_rows(degree)
        radial = along_first(radial_split[:, lanes(degree)], basis_split)
        radial_ref[lanes(degree), :] = radial
        sums = jnp.concatenate(
            [
                along_first(rows_ref[low:high, :], spread_ref[low:high, :]),
                along_first(their_rows_ref[low:high, :], halo_ref[low:high, :]),
            ],
            axis=1,
        )
        sums_ref[lanes(degree), :] = sums.astype(BF16)
        term = radial * sums
        total = term if total is None else total + term

    def value_of(block):
        start = block * SPAN
        both = total[:, start : start + PROBES] + total[:, start + PROBES : start + SPAN]
        return both.T

    for row in range(ROWS):
        values_ref[row] = value_of(row)
    for row in range(HALO):
        values_ref[first + row] += value_of(ROWS + row)
    for row in range(ROWS):
        for shard in range(shards):
            part = values_ref[row, shard * chunk : (shard + 1) * chunk, :]
            out_ref[row, shard] = part.astype(BF16)


def silu_slope(values):
    logistic = jax.nn.sigmoid(values)
    return logistic * (1.0 + values * (1.0 - logistic))


def sum_kernel(parts_ref, out_ref):
    total = parts_ref[0].astype(F32)
    for index in range(1, parts_ref.shape[0]):
        total = total + parts_ref[index].astype(F32)
    if len(out_ref.shape) == len(parts_ref.shape):
        for copy in range(out_ref.shape[0]):
            out_ref[copy] = total.astype(out_ref.dtype)
    else:
        out_ref[...] = total.astype(out_ref.dtype)


def readout_kernel(
    scale, parts_ref, const_ref, up_ref, head_ref, density_ref, column_ref
):
    chunk = parts_ref.shape[1]
    shard = lax.axis_index("x") * lax.axis_size("c") + lax.axis_index("c")
    start = pl.multiple_of(shard * chunk, chunk)
    column_ref[...] = jnp.broadcast_to(const_ref[2:3, :], (PROBES, PROBES)).T
    target = column_ref[pl.ds(start, chunk), :]
    summed = parts_ref[0].astype(F32)
    for index in range(1, parts_ref.shape[0]):
        summed = summed + parts_ref[index].astype(F32)
    w_hidden = const_ref[8:, :]
    w_out = const_ref[1:2, :]
    hidden_pre = matmul(summed, w_hidden, PRECISE) + const_ref[0:1, :]
    activated = jax.nn.silu(hidden_pre)
    density = jnp.sum(activated * w_out, axis=1, keepdims=True)
    error = density - target
    error_grad = error * scale
    pre_grad = w_out * silu_slope(hidden_pre) * error_grad
    spot = lax.broadcasted_iota(jnp.int32, (chunk, PROBES), 0) + start
    mask = (spot == lax.broadcasted_iota(jnp.int32, (chunk, PROBES), 1)).astype(F32)
    upstream = along_last(pre_grad, w_hidden, PRECISE)
    for copy in range(up_ref.shape[0]):
        up_ref[copy] = upstream.astype(BF16)
    density_ref[...] = jnp.sum(mask * density, axis=0, keepdims=True)
    head_ref[0:CHANS, :] = along_first(summed, pre_grad, PRECISE)
    bias = jnp.sum(pre_grad, axis=0, keepdims=True)
    out = jnp.sum(activated * error_grad, axis=0, keepdims=True)
    loss = jnp.sum(mask * error * error * (0.5 * scale), axis=0, keepdims=True)
    head_ref[CHANS : CHANS + 16, :] = jnp.concatenate(
        [bias, out, loss, jnp.zeros((13, CHANS), F32)], axis=0
    )


def own_slab():
    depth = lax.axis_index("zh") * lax.axis_size("zl") + lax.axis_index("zl")
    return depth * ROWS + lax.axis_index("y")


def backward_kernel(
    atoms_ref, theirs_ref, ints_ref, their_ints_ref, mixed_ref, their_mixed_ref, gates_ref, their_gates_ref,
    radial_ref, head_ref, density_ref, up_ref, sums_ref, spread_ref, halo_ref, payload_ref,
):
    shards = up_ref.shape[1]
    first = plane_halves()[1]

    def block_of(row):
        parts = [up_ref[row, shard].astype(F32) for shard in range(shards)]
        return [jnp.concatenate(parts, axis=0).T] * SLOTS

    blocks = []
    for row in list(range(ROWS)) + [first + row for row in range(HALO)]:
        blocks += block_of(row)
    upstream = jnp.concatenate(blocks, axis=1)
    scalar = jnp.concatenate([atoms_ref[:, lanes(0)], theirs_ref[:, lanes(0)]], axis=0)
    gates = jnp.concatenate([gates_ref[...], their_gates_ref[...]], axis=0)
    kinds = jnp.concatenate(
        [kind_rows(lists_of(ref)[1]) for ref in (ints_ref, their_ints_ref)], axis=1
    )
    basis_split = sums_ref[DEGREES * CHANS :, :]
    radial_grads = []
    for degree in range(DEGREES):
        low, high = first_rows(degree)
        size = high - low
        inner = halves(radial_ref[lanes(degree), :] * upstream, 0)
        grads = jnp.concatenate(
            [
                folded(along_last(spread_ref[low:high, :], inner[:, 0:OWN_PAIRS])),
                folded(along_last(halo_ref[low:high, :], inner[:, OWN_PAIRS:])),
            ],
            axis=0,
        )
        product = (sums_ref[lanes(degree), :].astype(F32) * upstream).astype(BF16)
        both = along_last(product, basis_split)
        radial_grads.append((both[:, 0:BASES] + both[:, BASES : 2 * BASES]).T)
        rows = jnp.concatenate(
            [component_rows(atoms_ref, degree), component_rows(theirs_ref, degree)], axis=0
        )
        mixed = jnp.concatenate([mixed_ref[low:high, :], their_mixed_ref[low:high, :]], axis=0)
        if degree == 0:
            mixed_grad = grads * silu_slope(mixed)
            embed_grad = matmul(kinds, grads, PRECISE)
        else:
            gate = gates[:, lanes(degree - 1)]
            spread_gate = jnp.concatenate(
                [over_components(gate[0:ATOMS, :], degree), over_components(gate[ATOMS:, :], degree)],
                axis=0,
            )
            mixed_grad = grads * spread_gate
            product = grads * mixed
            totals = []
            for side in range(2):
                total = product[side * size : side * size + ATOMS, :]
                for comp in range(1, 2 * degree + 1):
                    begin = side * size + comp * ATOMS
                    total = total + product[begin : begin + ATOMS, :]
                totals.append(total)
            total = jnp.concatenate(totals, axis=0)
            pre = halves(total * gate * (1.0 - gate), 1)
            start = (DEGREES + degree - 1) * CHANS
            payload_ref[start : start + CHANS, :] = folded(along_first(scalar, pre)).astype(BF16)
        payload_ref[degree * CHANS : (degree + 1) * CHANS, :] = folded(
            along_first(rows, halves(mixed_grad, 1))
        ).astype(BF16)
    base = (2 * DEGREES - 1) * CHANS
    payload_ref[base : base + CHANS + 16, :] = head_ref[...].astype(BF16)
    base += CHANS + 16
    payload_ref[base : base + 48, :] = jnp.concatenate(
        radial_grads + [embed_grad], axis=0
    ).astype(BF16)
    base += 48
    slabs = (PAYLOAD - base) // 3
    here = lax.broadcasted_iota(jnp.int32, (slabs, PROBES), 0) == own_slab()
    for part in parts_of(jnp.where(here, density_ref[...], 0.0)):
        payload_ref[base : base + slabs, :] = part
        base += slabs


def unpack_kernel(
    payload_ref, loss_ref, density_ref, deg_ref, gate_ref, embed_ref, radial_ref, hidden_ref,
    bias_ref, out_ref,
):
    for degree in range(DEGREES):
        deg_ref[degree] = payload_ref[lanes(degree), :].astype(F32)
    for degree in range(1, DEGREES):
        gate_ref[:, lanes(degree - 1)] = payload_ref[lanes(DEGREES + degree - 1), :].astype(F32)
    base = (2 * DEGREES - 1) * CHANS
    hidden_ref[...] = payload_ref[base : base + CHANS, :].astype(F32)
    base += CHANS
    misc = payload_ref[base : base + 16, :].astype(F32)
    bias_ref[...] = misc[0:1, :]
    out_ref[...] = misc[1:2, :]
    loss_ref[...] = jnp.sum(misc[2:3, :], axis=1, keepdims=True)
    base += 16
    small = payload_ref[base : base + 48, :].astype(F32)
    for degree in range(DEGREES):
        radial_ref[:, lanes(degree)] = small[degree * BASES : (degree + 1) * BASES, :]
    embed_ref[...] = small[DEGREES * BASES :, :]
    base += 48
    slabs = (PAYLOAD - base) // 3
    total = None
    for _ in range(3):
        part = payload_ref[base : base + slabs, :].astype(F32)
        total = part if total is None else total + part
        base += slabs
    here = lax.broadcasted_iota(jnp.int32, (slabs, PROBES), 0) == own_slab()
    density_ref[...] = jnp.sum(jnp.where(here, total, 0.0), axis=0, keepdims=True)


def shape(dims, dtype=F32):
    return jax.ShapeDtypeStruct(dims, dtype)


def call(kernel, outs, name, limit=32, **options):
    return pl.pallas_call(
        kernel,
        out_shape=outs,
        name=name,
        compiler_params=pltpu.CompilerParams(vmem_limit_bytes=limit * 1024 * 1024),
        **options,
    )


def to_partner(block):
    count = lax.axis_size(SLAB)
    route = [(i, (i + (ROWS if i % ROWS >= HALO else -ROWS)) % count) for i in range(count)]
    return lax.ppermute(block, SLAB, route)


def reduce_all(payload):
    count, depth = lax.axis_size(NEAR), lax.axis_size("zh")
    rows = PAYLOAD // count
    parts = lax.all_to_all(payload.reshape(count, rows, CHANS), NEAR, 0, 0)
    copies = call(sum_kernel, shape((depth, rows, CHANS), BF16), "sum_near")(parts)
    parts = lax.all_to_all(copies, "zh", 0, 0)
    copies = call(sum_kernel, shape((count, rows, CHANS), BF16), "sum_depth")(parts)
    return lax.all_to_all(copies, NEAR, 0, 0).reshape(PAYLOAD, CHANS)


def on_device(
    atom_feats, species, send_rows, neighbours, harmonics, distances, target,
    w_deg, w_gate, embed, w_radial, w_hidden, b_hidden, w_out,
):
    slab_count = lax.axis_size(SLAB)
    shards = lax.axis_size(ATOM)
    chunk = PROBES // shards
    scale = 1.0 / math.sqrt(PROBES * slab_count)
    species = species.reshape(1, ATOMS)
    lists = send_rows[0, 0]
    far = pl.BlockSpec(memory_space=pl.ANY)
    field_shape = (FIELDS, SLOTS, PROBES)
    with jax.named_scope("exchange_atoms"):
        theirs = to_partner(atom_feats)
    rows_of = [row.reshape(1, CHANS) for row in (b_hidden, w_out, target)]
    operands = (
        harmonics, distances, neighbours, lists, species, w_radial, embed, w_hidden, *rows_of
    )
    held = [
        shape((ROWS,) + field_shape),
        shape((8, CHANS)),
        shape((SMALL_ROWS, CHANS)),
    ]
    copies, ints, small = call(
        pack_kernel,
        held,
        "pack",
        limit=63,
        in_specs=[far] * len(operands),
        out_specs=[far] * len(held),
        scratch_shapes=[
            pltpu.VMEM(field_shape, F32),
            pltpu.VMEM(held[2].shape, F32),
            pltpu.VMEM((SLOTS, PROBES), jnp.int32),
            pltpu.VMEM(lists.shape, jnp.int32),
            pltpu.VMEM(species.shape, jnp.int32),
        ]
        + [pltpu.VMEM((1, CHANS), F32)] * 3
        + [
            pltpu.SemaphoreType.DMA((len(operands) - 1 + DEGREES,)),
            pltpu.SemaphoreType.DMA((2 + ROWS,)),
        ],
    )(*operands)
    with jax.named_scope("exchange_lists"):
        their_ints = to_partner(ints)
    with jax.named_scope("gather_pairs"):
        packs = lax.all_to_all(copies, "y", 0, 0)
    mixed_shapes = [shape((COMPS * ATOMS, CHANS)), shape((ATOMS, (DEGREES - 1) * CHANS))]
    tables = [
        pltpu.VMEM((COMPS * ATOMS, CHANS), BF16),
        pltpu.VMEM((1 + len(OFFSETS), ATOMS, ATOMS), BF16),
    ]
    operands = (atom_feats, w_deg, w_gate, small)
    feats, *weights = call(
        stage_kernel, [shape(operand.shape, operand.dtype) for operand in operands], "stage"
    )(*operands)
    (
        values, spread, halo, sums, radial, own_ints, consts,
        mixed, gates, their_mixed, their_gates,
    ) = call(
        pair_kernel,
        [
            shape((ROWS, shards, chunk, CHANS), BF16),
            shape((COMPS * ATOMS, OWN_PAIRS), BF16),
            shape((COMPS * ATOMS, HALO_PAIRS), BF16),
            shape((DEGREES * CHANS + 2 * BASES, PAIRS), BF16),
            shape((DEGREES * CHANS, PAIRS)),
            shape(ints.shape),
            shape((SMALL_ROWS - CONST_ROW, CHANS)),
        ]
        + mixed_shapes * 2,
        "pair_sums",
        scratch_shapes=tables * 2
        + [pltpu.VMEM(embed.shape, F32), pltpu.VMEM((ROWS, PROBES, CHANS), F32)],
    )(packs, theirs, their_ints, feats, *weights)
    with jax.named_scope("scatter_sums"):
        parts = lax.all_to_all(values.reshape(ROWS * shards, chunk, CHANS), PLANE, 0, 0)
    up, head, density_row = call(
        functools.partial(readout_kernel, scale),
        [
            shape((ROWS * shards, chunk, CHANS), BF16),
            shape((CHANS + 16, CHANS)),
            shape((1, PROBES)),
        ],
        "readout",
        scratch_shapes=[pltpu.VMEM((PROBES, PROBES), F32)],
    )(parts, consts)
    with jax.named_scope("gather_grads"):
        ups = lax.all_to_all(up, PLANE, 0, 0).reshape(ROWS, shards, chunk, CHANS)
    operands = (
        feats, theirs, own_ints, their_ints, mixed, their_mixed, gates, their_gates, radial,
        head, density_row, ups, sums, spread, halo,
    )
    payload = call(backward_kernel, shape((PAYLOAD, CHANS), BF16), "backward")(*operands)
    with jax.named_scope("reduce_grads"):
        payload = reduce_all(payload)
    loss, density, deg, gate, embed_grad, radial_grad, hidden, bias, out = call(
        unpack_kernel,
        [
            shape((1, 1)),
            shape((1, PROBES)),
            shape((DEGREES, CHANS, CHANS)),
            shape((CHANS, (DEGREES - 1) * CHANS)),
            shape((KINDS, CHANS)),
            shape((BASES, DEGREES * CHANS)),
            shape((CHANS, CHANS)),
            shape((1, CHANS)),
            shape((1, CHANS)),
        ],
        "unpack",
    )(payload)
    return (
        loss.reshape(()), density.reshape(PROBES), deg, gate, embed_grad, radial_grad, hidden,
        bias.reshape(CHANS), out.reshape(CHANS),
    )


def solution(mesh):
    slabs, shards = mesh.devices.shape
    fine = mesh.devices.reshape(slabs // 8, 2, 4, shards // 2, 2)
    fine = Mesh(fine, ("zh", "zl", "y", "x", "c"))
    in_specs = (
        P(SLAB + ATOM, None),
        P(SLAB + ATOM),
        P(SLAB, ATOM, None, None),
        P(ATOM, SLAB),
        P(None, ATOM, SLAB),
        P(ATOM, SLAB),
        P(SLAB),
        P(),
        P(),
        P(),
        P(),
        P(),
        P(),
        P(),
    )
    out_specs = (P(), P(SLAB), P(), P(), P(), P(), P(), P(), P())
    return jax.shard_map(
        on_device, mesh=fine, in_specs=in_specs, out_specs=out_specs, check_vma=False
    )
```

```python
import functools
import math

import jax
import jax.numpy as jnp
from jax import lax
from jax.experimental import pallas as pl
from jax.experimental.pallas import tpu as pltpu
from jax.sharding import Mesh, PartitionSpec as P

OFFSETS = (-2, -1, 1, 2)
CUTOFF = 4.0
PRECISE = lax.Precision.HIGHEST
F32 = jnp.float32
BF16 = jnp.bfloat16
SLAB = ("zh", "zl", "y")
ATOM = ("x", "c")
PLANE = ("y", "x", "c")
NEAR = ("zl", "y", "x", "c")
DEGREES = 5
COMPS = DEGREES * DEGREES
CHANS = 128
ATOMS = 64
SLOTS = 2
PROBES = 128
SPAN = SLOTS * PROBES
ROWS = 4
HALO = 2
OWN_PAIRS = ROWS * SPAN
HALO_PAIRS = HALO * SPAN
PAIRS = OWN_PAIRS + HALO_PAIRS
FIELDS = 32
BASES = 8
KINDS = 8
PAYLOAD = 1536
EMBED_ROW = DEGREES * BASES
INTS_ROW = EMBED_ROW + KINDS
CONST_ROW = INTS_ROW + 8
SMALL_ROWS = CONST_ROW + 8 + CHANS


def first_rows(degree):
    return degree * degree * ATOMS, (degree + 1) * (degree + 1) * ATOMS


def lanes(block):
    return slice(block * CHANS, (block + 1) * CHANS)


def along_first(left, right, precision=None):
    return lax.dot_general(
        left, right, (((0,), (0,)), ((), ())), preferred_element_type=F32, precision=precision
    )


def along_last(left, right, precision=None):
    return lax.dot_general(
        left, right, (((1,), (1,)), ((), ())), preferred_element_type=F32, precision=precision
    )


def matmul(left, right, precision=None):
    return jnp.dot(left, right, preferred_element_type=F32, precision=precision)


def component_rows(feats_ref, degree):
    parts = [feats_ref[:, lanes(m)] for m in range(degree * degree, (degree + 1) * (degree + 1))]
    return parts[0] if degree == 0 else jnp.concatenate(parts, axis=0)


def over_components(gate, degree):
    return jnp.concatenate([gate] * (2 * degree + 1), axis=0)


def kind_rows(species):
    ids = lax.broadcasted_iota(jnp.int32, (KINDS, ATOMS), 0).astype(F32)
    return (ids == species).astype(F32)


def owner_tables(lists, owners_ref):
    ids = lax.broadcasted_iota(jnp.int32, (ATOMS, ATOMS), 0).astype(F32)
    same = lax.broadcasted_iota(jnp.int32, (ATOMS, ATOMS), 1).astype(F32)
    for index in range(1 + len(OFFSETS)):
        row = same if index == 2 else lists[index - (index > 2)]
        owners_ref[index] = (ids == row).astype(BF16)


def started(pairs, sems):
    copies = [
        pltpu.make_async_copy(source, target, sems.at[index])
        for index, (source, target) in enumerate(pairs)
    ]
    for copy in copies:
        copy.start()
    return copies


def encode_rows(
    feats_ref, species, w_deg_ref, w_gate_ref, embed_ref, rows_ref, mixed_ref, gates_ref
):
    scalar = feats_ref[:, lanes(0)]
    gates = jax.nn.sigmoid(matmul(scalar, w_gate_ref[...]))
    gates_ref[...] = gates
    for degree in range(DEGREES):
        low, high = first_rows(degree)
        rows = component_rows(feats_ref, degree)
        mixed = matmul(rows, w_deg_ref[degree])
        mixed_ref[low:high, :] = mixed
        if degree == 0:
            added = jax.nn.silu(mixed) + along_first(
                kind_rows(species), embed_ref[...], PRECISE
            )
        else:
            added = mixed * over_components(gates[:, lanes(degree - 1)], degree)
        rows_ref[low:high, :] = (rows.astype(F32) + added).astype(BF16)


def lists_of(ints_ref):
    count = len(OFFSETS)
    lists = [ints_ref[which : which + 1, 0:ATOMS] for which in range(count)]
    return lists, ints_ref[count : count + 1, 0:ATOMS]


def parts_of(values):
    high = values.astype(BF16)
    rest = values - high.astype(F32)
    middle = rest.astype(BF16)
    low = (rest - middle.astype(F32)).astype(BF16)
    return high, middle, low


def halves(values, axis):
    return jnp.concatenate(parts_of(values)[0:2], axis=axis)


def folded(values):
    return values[:, 0:CHANS] + values[:, CHANS:]


def stacked(values, order):
    parts = [part.astype(F32) for part in parts_of(values)]
    return jnp.concatenate([parts[index] for index in order], axis=0).astype(BF16)


def pack_kernel(
    harm_hbm, dist_hbm, nbr_hbm, lists_hbm, species_hbm, w_radial_hbm, embed_hbm, w_hidden_hbm,
    b_hidden_hbm, w_out_hbm, target_hbm, copies_hbm, ints_hbm, small_hbm,
    pack_ref, small_ref, nbr_ref, lists_ref, species_ref, b_hidden_ref, w_out_ref, target_ref,
    sems, out_sems,
):
    copies = started(
        [
            (harm_hbm, pack_ref.at[pl.ds(0, COMPS)]),
            (dist_hbm, pack_ref.at[COMPS]),
            (nbr_hbm, nbr_ref),
            (lists_hbm, lists_ref),
            (species_hbm, species_ref),
            (embed_hbm, small_ref.at[pl.ds(EMBED_ROW, KINDS)]),
            (w_hidden_hbm, small_ref.at[pl.ds(CONST_ROW + 8, CHANS)]),
            (b_hidden_hbm, b_hidden_ref),
            (w_out_hbm, w_out_ref),
            (target_hbm, target_ref),
        ]
        + [
            (
                w_radial_hbm.at[:, pl.ds(degree * CHANS, CHANS)],
                small_ref.at[pl.ds(degree * BASES, BASES)],
            )
            for degree in range(DEGREES)
        ],
        sems,
    )
    pack_ref[COMPS + 2 :] = jnp.zeros((FIELDS - COMPS - 2, SLOTS, PROBES), F32)
    small_ref[INTS_ROW : CONST_ROW + 8, :] = jnp.zeros((16, CHANS), F32)
    for copy in copies:
        copy.wait()
    count = len(OFFSETS)
    small_ref[INTS_ROW : INTS_ROW + count, 0:ATOMS] = lists_ref[...].astype(F32)
    small_ref[INTS_ROW + count : INTS_ROW + count + 1, 0:ATOMS] = species_ref[...].astype(F32)
    small_ref[CONST_ROW : CONST_ROW + 3, :] = jnp.concatenate(
        [b_hidden_ref[...], w_out_ref[...], target_ref[...]], axis=0
    )
    pack_ref[COMPS + 1] = nbr_ref[...].astype(F32)
    writes = started(
        [(small_ref.at[pl.ds(INTS_ROW, 8)], ints_hbm), (small_ref, small_hbm)]
        + [(pack_ref, copies_hbm.at[row]) for row in range(ROWS)],
        out_sems,
    )
    for write in writes:
        write.wait()


def stage_kernel(*refs):
    half = len(refs) // 2
    for source, target in zip(refs[:half], refs[half:]):
        target[...] = source[...]


def plane_halves():
    row = lax.axis_index("y")
    upper = jnp.where(row > 1, 1, 0)
    return row, HALO - HALO * upper, row + ROWS - 2 * ROWS * upper


def pair_kernel(
    packs_ref, theirs_ref, their_ints_ref, feats_ref, w_deg_ref, w_gate_ref, small_ref,
    out_ref, spread_ref, halo_ref, sums_ref, radial_ref, ints_ref, const_ref,
    mixed_ref, gates_ref, their_mixed_ref, their_gates_ref,
    rows_ref, owners_ref, their_rows_ref, their_owners_ref, embed_ref, values_ref,
):
    embed_ref[...] = small_ref[EMBED_ROW:INTS_ROW, :]
    ints_ref[...] = small_ref[INTS_ROW:CONST_ROW, :]
    const_ref[...] = small_ref[CONST_ROW:, :]
    w_radial = jnp.concatenate(
        [small_ref[degree * BASES : (degree + 1) * BASES, :] for degree in range(DEGREES)], axis=1
    )
    radial_split = stacked(w_radial, (0, 0, 1, 1, 0, 2))
    lists, species = lists_of(ints_ref)
    owner_tables(lists, owners_ref)
    encode_rows(
        feats_ref, species, w_deg_ref, w_gate_ref, embed_ref, rows_ref, mixed_ref, gates_ref
    )
    shards, chunk = out_ref.shape[1], out_ref.shape[2]
    own_row, first, partner_row = plane_halves()
    sub = lax.broadcasted_iota(jnp.int32, (ATOMS, PROBES), 0).astype(F32)

    def spread_pairs(target_ref, tables_ref, begin, probe_row, atom_row):
        delta = probe_row - atom_row
        valid = jnp.logical_and(delta >= -2, delta <= 2)
        table = jnp.clip(delta + 2, 0, 4)
        block = jnp.where(delta < 0, delta + 3, jnp.where(delta > 0, delta + 2, 0))
        base = jnp.where(valid, block * ATOMS, 1 << 20).astype(F32)
        for slot in range(SLOTS):
            start = begin + slot * PROBES

            def row(field):
                return packs_ref[probe_row, field, slot : slot + 1, :]

            hot = (row(COMPS + 1) - base == sub).astype(BF16)
            hot = matmul(tables_ref[table], hot)
            for m in range(COMPS):
                target_ref[m * ATOMS : (m + 1) * ATOMS, start : start + PROBES] = (
                    hot * row(m)
                ).astype(BF16)

    for row in range(ROWS):
        spread_pairs(spread_ref, owners_ref, row * SPAN, row, own_row)
    their_lists, their_species = lists_of(their_ints_ref)
    owner_tables(their_lists, their_owners_ref)
    encode_rows(
        theirs_ref, their_species, w_deg_ref, w_gate_ref, embed_ref, their_rows_ref,
        their_mixed_ref, their_gates_ref,
    )
    for row in range(HALO):
        spread_pairs(halo_ref, their_owners_ref, row * SPAN, first + row, partner_row)
    dists = [packs_ref[row, COMPS, slot : slot + 1, :] for row in range(ROWS) for slot in range(SLOTS)]
    dists += [
        packs_ref[first + row, COMPS, slot : slot + 1, :]
        for row in range(HALO)
        for slot in range(SLOTS)
    ]
    dist = jnp.concatenate(dists, axis=1)
    orders = lax.broadcasted_iota(jnp.int32, (BASES, PAIRS), 0).astype(F32) + 1.0
    phase = math.pi * dist / CUTOFF
    envelope = 0.5 * (jnp.cos(phase) + 1.0) / dist
    basis_split = stacked(jnp.sin(phase * orders) * envelope, (0, 1, 0, 1, 2, 0))
    sums_ref[DEGREES * CHANS :, :] = basis_split[0 : 2 * BASES, :].astype(F32)
    total = None
    for degree in range(DEGREES):
        low, high = first_rows(degree)
        radial = along_first(radial_split[:, lanes(degree)], basis_split)
        radial_ref[lanes(degree), :] = radial
        sums = jnp.concatenate(
            [
                along_first(rows_ref[low:high, :], spread_ref[low:high, :]),
                along_first(their_rows_ref[low:high, :], halo_ref[low:high, :]),
            ],
            axis=1,
        )
        sums_ref[lanes(degree), :] = sums
        term = radial * sums
        total = term if total is None else total + term

    def value_of(block):
        start = block * SPAN
        both = total[:, start : start + PROBES] + total[:, start + PROBES : start + SPAN]
        return both.T

    for row in range(ROWS):
        values_ref[row] = value_of(row)
    for row in range(HALO):
        values_ref[first + row] += value_of(ROWS + row)
    for row in range(ROWS):
        for shard in range(shards):
            part = values_ref[row, shard * chunk : (shard + 1) * chunk, :]
            out_ref[row, shard] = part.astype(BF16)


def silu_slope(values):
    logistic = jax.nn.sigmoid(values)
    return logistic * (1.0 + values * (1.0 - logistic))


def sum_kernel(parts_ref, out_ref):
    total = parts_ref[0].astype(F32)
    for index in range(1, parts_ref.shape[0]):
        total = total + parts_ref[index].astype(F32)
    if len(out_ref.shape) == len(parts_ref.shape):
        for copy in range(out_ref.shape[0]):
            out_ref[copy] = total.astype(out_ref.dtype)
    else:
        out_ref[...] = total.astype(out_ref.dtype)


def readout_kernel(
    scale, parts_ref, const_ref, up_ref, head_ref, density_ref, column_ref
):
    chunk = parts_ref.shape[1]
    shard = lax.axis_index("x") * lax.axis_size("c") + lax.axis_index("c")
    start = pl.multiple_of(shard * chunk, chunk)
    column_ref[...] = jnp.broadcast_to(const_ref[2:3, :], (PROBES, PROBES)).T
    target = column_ref[pl.ds(start, chunk), :]
    summed = parts_ref[0].astype(F32)
    for index in range(1, parts_ref.shape[0]):
        summed = summed + parts_ref[index].astype(F32)
    w_hidden = const_ref[8:, :]
    w_out = const_ref[1:2, :]
    hidden_pre = matmul(summed, w_hidden, PRECISE) + const_ref[0:1, :]
    activated = jax.nn.silu(hidden_pre)
    density = jnp.sum(activated * w_out, axis=1, keepdims=True)
    error = density - target
    error_grad = error * scale
    pre_grad = w_out * silu_slope(hidden_pre) * error_grad
    spot = lax.broadcasted_iota(jnp.int32, (chunk, PROBES), 0) + start
    mask = (spot == lax.broadcasted_iota(jnp.int32, (chunk, PROBES), 1)).astype(F32)
    upstream = along_last(pre_grad, w_hidden, PRECISE)
    for copy in range(up_ref.shape[0]):
        up_ref[copy] = upstream.astype(BF16)
    density_ref[...] = jnp.sum(mask * density, axis=0, keepdims=True)
    head_ref[0:CHANS, :] = along_first(summed, pre_grad, PRECISE)
    bias = jnp.sum(pre_grad, axis=0, keepdims=True)
    out = jnp.sum(activated * error_grad, axis=0, keepdims=True)
    loss = jnp.sum(mask * error * error * (0.5 * scale), axis=0, keepdims=True)
    head_ref[CHANS : CHANS + 16, :] = jnp.concatenate(
        [bias, out, loss, jnp.zeros((13, CHANS), F32)], axis=0
    )


def own_slab():
    depth = lax.axis_index("zh") * lax.axis_size("zl") + lax.axis_index("zl")
    return depth * ROWS + lax.axis_index("y")


def backward_kernel(
    atoms_ref, theirs_ref, ints_ref, their_ints_ref, mixed_ref, their_mixed_ref, gates_ref, their_gates_ref,
    radial_ref, head_ref, density_ref, up_ref, sums_ref, spread_ref, halo_ref, payload_ref,
):
    shards = up_ref.shape[1]
    first = plane_halves()[1]

    def block_of(row):
        parts = [up_ref[row, shard].astype(F32) for shard in range(shards)]
        return [jnp.concatenate(parts, axis=0).T] * SLOTS

    blocks = []
    for row in list(range(ROWS)) + [first + row for row in range(HALO)]:
        blocks += block_of(row)
    upstream = jnp.concatenate(blocks, axis=1)
    scalar = jnp.concatenate([atoms_ref[:, lanes(0)], theirs_ref[:, lanes(0)]], axis=0)
    gates = jnp.concatenate([gates_ref[...], their_gates_ref[...]], axis=0)
    kinds = jnp.concatenate(
        [kind_rows(lists_of(ref)[1]) for ref in (ints_ref, their_ints_ref)], axis=1
    )
    basis_split = sums_ref[DEGREES * CHANS :, :].astype(BF16)
    radial_grads = []
    for degree in range(DEGREES):
        low, high = first_rows(degree)
        size = high - low
        inner = halves(radial_ref[lanes(degree), :] * upstream, 0)
        grads = jnp.concatenate(
            [
                folded(along_last(spread_ref[low:high, :], inner[:, 0:OWN_PAIRS])),
                folded(along_last(halo_ref[low:high, :], inner[:, OWN_PAIRS:])),
            ],
            axis=0,
        )
        product = halves(sums_ref[lanes(degree), :] * upstream, 0)
        both = along_last(product, basis_split)
        both = both[0:CHANS, :] + both[CHANS:, :]
        radial_grads.append((both[:, 0:BASES] + both[:, BASES : 2 * BASES]).T)
        rows = jnp.concatenate(
            [component_rows(atoms_ref, degree), component_rows(theirs_ref, degree)], axis=0
        )
        mixed = jnp.concatenate([mixed_ref[low:high, :], their_mixed_ref[low:high, :]], axis=0)
        if degree == 0:
            mixed_grad = grads * silu_slope(mixed)
            embed_grad = matmul(kinds, grads, PRECISE)
        else:
            gate = gates[:, lanes(degree - 1)]
            spread_gate = jnp.concatenate(
                [over_components(gate[0:ATOMS, :], degree), over_components(gate[ATOMS:, :], degree)],
                axis=0,
            )
            mixed_grad = grads * spread_gate
            product = grads * mixed
            totals = []
            for side in range(2):
                total = product[side * size : side * size + ATOMS, :]
                for comp in range(1, 2 * degree + 1):
                    begin = side * size + comp * ATOMS
                    total = total + product[begin : begin + ATOMS, :]
                totals.append(total)
            total = jnp.concatenate(totals, axis=0)
            pre = halves(total * gate * (1.0 - gate), 1)
            start = (DEGREES + degree - 1) * CHANS
            payload_ref[start : start + CHANS, :] = folded(along_first(scalar, pre)).astype(BF16)
        payload_ref[degree * CHANS : (degree + 1) * CHANS, :] = folded(
            along_first(rows, halves(mixed_grad, 1))
        ).astype(BF16)
    base = (2 * DEGREES - 1) * CHANS
    payload_ref[base : base + CHANS + 16, :] = head_ref[...].astype(BF16)
    base += CHANS + 16
    payload_ref[base : base + 48, :] = jnp.concatenate(
        radial_grads + [embed_grad], axis=0
    ).astype(BF16)
    base += 48
    slabs = (PAYLOAD - base) // 3
    here = lax.broadcasted_iota(jnp.int32, (slabs, PROBES), 0) == own_slab()
    for part in parts_of(jnp.where(here, density_ref[...], 0.0)):
        payload_ref[base : base + slabs, :] = part
        base += slabs


def unpack_kernel(
    payload_ref, loss_ref, density_ref, deg_ref, gate_ref, embed_ref, radial_ref, hidden_ref,
    bias_ref, out_ref,
):
    for degree in range(DEGREES):
        deg_ref[degree] = payload_ref[lanes(degree), :].astype(F32)
    for degree in range(1, DEGREES):
        gate_ref[:, lanes(degree - 1)] = payload_ref[lanes(DEGREES + degree - 1), :].astype(F32)
    base = (2 * DEGREES - 1) * CHANS
    hidden_ref[...] = payload_ref[base : base + CHANS, :].astype(F32)
    base += CHANS
    misc = payload_ref[base : base + 16, :].astype(F32)
    bias_ref[...] = misc[0:1, :]
    out_ref[...] = misc[1:2, :]
    loss_ref[...] = jnp.sum(misc[2:3, :], axis=1, keepdims=True)
    base += 16
    small = payload_ref[base : base + 48, :].astype(F32)
    for degree in range(DEGREES):
        radial_ref[:, lanes(degree)] = small[degree * BASES : (degree + 1) * BASES, :]
    embed_ref[...] = small[DEGREES * BASES :, :]
    base += 48
    slabs = (PAYLOAD - base) // 3
    total = None
    for _ in range(3):
        part = payload_ref[base : base + slabs, :].astype(F32)
        total = part if total is None else total + part
        base += slabs
    here = lax.broadcasted_iota(jnp.int32, (slabs, PROBES), 0) == own_slab()
    density_ref[...] = jnp.sum(jnp.where(here, total, 0.0), axis=0, keepdims=True)


def shape(dims, dtype=F32):
    return jax.ShapeDtypeStruct(dims, dtype)


def call(kernel, outs, name, limit=32, **options):
    return pl.pallas_call(
        kernel,
        out_shape=outs,
        name=name,
        compiler_params=pltpu.CompilerParams(vmem_limit_bytes=limit * 1024 * 1024),
        **options,
    )


def to_partner(block):
    count = lax.axis_size(SLAB)
    route = [(i, (i + (ROWS if i % ROWS >= HALO else -ROWS)) % count) for i in range(count)]
    return lax.ppermute(block, SLAB, route)


def reduce_all(payload):
    count, depth = lax.axis_size(NEAR), lax.axis_size("zh")
    rows = PAYLOAD // count
    parts = lax.all_to_all(payload.reshape(count, rows, CHANS), NEAR, 0, 0)
    copies = call(sum_kernel, shape((depth, rows, CHANS), BF16), "sum_near")(parts)
    parts = lax.all_to_all(copies, "zh", 0, 0)
    copies = call(sum_kernel, shape((count, rows, CHANS), BF16), "sum_depth")(parts)
    return lax.all_to_all(copies, NEAR, 0, 0).reshape(PAYLOAD, CHANS)


def on_device(
    atom_feats, species, send_rows, neighbours, harmonics, distances, target,
    w_deg, w_gate, embed, w_radial, w_hidden, b_hidden, w_out,
):
    slab_count = lax.axis_size(SLAB)
    shards = lax.axis_size(ATOM)
    chunk = PROBES // shards
    scale = 1.0 / math.sqrt(PROBES * slab_count)
    species = species.reshape(1, ATOMS)
    lists = send_rows[0, 0]
    far = pl.BlockSpec(memory_space=pl.ANY)
    field_shape = (FIELDS, SLOTS, PROBES)
    with jax.named_scope("exchange_atoms"):
        theirs = to_partner(atom_feats)
    rows_of = [row.reshape(1, CHANS) for row in (b_hidden, w_out, target)]
    operands = (
        harmonics, distances, neighbours, lists, species, w_radial, embed, w_hidden, *rows_of
    )
    held = [
        shape((ROWS,) + field_shape),
        shape((8, CHANS)),
        shape((SMALL_ROWS, CHANS)),
    ]
    copies, ints, small = call(
        pack_kernel,
        held,
        "pack",
        limit=63,
        in_specs=[far] * len(operands),
        out_specs=[far] * len(held),
        scratch_shapes=[
            pltpu.VMEM(field_shape, F32),
            pltpu.VMEM(held[2].shape, F32),
            pltpu.VMEM((SLOTS, PROBES), jnp.int32),
            pltpu.VMEM(lists.shape, jnp.int32),
            pltpu.VMEM(species.shape, jnp.int32),
        ]
        + [pltpu.VMEM((1, CHANS), F32)] * 3
        + [
            pltpu.SemaphoreType.DMA((len(operands) - 1 + DEGREES,)),
            pltpu.SemaphoreType.DMA((2 + ROWS,)),
        ],
    )(*operands)
    with jax.named_scope("exchange_lists"):
        their_ints = to_partner(ints)
    with jax.named_scope("gather_pairs"):
        packs = lax.all_to_all(copies, "y", 0, 0)
    mixed_shapes = [shape((COMPS * ATOMS, CHANS)), shape((ATOMS, (DEGREES - 1) * CHANS))]
    tables = [
        pltpu.VMEM((COMPS * ATOMS, CHANS), BF16),
        pltpu.VMEM((1 + len(OFFSETS), ATOMS, ATOMS), BF16),
    ]
    operands = (atom_feats, w_deg, w_gate, small)
    feats, *weights = call(
        stage_kernel, [shape(operand.shape, operand.dtype) for operand in operands], "stage"
    )(*operands)
    (
        values, spread, halo, sums, radial, own_ints, consts,
        mixed, gates, their_mixed, their_gates,
    ) = call(
        pair_kernel,
        [
            shape((ROWS, shards, chunk, CHANS), BF16),
            shape((COMPS * ATOMS, OWN_PAIRS), BF16),
            shape((COMPS * ATOMS, HALO_PAIRS), BF16),
            shape((DEGREES * CHANS + 2 * BASES, PAIRS)),
            shape((DEGREES * CHANS, PAIRS)),
            shape(ints.shape),
            shape((SMALL_ROWS - CONST_ROW, CHANS)),
        ]
        + mixed_shapes * 2,
        "pair_sums",
        scratch_shapes=tables * 2
        + [pltpu.VMEM(embed.shape, F32), pltpu.VMEM((ROWS, PROBES, CHANS), F32)],
    )(packs, theirs, their_ints, feats, *weights)
    with jax.named_scope("scatter_sums"):
        parts = lax.all_to_all(values.reshape(ROWS * shards, chunk, CHANS), PLANE, 0, 0)
    up, head, density_row = call(
        functools.partial(readout_kernel, scale),
        [
            shape((ROWS * shards, chunk, CHANS), BF16),
            shape((CHANS + 16, CHANS)),
            shape((1, PROBES)),
        ],
        "readout",
        scratch_shapes=[pltpu.VMEM((PROBES, PROBES), F32)],
    )(parts, consts)
    with jax.named_scope("gather_grads"):
        ups = lax.all_to_all(up, PLANE, 0, 0).reshape(ROWS, shards, chunk, CHANS)
    operands = (
        feats, theirs, own_ints, their_ints, mixed, their_mixed, gates, their_gates, radial,
        head, density_row, ups, sums, spread, halo,
    )
    payload = call(backward_kernel, shape((PAYLOAD, CHANS), BF16), "backward")(*operands)
    with jax.named_scope("reduce_grads"):
        payload = reduce_all(payload)
    loss, density, deg, gate, embed_grad, radial_grad, hidden, bias, out = call(
        unpack_kernel,
        [
            shape((1, 1)),
            shape((1, PROBES)),
            shape((DEGREES, CHANS, CHANS)),
            shape((CHANS, (DEGREES - 1) * CHANS)),
            shape((KINDS, CHANS)),
            shape((BASES, DEGREES * CHANS)),
            shape((CHANS, CHANS)),
            shape((1, CHANS)),
            shape((1, CHANS)),
        ],
        "unpack",
    )(payload)
    return (
        loss.reshape(()), density.reshape(PROBES), deg, gate, embed_grad, radial_grad, hidden,
        bias.reshape(CHANS), out.reshape(CHANS),
    )


def solution(mesh):
    slabs, shards = mesh.devices.shape
    fine = mesh.devices.reshape(slabs // 8, 2, 4, shards // 2, 2)
    fine = Mesh(fine, ("zh", "zl", "y", "x", "c"))
    in_specs = (
        P(SLAB + ATOM, None),
        P(SLAB + ATOM),
        P(SLAB, ATOM, None, None),
        P(ATOM, SLAB),
        P(None, ATOM, SLAB),
        P(ATOM, SLAB),
        P(SLAB),
        P(),
        P(),
        P(),
        P(),
        P(),
        P(),
        P(),
    )
    out_specs = (P(), P(SLAB), P(), P(), P(), P(), P(), P(), P())
    return jax.shard_map(
        on_device, mesh=fine, in_specs=in_specs, out_specs=out_specs, check_vma=False
    )
```
